32 devices in a mesh: seq: 8 (over z, y), dp: 4 (over x, core).
Axes of the slice: x: 2, y: 2, z: 4, core: 2. Of those that a mesh axis runs over, the one named last changes fastest.
Arguments:
- layer_inputs: bfloat16 [4, 2048, 4096], P('dp', 'seq')
- doc_start: int32 [4, 2048], P('dp', 'seq'), may hold values from 0 to 2047, as said below
- w_qkv: bfloat16 [4096, 512], P(('seq', 'dp'))
- d_context: bfloat16 [4, 2048, 256], P('dp', 'seq'), may hold values from -6 to 6
Outputs:
- d_x: bfloat16 [4, 2048, 4096], P('dp', 'seq')
- g_qkv: float32 [4096, 512], P(('seq', 'dp'))
The draws below stay inside these ranges and needn't reach their ends.
Inputs may be any that keep to these rules, and one draw needn't show every extreme that they name: doc_start[g, i] is at most i, never falls along positions, doc_start[g, 0] = 0, and doc_start[g, doc_start[g, i]] = doc_start[g, i].
All inputs are finite; a program needn't handle non-finite values.
Results may differ from the reference program's by a relative error of at most 0.017.
Values may be sent and summed in bfloat16 or wider, within the bound.
A program may use at most 64 MiB of HBM per device.

```python
import jax
import jax.numpy as jnp
from jax import lax

D = 4096
HD = 128
QH = 2
TOK_DEV = 256
WIN = 256
GROUPS = 4
TOKENS = 2048
N_SEQ = 8


def draw_layer_inputs(key, part):
    full_shape = (GROUPS, TOKENS, D)
    values = jax.random.normal(jax.random.fold_in(key, 21), full_shape, jnp.float32)
    return jnp.clip(values, -6.0, 6.0).astype(jnp.bfloat16)


def draw_w_qkv(key, part):
    q_width = QH * HD
    table_fresh = jax.random.normal(jax.random.fold_in(key, 31), (D, q_width + 2 * HD), jnp.float32) * D ** (-0.5)
    return table_fresh.astype(jnp.bfloat16)


def draw_doc_start(key, part):
    start_marks = jax.random.randint(jax.random.fold_in(key, 41), (GROUPS, TOKENS), 0, TOK_DEV)
    position_index = jnp.arange(TOKENS, dtype=jnp.int32)[None, :]
    opening = (start_marks == 0) | (position_index == 0) | (position_index == TOKENS - 1)
    return lax.cummax(jnp.where(opening, position_index, 0), axis=1).astype(jnp.int32)


def block_scale(own_key, dims, pieces, least, top_value):
    def one(dim, blocks):
        steps = jax.random.uniform(jax.random.fold_in(jax.random.fold_in(own_key, 6), dim), (blocks,), jnp.float32, least / len(pieces), top_value / len(pieces))
        return jnp.repeat(jnp.exp(steps), dims[dim] // blocks).reshape((-1,) + (1,) * (len(dims) - dim - 1))

    level = one(*pieces[0])
    for cut in pieces[1:]:
        level = level * one(*cut)
    return level


def normal_values(key, dims, deviation, limit, cuts=(), kind=jnp.bfloat16):
    array = deviation * jax.random.normal(key, dims, jnp.float32)
    if cuts:
        array = array * block_scale(key, dims, cuts, -0.22, 0.18)
    return jnp.clip(array, -limit, limit).astype(kind)


def setup_inputs(seed: int = 0) -> dict:
    splits = jax.random.split(jax.random.key(seed), 5)
    layer_inputs = draw_layer_inputs(jax.random.fold_in(splits[4], 71), 0)
    doc_start = draw_doc_start(jax.random.fold_in(splits[4], 71), 0)
    w_qkv = draw_w_qkv(jax.random.fold_in(splits[4], 71), 0)
    d_context = normal_values(splits[3], (GROUPS, TOKENS, QH * HD), 1.0, 6.0, ((0, 4), (1, 8)))
    return dict(layer_inputs=layer_inputs, doc_start=doc_start, w_qkv=w_qkv, d_context=d_context)


def masked_scores(queries, key_rows, doc_first, query_pos, key_pos):
    inv_root = queries.shape[2] ** -0.5
    scores = jnp.einsum("rhd,kd->hrk", queries.astype(jnp.float32), key_rows.astype(jnp.float32)) * inv_root
    visible = (key_pos[None, :] <= query_pos[:, None]) & (key_pos[None, :] > query_pos[:, None] - WIN) & (key_pos[None, :] >= doc_first[:, None])
    return jnp.where(visible[None, :, :], scores, -jnp.inf)


def backward_terms(queries, key_rows, value_rows, out_grad, attn_probs, prob_low, row_dot):
    inv_root = queries.shape[2] ** -0.5
    prob_grad = jnp.einsum("rhd,kd->hrk", out_grad.astype(jnp.float32), value_rows.astype(jnp.float32))
    score_grad = (attn_probs * (prob_grad - row_dot[:, :, None])).astype(jnp.bfloat16)
    grad_query = jnp.einsum("hrk,kd->rhd", score_grad.astype(jnp.float32), key_rows.astype(jnp.float32)) * inv_root
    grad_keys = jnp.einsum("hrk,rhd->kd", score_grad.astype(jnp.float32), queries.astype(jnp.float32)) * inv_root
    grad_values = jnp.einsum("hrk,rhd->kd", prob_low.astype(jnp.float32), out_grad.astype(jnp.float32))
    return grad_query, grad_keys, grad_values


def local_pass(queries, key_rows, value_rows, out_grad, doc_first, query_pos, key_pos):
    scores = masked_scores(queries, key_rows, doc_first, query_pos, key_pos)
    row_max = jnp.max(scores, axis=2)
    log_total = row_max + jnp.log(jnp.sum(jnp.exp(scores - row_max[:, :, None]), axis=2))
    attn_probs = jnp.exp(scores - log_total[:, :, None])
    prob_low = attn_probs.astype(jnp.bfloat16)
    context = jnp.einsum("hrk,kd->rhd", prob_low.astype(jnp.float32), value_rows.astype(jnp.float32))
    row_dot = jnp.sum(out_grad.astype(jnp.float32) * context, axis=2).T
    return backward_terms(queries, key_rows, value_rows, out_grad, attn_probs, prob_low, row_dot)


def reference(layer_inputs, doc_start, w_qkv, d_context):
    q_width = QH * HD
    positions = jnp.arange(TOKENS, dtype=jnp.int32).reshape(N_SEQ, TOK_DEV)
    key_pos = jnp.concatenate([positions - TOK_DEV, positions], axis=1)
    grad_total = jnp.zeros((D, (QH + 2) * HD), jnp.float32)
    input_grads = []
    for group_index in range(GROUPS):
        x_group = layer_inputs[group_index]
        projected = jnp.dot(x_group, w_qkv, preferred_element_type=jnp.float32).astype(jnp.bfloat16)
        queries = projected[:, :q_width].reshape(N_SEQ, TOK_DEV, QH, HD)
        key_own = projected[:, q_width:q_width + HD].reshape(N_SEQ, TOK_DEV, HD)
        value_own = projected[:, q_width + HD:].reshape(N_SEQ, TOK_DEV, HD)
        zero_rows = jnp.zeros((1, TOK_DEV, HD), jnp.bfloat16)
        key_rows = jnp.concatenate([jnp.concatenate([zero_rows, key_own[:-1]], axis=0), key_own], axis=1)
        value_rows = jnp.concatenate([jnp.concatenate([zero_rows, value_own[:-1]], axis=0), value_own], axis=1)
        out_grad = d_context[group_index].reshape(N_SEQ, TOK_DEV, QH, HD)
        doc_first = doc_start[group_index].reshape(N_SEQ, TOK_DEV)

        def one_block(block_item):
            return local_pass(*block_item)

        grad_query, grad_keys, grad_values = lax.map(one_block, (queries, key_rows, value_rows, out_grad, doc_first, positions, key_pos))
        float_zero = jnp.zeros((1, TOK_DEV, HD), jnp.float32)
        key_total = grad_keys[:, TOK_DEV:] + jnp.concatenate([grad_keys[1:, :TOK_DEV], float_zero], axis=0)
        value_total = grad_values[:, TOK_DEV:] + jnp.concatenate([grad_values[1:, :TOK_DEV], float_zero], axis=0)
        grad_proj = jnp.concatenate([
            grad_query.astype(jnp.bfloat16).reshape(TOKENS, q_width),
            key_total.astype(jnp.bfloat16).reshape(TOKENS, HD),
            value_total.astype(jnp.bfloat16).reshape(TOKENS, HD)], axis=1)
        input_grads.append(lax.dot_general(grad_proj, w_qkv, (((1,), (1,)), ((), ())), preferred_element_type=jnp.float32).astype(jnp.bfloat16))
        grad_total = grad_total + lax.dot_general(x_group, grad_proj, (((0,), (0,)), ((), ())), preferred_element_type=jnp.float32)
    return jnp.stack(input_grads), grad_total
```

```python
import functools

import jax
import jax.numpy as jnp
from jax import lax
from jax.experimental import pallas as pl
from jax.experimental.pallas import tpu as pltpu
from jax.sharding import PartitionSpec as P

WIN = 256


def from_partner(block, axis, stride):
    count = lax.axis_size(axis)
    route = []
    for low in range(count):
        high = low | 1 << stride
        if high != low and high < count:
            route += [(low, high), (high, low)]
    return lax.ppermute(block, axis, route)


def from_behind(block, axis, distance):
    devices = range(lax.axis_size(axis))
    route = [(i - distance, i) for i in devices if i - distance in devices]
    return lax.ppermute(block, axis, route)


def masked_scores(queries, key_rows, doc_first, query_pos, key_pos):
    inv_root = queries.shape[2] ** (-0.5)
    scores = (
        jnp.einsum("rhd,kd->hrk", queries, key_rows, preferred_element_type=jnp.float32) * inv_root
    )
    visible = (
        (key_pos[None, :] <= query_pos[:, None])
        & (key_pos[None, :] > query_pos[:, None] - WIN)
        & (key_pos[None, :] >= doc_first[:, None])
    )
    return jnp.where(visible[None, :, :], scores, -jnp.inf)


def backward_terms(queries, key_rows, value_rows, out_grad, attn_probs, prob_low, row_dot):
    inv_root = queries.shape[2] ** (-0.5)
    prob_grad = jnp.einsum("rhd,kd->hrk", out_grad, value_rows, preferred_element_type=jnp.float32)
    score_grad = (attn_probs * (prob_grad - row_dot[:, :, None])).astype(jnp.bfloat16)
    grad_query = (
        jnp.einsum("hrk,kd->rhd", score_grad, key_rows, preferred_element_type=jnp.float32)
        * inv_root
    )
    grad_keys = (
        jnp.einsum("hrk,rhd->kd", score_grad, queries, preferred_element_type=jnp.float32)
        * inv_root
    )
    grad_values = jnp.einsum("hrk,rhd->kd", prob_low, out_grad, preferred_element_type=jnp.float32)
    return (grad_query, grad_keys, grad_values)


def local_pass(queries, key_rows, value_rows, out_grad, doc_first, query_pos, key_pos):
    scores = masked_scores(queries, key_rows, doc_first, query_pos, key_pos)
    row_max = jnp.max(scores, axis=2)
    log_total = row_max + jnp.log(jnp.sum(jnp.exp(scores - row_max[:, :, None]), axis=2))
    attn_probs = jnp.exp(scores - log_total[:, :, None])
    prob_low = attn_probs.astype(jnp.bfloat16)
    context = jnp.einsum("hrk,kd->rhd", prob_low, value_rows, preferred_element_type=jnp.float32)
    row_dot = jnp.sum(out_grad.astype(jnp.float32) * context, axis=2).T
    grad_query, grad_keys, grad_values = backward_terms(
        queries, key_rows, value_rows, out_grad, attn_probs, prob_low, row_dot
    )
    return (grad_query, grad_keys, grad_values, log_total, row_dot)


def halve_over_seq(buffer, bit_index):
    half_rows = buffer.shape[0] // 2
    my_bit = lax.axis_index("seq") >> bit_index & 1
    kept_half = lax.dynamic_slice_in_dim(buffer, my_bit * half_rows, half_rows, 0)
    sent_half = lax.dynamic_slice_in_dim(buffer, (1 - my_bit) * half_rows, half_rows, 0)
    return kept_half + from_partner(sent_half.astype(jnp.bfloat16), "seq", bit_index).astype(
        sent_half.dtype
    )


def halve_over_dp(buffer, bit_index):
    half_rows = buffer.shape[0] // 2
    my_bit = lax.axis_index("dp") >> bit_index & 1
    kept_half = lax.dynamic_slice_in_dim(buffer, my_bit * half_rows, half_rows, 0)
    sent_half = lax.dynamic_slice_in_dim(buffer, (1 - my_bit) * half_rows, half_rows, 0)
    return kept_half + from_partner(sent_half.astype(jnp.bfloat16), "dp", bit_index).astype(
        sent_half.dtype
    )


def body(layer_inputs, doc_start, w_qkv, d_context):
    x_local = layer_inputs[0]
    tok_rows = x_local.shape[0]
    q_width = d_context.shape[2]
    head_dim = (w_qkv.shape[1] - q_width) // 2
    heads = q_width // head_dim
    out_grad = d_context[0].reshape(tok_rows, heads, head_dim)
    doc_first = doc_start[0]
    positions = lax.axis_index("seq") * tok_rows + jnp.arange(tok_rows, dtype=jnp.int32)
    full_weights = lax.all_gather(w_qkv, ("seq", "dp"), axis=0, tiled=True)
    projected = jnp.dot(x_local, full_weights, preferred_element_type=jnp.float32)
    projected = projected.astype(jnp.bfloat16)
    queries = projected[:, :q_width].reshape(tok_rows, heads, head_dim)
    key_value = projected[:, q_width:]
    prior = from_behind(key_value, "seq", 1)
    key_rows = jnp.concatenate([prior[:, :head_dim], key_value[:, :head_dim]], axis=0)
    value_rows = jnp.concatenate([prior[:, head_dim:], key_value[:, head_dim:]], axis=0)
    key_pos = jnp.concatenate([positions - tok_rows, positions])
    grad_query, grad_keys, grad_values, log_total, row_dot = local_pass(
        queries, key_rows, value_rows, out_grad, doc_first, positions, key_pos
    )
    returned = from_behind(
        jnp.concatenate([grad_keys[:tok_rows], grad_values[:tok_rows]], axis=1).astype(
            jnp.bfloat16
        ),
        "seq",
        -1,
    ).astype(jnp.float32)
    far_keys = returned[:, :head_dim]
    far_values = returned[:, head_dim:]
    key_grad = (grad_keys[tok_rows:] + far_keys).astype(jnp.bfloat16)
    value_grad = (grad_values[tok_rows:] + far_values).astype(jnp.bfloat16)
    grad_proj = jnp.concatenate(
        [grad_query.astype(jnp.bfloat16).reshape(tok_rows, q_width), key_grad, value_grad], axis=1
    )
    input_grad = lax.dot_general(
        grad_proj, full_weights, (((1,), (1,)), ((), ())), preferred_element_type=jnp.float32
    )
    input_grad = input_grad.astype(jnp.bfloat16).reshape(1, tok_rows, x_local.shape[1])
    partial_grad = lax.dot_general(
        x_local, grad_proj, (((0,), (0,)), ((), ())), preferred_element_type=jnp.float32
    )
    seq_count = lax.axis_size("seq")
    dp_count = lax.axis_size("dp")
    seq_levels = seq_count.bit_length() - 1
    dp_levels = dp_count.bit_length() - 1
    buffer = partial_grad
    for bit_index in range(seq_levels - 1, -1, -1):
        buffer = halve_over_seq(buffer, bit_index)
    for bit_index in range(dp_levels - 1, -1, -1):
        buffer = halve_over_dp(buffer, bit_index)
    return (input_grad, buffer)


BF = jnp.bfloat16
F32 = jnp.float32
NZ = 4
ORDER = (0, 1, 3, 2)


def dot_nn(a, b):
    return jnp.dot(a, b, preferred_element_type=F32)


def dot_nt(a, b):
    return lax.dot_general(a, b, (((1,), (1,)), ((), ())), preferred_element_type=F32)


def dot_tn(a, b):
    return lax.dot_general(a, b, (((0,), (0,)), ((), ())), preferred_element_type=F32)


def flip(v, f):
    return v + f * (1 - 2 * v)


def remote(src, dst, send, recv, device):
    return pltpu.make_async_remote_copy(
        src_ref=src,
        dst_ref=dst,
        send_sem=send,
        recv_sem=recv,
        device_id=device,
        device_id_type=pl.DeviceIdType.MESH,
    )


def fused(
    x_hbm, doc_ref, w_hbm, do_ref, dx_hbm, g_ref,
    xv, xt, wv, acc, qs, dos, kv, dkv, pst, dst_, gp, dxv,
    gb, rd, sb, rb, sa, ra, sz, rz, kz,
    lsem, wsend, wrecv, hsend, hrecv, gsend, grecv, osem,
):
    s = lax.axis_index("seq")
    d = lax.axis_index("dp")
    z, y = s // 2, s % 2
    x, c = d // 2, d % 2
    tok = xv.shape[0]
    rows = wv.shape[1]
    hd = qs.shape[1]
    inv_root = hd ** (-0.5)
    my_a = x * (1 - c) + y * c
    my_b = y * (1 - c) + x * c

    def device(zz, yy, xx, cc):
        return (zz * 2 + yy, xx * 2 + cc)

    sib = device(z, y, x, 1 - c)
    part_a = device(z, flip(y, c), flip(x, 1 - c), c)
    part_b = device(z, flip(y, 1 - c), flip(x, c), c)
    zdev = [device((z + k) % NZ, y, x, c) for k in range(NZ)]

    def plane_block(k, a, b, plane):
        zz = (z + NZ - k) % NZ
        xx = flip(x, a * (1 - plane) + b * plane)
        yy = flip(y, b * (1 - plane) + a * plane)
        return ((zz * 2 + yy) * 2 + xx) * 2 + plane

    load_w = pltpu.make_async_copy(w_hbm, wv.at[s * 4 + d], lsem.at[0])
    load_x = pltpu.make_async_copy(x_hbm.at[0], xv, lsem.at[1])
    load_w.start()
    load_x.start()

    barrier = pltpu.get_barrier_semaphore()
    for dev in [sib, part_a, part_b] + zdev[1:]:
        pl.semaphore_signal(barrier, inc=1, device_id=dev, device_id_type=pl.DeviceIdType.MESH)
    extra_up = (y == 1) & (z < NZ - 1)
    extra_down = (y == 0) & (z > 0)

    @pl.when(extra_up)
    def _():
        pl.semaphore_signal(
            barrier, inc=1, device_id=(s + 1, d), device_id_type=pl.DeviceIdType.MESH
        )

    @pl.when(extra_down)
    def _():
        pl.semaphore_signal(
            barrier, inc=1, device_id=(s - 1, d), device_id_type=pl.DeviceIdType.MESH
        )

    @pl.when(extra_up | extra_down)
    def _():
        pl.semaphore_wait(barrier, 7)

    @pl.when(jnp.logical_not(extra_up | extra_down))
    def _():
        pl.semaphore_wait(barrier, 6)

    load_w.wait()

    sent = []

    def push(block, dev, send_index, recv_index):
        copy = remote(
            wv.at[block], wv.at[block], wsend.at[send_index], wrecv.at[recv_index], dev
        )
        copy.start()
        sent.append(copy)

    def arrived(block, index):
        remote(wv.at[block], wv.at[block], wsend.at[0], wrecv.at[index], sib).wait_recv()

    own = plane_block(0, 0, 0, c)

    def stage_z(k):
        block = plane_block(k, 0, 0, c)
        if k:
            arrived(block, k)
        push(block, part_a, 4 + k, 4 + k)
        push(block, part_b, 8 + 2 * k, 8 + 2 * k)
        if k == 0:
            for j in ORDER[1:]:
                push(own, zdev[j], j, j)
        push(block, sib, 16 + 4 * k, 16 + 4 * k)

    def stage_a(k):
        block = plane_block(k, 1, 0, c)
        arrived(block, 4 + k)
        push(block, part_b, 9 + 2 * k, 9 + 2 * k)
        push(block, sib, 17 + 4 * k, 17 + 4 * k)

    def stage_b(k):
        for a in range(2):
            block = plane_block(k, a, 1, c)
            arrived(block, 8 + 2 * k + a)
            push(block, sib, 18 + 4 * k + a, 18 + 4 * k + a)

    def stage_d(k):
        for b in range(2):
            for a in range(2):
                arrived(plane_block(k, a, b, 1 - c), 16 + 4 * k + 2 * b + a)
        zz = (z + NZ - k) % NZ
        span = 8 * rows
        xs = xv[:, pl.ds(pl.multiple_of(zz * span, span), span)]
        ws = wv[pl.ds(zz * 8, 8)].reshape(span, wv.shape[2])
        part = dot_nn(xs, ws)
        if k == ORDER[0]:
            acc[...] = part
        else:
            acc[...] += part

    def transpose_x(j, carry):
        zz, yy, xx, cc = j // 8, (j // 4) % 2, (j // 2) % 2, j % 2
        b_at = yy * (1 - cc) + xx * cc
        a_at = xx * (1 - cc) + yy * cc
        xt[cc, b_at, a_at, zz] = xv[:, pl.ds(pl.multiple_of(j * rows, rows), rows)].T
        return carry

    for t in range(NZ + 3):
        if t < NZ:
            stage_z(ORDER[t])
        if t == 0:
            load_x.wait()
            doc = jnp.broadcast_to(doc_ref[...], (tok, tok)).T
        if 0 <= t - 1 < NZ:
            stage_a(ORDER[t - 1])
        if 0 <= t - 2 < NZ:
            stage_b(ORDER[t - 2])
        if 0 <= t - 3 < NZ:
            stage_d(ORDER[t - 3])
        if t < NZ:
            lax.fori_loop(t * 8, t * 8 + 8, transpose_x, 0)
        if t == 1:
            row = lax.broadcasted_iota(jnp.int32, (tok, tok), 0)
            col = lax.broadcasted_iota(jnp.int32, (tok, tok), 1)
            vis_own = jnp.where((col <= row) & (col + s * tok >= doc), 0.0, -jnp.inf)
            vis_pri = jnp.where((col > row) & (col + (s - 1) * tok >= doc), 0.0, -jnp.inf)
            for h in range(2):
                dos[h * tok : (h + 1) * tok, :] = do_ref[0, :, h * hd : (h + 1) * hd]

    kv[1] = acc[:, 2 * hd :].astype(BF)
    halo = remote(kv.at[1], kv.at[0], hsend.at[0], hrecv.at[0], ((s + 1) % 8, d))
    first, last = s == 0, s == 7

    @pl.when(s < 7)
    def _():
        halo.start()

    @pl.when(first)
    def _():
        kv[0] = jnp.zeros_like(kv[0])

    for h in range(2):
        qs[h * tok : (h + 1) * tok, :] = acc[:, h * hd : (h + 1) * hd].astype(BF)
    k_own = kv[1, :, :hd]
    v_own = kv[1, :, hd:]
    own_scores = [
        dot_nt(qs[h * tok : (h + 1) * tok, :], k_own) * inv_root + vis_own for h in range(2)
    ]
    own_pg = [dot_nt(dos[h * tok : (h + 1) * tok, :], v_own) for h in range(2)]

    @pl.when(s > 0)
    def _():
        halo.wait_recv()

    k_pri = kv[0, :, :hd]
    v_pri = kv[0, :, hd:]
    for h in range(2):
        span = slice(h * tok, (h + 1) * tok)
        s_own = own_scores[h]
        s_pri = dot_nt(qs[span, :], k_pri) * inv_root + vis_pri
        pg_own = own_pg[h]
        pg_pri = dot_nt(dos[span, :], v_pri)
        top = jnp.max(jnp.maximum(s_own, s_pri), axis=1, keepdims=True)
        e_own = jnp.exp(s_own - top)
        e_pri = jnp.exp(s_pri - top)
        scale = 1.0 / jnp.sum(e_own + e_pri, axis=1, keepdims=True)
        p_own = e_own * scale
        p_pri = e_pri * scale
        l_own = p_own.astype(BF)
        l_pri = p_pri.astype(BF)
        row_dot = jnp.sum(
            l_own.astype(F32) * pg_own + l_pri.astype(F32) * pg_pri, axis=1, keepdims=True
        )
        pst[0, span, :] = l_pri
        pst[1, span, :] = l_own
        dst_[0, span, :] = (p_pri * (pg_pri - row_dot)).astype(BF)
        dst_[1, span, :] = (p_own * (pg_own - row_dot)).astype(BF)

    dkv[0, :, :hd] = (dot_tn(dst_[0], qs[...]) * inv_root).astype(BF)
    dkv[0, :, hd:] = dot_tn(pst[0], dos[...]).astype(BF)
    back = remote(dkv.at[0], dkv.at[1], hsend.at[1], hrecv.at[1], ((s + 7) % 8, d))

    @pl.when(s > 0)
    def _():
        back.start()

    @pl.when(last)
    def _():
        dkv[1] = jnp.zeros_like(dkv[1])

    for h in range(2):
        span = slice(h * tok, (h + 1) * tok)
        gp[:, h * hd : (h + 1) * hd] = (
            (dot_nn(dst_[1, span, :], k_own) + dot_nn(dst_[0, span, :], k_pri)) * inv_root
        ).astype(BF)

    half = 2 * hd
    rsent = []

    def weight_part(h, plane, b_at):
        gph = gp[:, h * half : (h + 1) * half]

        def one(j, carry):
            a_at, zz = j // 2, (j % 2) * 2
            lhs = xt[plane, b_at, a_at, pl.ds(zz, 2)].reshape(2 * rows, tok)
            gb[h, plane, b_at, a_at, pl.ds(zz, 2)] = (
                dot_nn(lhs, gph).astype(BF).reshape(2, rows, half)
            )
            return carry

        lax.fori_loop(0, 4, one, 0)

    def rpush(src, dst, index, dev):
        copy = remote(src, dst, gsend.at[index], grecv.at[index], dev)
        copy.start()
        rsent.append(copy)
        return copy

    def produce(h):
        copies = []
        for j in range(2):
            b_at = flip(my_a, 1 - j)
            weight_part(h, 1 - c, b_at)
            copies.append(rpush(gb.at[h, 1 - c, b_at], rd.at[h, j], 7 * h + j, sib))
        weight_part(h, c, 1 - my_b)
        weight_part(h, c, my_b)
        return copies

    def send_b(h, copies):
        copies[0].wait_recv()

        def one(j, carry):
            a_at, zz = j // NZ, j % NZ
            sb[h, a_at, zz] = (
                gb[h, c, 1 - my_b, a_at, zz].astype(F32) + rd[h, 0, a_at, zz].astype(F32)
            ).astype(BF)
            return carry

        lax.fori_loop(0, 2 * NZ, one, 0)
        return rpush(sb.at[h], rb.at[h], 7 * h + 2, part_b)

    def sum_b(h, a_at, zz):
        return (
            gb[h, c, my_b, a_at, zz].astype(F32)
            + rd[h, 1, a_at, zz].astype(F32)
            + rb[h, a_at, zz].astype(F32)
        )

    def send_a(h, copies, copy_b):
        copies[1].wait_recv()
        copy_b.wait_recv()

        def one(zz, carry):
            sa[h, zz] = sum_b(h, 1 - my_a, zz).astype(BF)
            return carry

        lax.fori_loop(0, NZ, one, 0)
        return rpush(sa.at[h], ra.at[h], 7 * h + 3, part_a)

    def send_z(h, copy_a):
        copy_a.wait_recv()
        copies = []
        for k in (2, 1, 3):
            zz = (z + k) % NZ
            sz[h, k] = (sum_b(h, my_a, zz) + ra[h, zz].astype(F32)).astype(BF)
            copies.append(rpush(sz.at[h, k], rz.at[h, k], 7 * h + 3 + k, zdev[k]))
        kz[h] = sum_b(h, my_a, z) + ra[h, z].astype(F32)
        return copies

    def finish(h, copies):
        for copy in copies:
            copy.wait_recv()
        g_ref[:, h * half : (h + 1) * half] = (
            kz[h] + rz[h, 1].astype(F32) + rz[h, 2].astype(F32) + rz[h, 3].astype(F32)
        )

    d0 = produce(0)
    own_dk = dot_tn(dst_[1], qs[...]) * inv_root
    own_dv = dot_tn(pst[1], dos[...])
    b0 = send_b(0, d0)

    @pl.when(s < 7)
    def _():
        back.wait_recv()

    gp[:, half : half + hd] = (own_dk + dkv[1, :, :hd].astype(F32)).astype(BF)
    gp[:, half + hd :] = (own_dv + dkv[1, :, hd:].astype(F32)).astype(BF)
    d1 = produce(1)
    b1 = send_b(1, d1)

    def input_grad(j, carry):
        width = dxv.shape[1] // 8
        at = pl.multiple_of(j * width, width)
        ws = wv[pl.ds(j * 4, 4)].reshape(width, wv.shape[2])
        dxv[:, pl.ds(at, width)] = dot_nt(gp[...], ws).astype(BF)
        return carry

    lax.fori_loop(0, 8, input_grad, 0)
    store_dx = pltpu.make_async_copy(dxv, dx_hbm.at[0], osem)
    store_dx.start()

    a0 = send_a(0, d0, b0)
    z0 = send_z(0, a0)
    a1 = send_a(1, d1, b1)
    z1 = send_z(1, a1)
    finish(0, z0)
    finish(1, z1)

    store_dx.wait()
    for copy in sent + rsent:
        copy.wait_send()

    @pl.when(s < 7)
    def _():
        halo.wait_send()

    @pl.when(s > 0)
    def _():
        back.wait_send()


def kernel_body(layer_inputs, doc_start, w_qkv, d_context):
    tok, width = layer_inputs.shape[1:]
    rows, cols = w_qkv.shape
    hd = cols // 4
    half = 2 * hd
    blocks = width // rows
    dma = pltpu.SemaphoreType.DMA
    return pl.pallas_call(
        fused,
        out_shape=(
            jax.ShapeDtypeStruct(layer_inputs.shape, BF),
            jax.ShapeDtypeStruct((rows, cols), F32),
        ),
        in_specs=[
            pl.BlockSpec(memory_space=pl.ANY),
            pl.BlockSpec(memory_space=pltpu.VMEM),
            pl.BlockSpec(memory_space=pl.ANY),
            pl.BlockSpec(memory_space=pltpu.VMEM),
        ],
        out_specs=(
            pl.BlockSpec(memory_space=pl.ANY),
            pl.BlockSpec(memory_space=pltpu.VMEM),
        ),
        scratch_shapes=[
            pltpu.VMEM((tok, width), BF),
            pltpu.VMEM((2, 2, 2, NZ, rows, tok), BF),
            pltpu.VMEM((blocks, rows, cols), BF),
            pltpu.VMEM((tok, cols), F32),
            pltpu.VMEM((2 * tok, hd), BF),
            pltpu.VMEM((2 * tok, hd), BF),
            pltpu.VMEM((2, tok, half), BF),
            pltpu.VMEM((2, tok, half), BF),
            pltpu.VMEM((2, 2 * tok, tok), BF),
            pltpu.VMEM((2, 2 * tok, tok), BF),
            pltpu.VMEM((tok, cols), BF),
            pltpu.VMEM((tok, width), BF),
            pltpu.VMEM((2, 2, 2, 2, NZ, rows, half), BF),
            pltpu.VMEM((2, 2, 2, NZ, rows, half), BF),
            pltpu.VMEM((2, 2, NZ, rows, half), BF),
            pltpu.VMEM((2, 2, NZ, rows, half), BF),
            pltpu.VMEM((2, NZ, rows, half), BF),
            pltpu.VMEM((2, NZ, rows, half), BF),
            pltpu.VMEM((2, NZ, rows, half), BF),
            pltpu.VMEM((2, NZ, rows, half), BF),
            pltpu.VMEM((2, rows, half), F32),
            dma((2,)),
            dma((32,)),
            dma((32,)),
            dma((2,)),
            dma((2,)),
            dma((14,)),
            dma((14,)),
            dma,
        ],
        compiler_params=pltpu.CompilerParams(
            collective_id=0, has_side_effects=True, vmem_limit_bytes=48 * 1024 * 1024
        ),
    )(layer_inputs, doc_start, w_qkv, d_context)


def solution(mesh):
    fits = mesh.shape["seq"] == 8 and mesh.shape["dp"] == 4
    return jax.shard_map(
        kernel_body if fits else body,
        mesh=mesh,
        in_specs=(
            P("dp", "seq", None),
            P("dp", "seq"),
            P(("seq", "dp"), None),
            P("dp", "seq", None),
        ),
        out_specs=(P("dp", "seq", None), P(("seq", "dp"), None)),
        check_vma=False,
    )
```

```python
import jax
import jax.numpy as jnp
from jax import lax
from jax.experimental import pallas as pl
from jax.experimental.pallas import tpu as pltpu
from jax.sharding import PartitionSpec as P

WIN = 256


def from_partner(block, axis, stride):
    count = lax.axis_size(axis)
    route = []
    for low in range(count):
        high = low | 1 << stride
        if high != low and high < count:
            route += [(low, high), (high, low)]
    return lax.ppermute(block, axis, route)


def from_behind(block, axis, distance):
    devices = range(lax.axis_size(axis))
    route = [(i - distance, i) for i in devices if i - distance in devices]
    return lax.ppermute(block, axis, route)


def masked_scores(queries, key_rows, doc_first, query_pos, key_pos):
    inv_root = queries.shape[2] ** (-0.5)
    scores = (
        jnp.einsum("rhd,kd->hrk", queries, key_rows, preferred_element_type=jnp.float32) * inv_root
    )
    visible = (
        (key_pos[None, :] <= query_pos[:, None])
        & (key_pos[None, :] > query_pos[:, None] - WIN)
        & (key_pos[None, :] >= doc_first[:, None])
    )
    return jnp.where(visible[None, :, :], scores, -jnp.inf)


def backward_terms(queries, key_rows, value_rows, out_grad, attn_probs, prob_low, row_dot):
    inv_root = queries.shape[2] ** (-0.5)
    prob_grad = jnp.einsum("rhd,kd->hrk", out_grad, value_rows, preferred_element_type=jnp.float32)
    score_grad = (attn_probs * (prob_grad - row_dot[:, :, None])).astype(jnp.bfloat16)
    grad_query = (
        jnp.einsum("hrk,kd->rhd", score_grad, key_rows, preferred_element_type=jnp.float32)
        * inv_root
    )
    grad_keys = (
        jnp.einsum("hrk,rhd->kd", score_grad, queries, preferred_element_type=jnp.float32)
        * inv_root
    )
    grad_values = jnp.einsum("hrk,rhd->kd", prob_low, out_grad, preferred_element_type=jnp.float32)
    return (grad_query, grad_keys, grad_values)


def local_pass(queries, key_rows, value_rows, out_grad, doc_first, query_pos, key_pos):
    scores = masked_scores(queries, key_rows, doc_first, query_pos, key_pos)
    row_max = jnp.max(scores, axis=2)
    log_total = row_max + jnp.log(jnp.sum(jnp.exp(scores - row_max[:, :, None]), axis=2))
    attn_probs = jnp.exp(scores - log_total[:, :, None])
    prob_low = attn_probs.astype(jnp.bfloat16)
    context = jnp.einsum("hrk,kd->rhd", prob_low, value_rows, preferred_element_type=jnp.float32)
    row_dot = jnp.sum(out_grad.astype(jnp.float32) * context, axis=2).T
    grad_query, grad_keys, grad_values = backward_terms(
        queries, key_rows, value_rows, out_grad, attn_probs, prob_low, row_dot
    )
    return (grad_query, grad_keys, grad_values, log_total, row_dot)


def halve_over_seq(buffer, bit_index):
    half_rows = buffer.shape[0] // 2
    my_bit = lax.axis_index("seq") >> bit_index & 1
    kept_half = lax.dynamic_slice_in_dim(buffer, my_bit * half_rows, half_rows, 0)
    sent_half = lax.dynamic_slice_in_dim(buffer, (1 - my_bit) * half_rows, half_rows, 0)
    return kept_half + from_partner(sent_half.astype(jnp.bfloat16), "seq", bit_index).astype(
        sent_half.dtype
    )


def halve_over_dp(buffer, bit_index):
    half_rows = buffer.shape[0] // 2
    my_bit = lax.axis_index("dp") >> bit_index & 1
    kept_half = lax.dynamic_slice_in_dim(buffer, my_bit * half_rows, half_rows, 0)
    sent_half = lax.dynamic_slice_in_dim(buffer, (1 - my_bit) * half_rows, half_rows, 0)
    return kept_half + from_partner(sent_half.astype(jnp.bfloat16), "dp", bit_index).astype(
        sent_half.dtype
    )


def body(layer_inputs, doc_start, w_qkv, d_context):
    x_local = layer_inputs[0]
    tok_rows = x_local.shape[0]
    q_width = d_context.shape[2]
    head_dim = (w_qkv.shape[1] - q_width) // 2
    heads = q_width // head_dim
    out_grad = d_context[0].reshape(tok_rows, heads, head_dim)
    doc_first = doc_start[0]
    positions = lax.axis_index("seq") * tok_rows + jnp.arange(tok_rows, dtype=jnp.int32)
    full_weights = lax.all_gather(w_qkv, ("seq", "dp"), axis=0, tiled=True)
    projected = jnp.dot(x_local, full_weights, preferred_element_type=jnp.float32)
    projected = projected.astype(jnp.bfloat16)
    queries = projected[:, :q_width].reshape(tok_rows, heads, head_dim)
    key_value = projected[:, q_width:]
    prior = from_behind(key_value, "seq", 1)
    key_rows = jnp.concatenate([prior[:, :head_dim], key_value[:, :head_dim]], axis=0)
    value_rows = jnp.concatenate([prior[:, head_dim:], key_value[:, head_dim:]], axis=0)
    key_pos = jnp.concatenate([positions - tok_rows, positions])
    grad_query, grad_keys, grad_values, log_total, row_dot = local_pass(
        queries, key_rows, value_rows, out_grad, doc_first, positions, key_pos
    )
    returned = from_behind(
        jnp.concatenate([grad_keys[:tok_rows], grad_values[:tok_rows]], axis=1).astype(
            jnp.bfloat16
        ),
        "seq",
        -1,
    ).astype(jnp.float32)
    far_keys = returned[:, :head_dim]
    far_values = returned[:, head_dim:]
    key_grad = (grad_keys[tok_rows:] + far_keys).astype(jnp.bfloat16)
    value_grad = (grad_values[tok_rows:] + far_values).astype(jnp.bfloat16)
    grad_proj = jnp.concatenate(
        [grad_query.astype(jnp.bfloat16).reshape(tok_rows, q_width), key_grad, value_grad], axis=1
    )
    input_grad = lax.dot_general(
        grad_proj, full_weights, (((1,), (1,)), ((), ())), preferred_element_type=jnp.float32
    )
    input_grad = input_grad.astype(jnp.bfloat16).reshape(1, tok_rows, x_local.shape[1])
    partial_grad = lax.dot_general(
        x_local, grad_proj, (((0,), (0,)), ((), ())), preferred_element_type=jnp.float32
    )
    seq_count = lax.axis_size("seq")
    dp_count = lax.axis_size("dp")
    seq_levels = seq_count.bit_length() - 1
    dp_levels = dp_count.bit_length() - 1
    buffer = partial_grad
    for bit_index in range(seq_levels - 1, -1, -1):
        buffer = halve_over_seq(buffer, bit_index)
    for bit_index in range(dp_levels - 1, -1, -1):
        buffer = halve_over_dp(buffer, bit_index)
    return (input_grad, buffer)


BF = jnp.bfloat16
F32 = jnp.float32
NZ = 4
ORDER = (0, 1, 3, 2)


def dot_nn(a, b):
    return jnp.dot(a, b, preferred_element_type=F32)


def dot_nt(a, b):
    return lax.dot_general(a, b, (((1,), (1,)), ((), ())), preferred_element_type=F32)


def dot_tn(a, b):
    return lax.dot_general(a, b, (((0,), (0,)), ((), ())), preferred_element_type=F32)


def flip(v, f):
    return v + f * (1 - 2 * v)


def remote(src, dst, send, recv, device):
    return pltpu.make_async_remote_copy(
        src_ref=src,
        dst_ref=dst,
        send_sem=send,
        recv_sem=recv,
        device_id=device,
        device_id_type=pl.DeviceIdType.MESH,
    )


CHUNKS = (2, 1, 3, 0)


def fused(
    x_hbm, doc_hbm, w_hbm, do_hbm, dx_hbm, g_ref,
    xv, docv, xt, wv, acc, qs, dos, pgs, kv, dkv, pst, dst_, gp, dxv,
    gb, rd, sb, rb, sa, ra, sz, rz, kz,
    lsem, wsend, wrecv, hsend, hrecv, gsend, grecv, osem,
):
    s = lax.axis_index("seq")
    d = lax.axis_index("dp")
    z, y = s // 2, s % 2
    x, c = d // 2, d % 2
    tok = xv.shape[0]
    rows = wv.shape[2]
    hd = qs.shape[1]
    half = 2 * hd
    inv_root = hd ** (-0.5)
    my_a = x * (1 - c) + y * c
    my_b = y * (1 - c) + x * c

    def device(zz, yy, xx, cc):
        return (zz * 2 + yy, xx * 2 + cc)

    sib = device(z, y, x, 1 - c)
    part_a = device(z, flip(y, c), flip(x, 1 - c), c)
    part_b = device(z, flip(y, 1 - c), flip(x, c), c)
    zdev = [device((z + k) % NZ, y, x, c) for k in range(NZ)]

    def plane_block(k, a, b, plane):
        zz = (z + NZ - k) % NZ
        xx = flip(x, a * (1 - plane) + b * plane)
        yy = flip(y, b * (1 - plane) + a * plane)
        return ((zz * 2 + yy) * 2 + xx) * 2 + plane

    own = s * 4 + d
    loads = [
        pltpu.make_async_copy(w_hbm.at[:, pl.ds(half, half)], wv.at[1, own], lsem.at[0]),
        pltpu.make_async_copy(w_hbm.at[:, pl.ds(0, half)], wv.at[0, own], lsem.at[1]),
        pltpu.make_async_copy(x_hbm.at[0], xv, lsem.at[2]),
        pltpu.make_async_copy(doc_hbm, docv, lsem.at[3]),
    ] + [
        pltpu.make_async_copy(
            do_hbm.at[0, :, pl.ds(h * hd, hd)], dos.at[pl.ds(h * tok, tok)], lsem.at[4 + h]
        )
        for h in range(2)
    ]
    for load in loads:
        load.start()

    barrier = pltpu.get_barrier_semaphore()
    for dev in [sib, part_a, part_b] + zdev[1:]:
        pl.semaphore_signal(barrier, inc=1, device_id=dev, device_id_type=pl.DeviceIdType.MESH)
    extra_up = (y == 1) & (z < NZ - 1)
    extra_down = (y == 0) & (z > 0)

    @pl.when(extra_up)
    def _():
        pl.semaphore_signal(
            barrier, inc=1, device_id=(s + 1, d), device_id_type=pl.DeviceIdType.MESH
        )

    @pl.when(extra_down)
    def _():
        pl.semaphore_signal(
            barrier, inc=1, device_id=(s - 1, d), device_id_type=pl.DeviceIdType.MESH
        )

    loads[0].wait()
    loads[1].wait()

    @pl.when(extra_up | extra_down)
    def _():
        pl.semaphore_wait(barrier, 7)

    @pl.when(jnp.logical_not(extra_up | extra_down))
    def _():
        pl.semaphore_wait(barrier, 6)

    sent = []

    def push(h, block, dev, index):
        copy = remote(
            wv.at[h, block], wv.at[h, block], wsend.at[h, index], wrecv.at[h, index], dev
        )
        copy.start()
        sent.append(copy)

    def arrived(h, block, index):
        ref = wv.at[h, block]
        remote(ref, ref, wsend.at[h, 0], wrecv.at[h, index], sib).wait_recv()

    def push_z(h):
        for k in ORDER[1:]:
            push(h, own, zdev[k], k)

    def stage_z(h, k):
        block = plane_block(k, 0, 0, c)
        if k:
            arrived(h, block, k)
        push(h, block, part_a, 4 + k)
        push(h, block, part_b, 8 + 2 * k)
        push(h, block, sib, 16 + 4 * k)

    def stage_a(h, k):
        block = plane_block(k, 1, 0, c)
        arrived(h, block, 4 + k)
        push(h, block, part_b, 9 + 2 * k)
        push(h, block, sib, 17 + 4 * k)

    def stage_b(h, k):
        for a in range(2):
            block = plane_block(k, a, 1, c)
            arrived(h, block, 8 + 2 * k + a)
            push(h, block, sib, 18 + 4 * k + a)

    def stage_d(h, k):
        for b in range(2):
            for a in range(2):
                arrived(h, plane_block(k, a, b, 1 - c), 16 + 4 * k + 2 * b + a)
        zz = (z + NZ - k) % NZ
        span = 8 * rows
        xs = xv[:, pl.ds(pl.multiple_of(zz * span, span), span)]
        part = dot_nn(xs, wv[h, pl.ds(zz * 8, 8)].reshape(span, half))
        if k == ORDER[0]:
            acc[h] = part
        else:
            acc[h] += part

    def transpose_x(j, carry):
        zz, yy, xx, cc = j // 8, (j // 4) % 2, (j // 2) % 2, j % 2
        b_at = yy * (1 - cc) + xx * cc
        a_at = xx * (1 - cc) + yy * cc
        xt[zz, cc, b_at, a_at] = xv[:, pl.ds(pl.multiple_of(j * rows, rows), rows)].T
        return carry

    halo = remote(kv.at[1], kv.at[0], hsend.at[0], hrecv.at[0], ((s + 1) % 8, d))

    def send_halo():
        kv[1] = acc[1].astype(BF)

        @pl.when(s < 7)
        def _():
            halo.start()

        @pl.when(s == 0)
        def _():
            kv[0] = jnp.zeros_like(kv[0])

    def value_grads():
        @pl.when(s > 0)
        def _():
            halo.wait_recv()

        for j in range(2):
            pgs[j] = dot_nt(dos[...], kv[j, :, hd:])

    steps = [(h, k) for h in (1, 0) for k in ORDER]
    n_steps = len(steps)
    push_z(1)
    for t in range(n_steps + 3):
        if t == 3:
            push_z(0)
        if 0 <= t - 1 < n_steps:
            stage_a(*steps[t - 1])
        if t < n_steps:
            stage_z(*steps[t])
        if 0 <= t - 2 < n_steps:
            stage_b(*steps[t - 2])
        if t == 0:
            for load in loads[2:]:
                load.wait()
            doc = jnp.broadcast_to(docv[...], (tok, tok)).T
            row = lax.broadcasted_iota(jnp.int32, (tok, tok), 0)
            col = lax.broadcasted_iota(jnp.int32, (tok, tok), 1)
            vis_own = jnp.where((col <= row) & (col + s * tok >= doc), 0.0, -jnp.inf)
            vis_pri = jnp.where((col > row) & (col + (s - 1) * tok >= doc), 0.0, -jnp.inf)
        if t == n_steps + 2:
            value_grads()
        if 0 <= t - 3 < n_steps:
            stage_d(*steps[t - 3])
        if t == 6:
            send_halo()
        if t < n_steps:
            lax.fori_loop(t * 4, t * 4 + 4, transpose_x, 0)

    for h in range(2):
        qs[h * tok : (h + 1) * tok, :] = acc[0, :, h * hd : (h + 1) * hd].astype(BF)
    k_own = kv[1, :, :hd]
    k_pri = kv[0, :, :hd]
    for h in range(2):
        span = slice(h * tok, (h + 1) * tok)
        s_own = dot_nt(qs[span, :], k_own) * inv_root + vis_own
        s_pri = dot_nt(qs[span, :], k_pri) * inv_root + vis_pri
        pg_own = pgs[1, span, :]
        pg_pri = pgs[0, span, :]
        top = jnp.max(jnp.maximum(s_own, s_pri), axis=1, keepdims=True)
        e_own = jnp.exp(s_own - top)
        e_pri = jnp.exp(s_pri - top)
        scale = 1.0 / jnp.sum(e_own + e_pri, axis=1, keepdims=True)
        p_own = e_own * scale
        p_pri = e_pri * scale
        l_own = p_own.astype(BF)
        l_pri = p_pri.astype(BF)
        row_dot = jnp.sum(
            l_own.astype(F32) * pg_own + l_pri.astype(F32) * pg_pri, axis=1, keepdims=True
        )
        pst[0, span, :] = l_pri
        pst[1, span, :] = l_own
        dst_[0, span, :] = (p_pri * (pg_pri - row_dot)).astype(BF)
        dst_[1, span, :] = (p_own * (pg_own - row_dot)).astype(BF)

    dkv[0, :, :hd] = (dot_tn(dst_[0], qs[...]) * inv_root).astype(BF)
    dkv[0, :, hd:] = dot_tn(pst[0], dos[...]).astype(BF)
    back = remote(dkv.at[0], dkv.at[1], hsend.at[1], hrecv.at[1], ((s + 7) % 8, d))

    @pl.when(s > 0)
    def _():
        back.start()

    @pl.when(s == 7)
    def _():
        dkv[1] = jnp.zeros_like(dkv[1])

    for h in range(2):
        span = slice(h * tok, (h + 1) * tok)
        gp[0, :, h * hd : (h + 1) * hd] = (
            (dot_nn(dst_[1, span, :], k_own) + dot_nn(dst_[0, span, :], k_pri)) * inv_root
        ).astype(BF)

    rsent = {}

    def rpush(src, dst, h, k, stage, dev):
        index = (h * NZ + k) * 4 + stage
        copy = remote(src, dst, gsend.at[index], grecv.at[index], dev)
        copy.start()
        rsent[h, k, stage] = copy

    def weight_part(h, k, plane):
        lhs = xt[(z + k) % NZ, plane].reshape(4 * rows, tok)
        gb[h, k, plane] = dot_nn(lhs, gp[h]).astype(BF).reshape(2, 2, rows, half)

    def produce(h, k):
        weight_part(h, k, 1 - c)
        rpush(gb.at[h, k, 1 - c], rd.at[h, k], h, k, 0, sib)
        weight_part(h, k, c)

    def chip_sum(h, k, b_at, a_at):
        return gb[h, k, c, b_at, a_at].astype(F32) + rd[h, k, b_at, a_at].astype(F32)

    def send_b(h, k):
        rsent[h, k, 0].wait_recv()
        for a_at in range(2):
            sb[h, k, a_at] = chip_sum(h, k, 1 - my_b, a_at).astype(BF)
        rpush(sb.at[h, k], rb.at[h, k], h, k, 1, part_b)

    def send_a(h, k):
        rsent[h, k, 1].wait_recv()
        sa[h, k] = (
            chip_sum(h, k, my_b, 1 - my_a) + rb[h, k, 1 - my_a].astype(F32)
        ).astype(BF)
        rpush(sa.at[h, k], ra.at[h, k], h, k, 2, part_a)

    def send_z(h, k):
        rsent[h, k, 2].wait_recv()
        total = (
            chip_sum(h, k, my_b, my_a)
            + rb[h, k, my_a].astype(F32)
            + ra[h, k].astype(F32)
        )
        if k:
            sz[h, k] = total.astype(BF)
            rpush(sz.at[h, k], rz.at[h, k], h, k, 3, zdev[k])
        else:
            kz[h] = total

    def finish(h):
        total = kz[h]
        for k in CHUNKS[:3]:
            rsent[h, k, 3].wait_recv()
            total += rz[h, k].astype(F32)
        g_ref[:, h * half : (h + 1) * half] = total

    def input_grad(j, carry):
        width = dxv.shape[1] // 8
        at = pl.multiple_of(j * width, width)
        ws = [wv[h, pl.ds(j * 4, 4)].reshape(width, half) for h in range(2)]
        dxv[:, pl.ds(at, width)] = (dot_nt(gp[0], ws[0]) + dot_nt(gp[1], ws[1])).astype(BF)
        return carry

    for i in range(NZ + 1):
        if i < NZ:
            produce(0, CHUNKS[i])
        if i > 0:
            send_b(0, CHUNKS[i - 1])
    own_dk = dot_tn(dst_[1], qs[...]) * inv_root
    own_dv = dot_tn(pst[1], dos[...])

    @pl.when(s < 7)
    def _():
        back.wait_recv()

    gp[1, :, :hd] = (own_dk + dkv[1, :, :hd].astype(F32)).astype(BF)
    gp[1, :, hd:] = (own_dv + dkv[1, :, hd:].astype(F32)).astype(BF)
    for i in range(NZ + 1):
        if i < NZ:
            produce(1, CHUNKS[i])
            send_a(0, CHUNKS[i])
        if i > 0:
            send_b(1, CHUNKS[i - 1])
    for i in range(NZ):
        send_z(0, CHUNKS[i])
        lax.fori_loop(2 * i, 2 * i + 2, input_grad, 0)
    store_dx = pltpu.make_async_copy(dxv, dx_hbm.at[0], osem)
    store_dx.start()
    for i in range(NZ + 1):
        if i < NZ:
            send_a(1, CHUNKS[i])
        if i > 0:
            send_z(1, CHUNKS[i - 1])
    finish(0)
    finish(1)

    store_dx.wait()
    for copy in sent + list(rsent.values()):
        copy.wait_send()

    @pl.when(s < 7)
    def _():
        halo.wait_send()

    @pl.when(s > 0)
    def _():
        back.wait_send()


def kernel_body(layer_inputs, doc_start, w_qkv, d_context):
    tok, width = layer_inputs.shape[1:]
    rows, cols = w_qkv.shape
    hd = cols // 4
    half = 2 * hd
    blocks = width // rows
    dma = pltpu.SemaphoreType.DMA
    block = (rows, half)
    return pl.pallas_call(
        fused,
        out_shape=(
            jax.ShapeDtypeStruct(layer_inputs.shape, BF),
            jax.ShapeDtypeStruct((rows, cols), F32),
        ),
        in_specs=[pl.BlockSpec(memory_space=pl.ANY)] * 4,
        out_specs=(
            pl.BlockSpec(memory_space=pl.ANY),
            pl.BlockSpec(memory_space=pltpu.VMEM),
        ),
        scratch_shapes=[
            pltpu.VMEM((tok, width), BF),
            pltpu.VMEM((1, tok), jnp.int32),
            pltpu.VMEM((NZ, 2, 2, 2, rows, tok), BF),
            pltpu.VMEM((2, blocks) + block, BF),
            pltpu.VMEM((2, tok, half), F32),
            pltpu.VMEM((2 * tok, hd), BF),
            pltpu.VMEM((2 * tok, hd), BF),
            pltpu.VMEM((2, 2 * tok, tok), F32),
            pltpu.VMEM((2, tok, half), BF),
            pltpu.VMEM((2, tok, half), BF),
            pltpu.VMEM((2, 2 * tok, tok), BF),
            pltpu.VMEM((2, 2 * tok, tok), BF),
            pltpu.VMEM((2, tok, half), BF),
            pltpu.VMEM((tok, width), BF),
            pltpu.VMEM((2, NZ, 2, 2, 2) + block, BF),
            pltpu.VMEM((2, NZ, 2, 2) + block, BF),
            pltpu.VMEM((2, NZ, 2) + block, BF),
            pltpu.VMEM((2, NZ, 2) + block, BF),
            pltpu.VMEM((2, NZ) + block, BF),
            pltpu.VMEM((2, NZ) + block, BF),
            pltpu.VMEM((2, NZ) + block, BF),
            pltpu.VMEM((2, NZ) + block, BF),
            pltpu.VMEM((2,) + block, F32),
            dma((6,)),
            dma((2, 32)),
            dma((2, 32)),
            dma((2,)),
            dma((2,)),
            dma((32,)),
            dma((32,)),
            dma,
        ],
        compiler_params=pltpu.CompilerParams(
            collective_id=0, has_side_effects=True, vmem_limit_bytes=60 * 1024 * 1024
        ),
    )(layer_inputs, doc_start, w_qkv, d_context)


def solution(mesh):
    fits = mesh.shape["seq"] == 8 and mesh.shape["dp"] == 4
    return jax.shard_map(
        kernel_body if fits else body,
        mesh=mesh,
        in_specs=(
            P("dp", "seq", None),
            P("dp", "seq"),
            P(("seq", "dp"), None),
            P("dp", "seq", None),
        ),
        out_specs=(P("dp", "seq", None), P(("seq", "dp"), None)),
        check_vma=False,
    )
```

```python
import jax
import jax.numpy as jnp
from jax import lax
from jax.experimental import pallas as pl
from jax.experimental.pallas import tpu as pltpu
from jax.sharding import PartitionSpec as P

WIN = 256


def from_partner(block, axis, stride):
    count = lax.axis_size(axis)
    route = []
    for low in range(count):
        high = low | 1 << stride
        if high != low and high < count:
            route += [(low, high), (high, low)]
    return lax.ppermute(block, axis, route)


def from_behind(block, axis, distance):
    devices = range(lax.axis_size(axis))
    route = [(i - distance, i) for i in devices if i - distance in devices]
    return lax.ppermute(block, axis, route)


def masked_scores(queries, key_rows, doc_first, query_pos, key_pos):
    inv_root = queries.shape[2] ** (-0.5)
    scores = (
        jnp.einsum("rhd,kd->hrk", queries, key_rows, preferred_element_type=jnp.float32) * inv_root
    )
    visible = (
        (key_pos[None, :] <= query_pos[:, None])
        & (key_pos[None, :] > query_pos[:, None] - WIN)
        & (key_pos[None, :] >= doc_first[:, None])
    )
    return jnp.where(visible[None, :, :], scores, -jnp.inf)


def backward_terms(queries, key_rows, value_rows, out_grad, attn_probs, prob_low, row_dot):
    inv_root = queries.shape[2] ** (-0.5)
    prob_grad = jnp.einsum("rhd,kd->hrk", out_grad, value_rows, preferred_element_type=jnp.float32)
    score_grad = (attn_probs * (prob_grad - row_dot[:, :, None])).astype(jnp.bfloat16)
    grad_query = (
        jnp.einsum("hrk,kd->rhd", score_grad, key_rows, preferred_element_type=jnp.float32)
        * inv_root
    )
    grad_keys = (
        jnp.einsum("hrk,rhd->kd", score_grad, queries, preferred_element_type=jnp.float32)
        * inv_root
    )
    grad_values = jnp.einsum("hrk,rhd->kd", prob_low, out_grad, preferred_element_type=jnp.float32)
    return (grad_query, grad_keys, grad_values)


def local_pass(queries, key_rows, value_rows, out_grad, doc_first, query_pos, key_pos):
    scores = masked_scores(queries, key_rows, doc_first, query_pos, key_pos)
    row_max = jnp.max(scores, axis=2)
    log_total = row_max + jnp.log(jnp.sum(jnp.exp(scores - row_max[:, :, None]), axis=2))
    attn_probs = jnp.exp(scores - log_total[:, :, None])
    prob_low = attn_probs.astype(jnp.bfloat16)
    context = jnp.einsum("hrk,kd->rhd", prob_low, value_rows, preferred_element_type=jnp.float32)
    row_dot = jnp.sum(out_grad.astype(jnp.float32) * context, axis=2).T
    grad_query, grad_keys, grad_values = backward_terms(
        queries, key_rows, value_rows, out_grad, attn_probs, prob_low, row_dot
    )
    return (grad_query, grad_keys, grad_values, log_total, row_dot)


def halve_over_seq(buffer, bit_index):
    half_rows = buffer.shape[0] // 2
    my_bit = lax.axis_index("seq") >> bit_index & 1
    kept_half = lax.dynamic_slice_in_dim(buffer, my_bit * half_rows, half_rows, 0)
    sent_half = lax.dynamic_slice_in_dim(buffer, (1 - my_bit) * half_rows, half_rows, 0)
    return kept_half + from_partner(sent_half.astype(jnp.bfloat16), "seq", bit_index).astype(
        sent_half.dtype
    )


def halve_over_dp(buffer, bit_index):
    half_rows = buffer.shape[0] // 2
    my_bit = lax.axis_index("dp") >> bit_index & 1
    kept_half = lax.dynamic_slice_in_dim(buffer, my_bit * half_rows, half_rows, 0)
    sent_half = lax.dynamic_slice_in_dim(buffer, (1 - my_bit) * half_rows, half_rows, 0)
    return kept_half + from_partner(sent_half.astype(jnp.bfloat16), "dp", bit_index).astype(
        sent_half.dtype
    )


def body(layer_inputs, doc_start, w_qkv, d_context):
    x_local = layer_inputs[0]
    tok_rows = x_local.shape[0]
    q_width = d_context.shape[2]
    head_dim = (w_qkv.shape[1] - q_width) // 2
    heads = q_width // head_dim
    out_grad = d_context[0].reshape(tok_rows, heads, head_dim)
    doc_first = doc_start[0]
    positions = lax.axis_index("seq") * tok_rows + jnp.arange(tok_rows, dtype=jnp.int32)
    full_weights = lax.all_gather(w_qkv, ("seq", "dp"), axis=0, tiled=True)
    projected = jnp.dot(x_local, full_weights, preferred_element_type=jnp.float32)
    projected = projected.astype(jnp.bfloat16)
    queries = projected[:, :q_width].reshape(tok_rows, heads, head_dim)
    key_value = projected[:, q_width:]
    prior = from_behind(key_value, "seq", 1)
    key_rows = jnp.concatenate([prior[:, :head_dim], key_value[:, :head_dim]], axis=0)
    value_rows = jnp.concatenate([prior[:, head_dim:], key_value[:, head_dim:]], axis=0)
    key_pos = jnp.concatenate([positions - tok_rows, positions])
    grad_query, grad_keys, grad_values, log_total, row_dot = local_pass(
        queries, key_rows, value_rows, out_grad, doc_first, positions, key_pos
    )
    returned = from_behind(
        jnp.concatenate([grad_keys[:tok_rows], grad_values[:tok_rows]], axis=1).astype(
            jnp.bfloat16
        ),
        "seq",
        -1,
    ).astype(jnp.float32)
    far_keys = returned[:, :head_dim]
    far_values = returned[:, head_dim:]
    key_grad = (grad_keys[tok_rows:] + far_keys).astype(jnp.bfloat16)
    value_grad = (grad_values[tok_rows:] + far_values).astype(jnp.bfloat16)
    grad_proj = jnp.concatenate(
        [grad_query.astype(jnp.bfloat16).reshape(tok_rows, q_width), key_grad, value_grad], axis=1
    )
    input_grad = lax.dot_general(
        grad_proj, full_weights, (((1,), (1,)), ((), ())), preferred_element_type=jnp.float32
    )
    input_grad = input_grad.astype(jnp.bfloat16).reshape(1, tok_rows, x_local.shape[1])
    partial_grad = lax.dot_general(
        x_local, grad_proj, (((0,), (0,)), ((), ())), preferred_element_type=jnp.float32
    )
    seq_count = lax.axis_size("seq")
    dp_count = lax.axis_size("dp")
    seq_levels = seq_count.bit_length() - 1
    dp_levels = dp_count.bit_length() - 1
    buffer = partial_grad
    for bit_index in range(seq_levels - 1, -1, -1):
        buffer = halve_over_seq(buffer, bit_index)
    for bit_index in range(dp_levels - 1, -1, -1):
        buffer = halve_over_dp(buffer, bit_index)
    return (input_grad, buffer)


BF = jnp.bfloat16
F32 = jnp.float32
NZ = 4
ORDER = (
    ("z", 1, 0), ("z", 1, 1), ("a", 1, 0), ("b", 1, 0, 0), ("z", 1, 2), ("prep",), ("a", 1, 1),
    ("b", 1, 1, 0), ("b", 1, 0, 1), ("z", 1, 3), ("turn", 0), ("b", 1, 2, 0), ("a", 1, 2),
    ("turn", 1), ("b", 1, 1, 1), ("b", 1, 3, 0), ("a", 1, 3), ("z", 0, 0), ("d", 1, 0),
    ("b", 1, 2, 1), ("d", 1, 1), ("z", 0, 1), ("b", 1, 3, 1), ("z", 0, 2), ("a", 0, 0),
    ("d", 1, 2), ("b", 0, 0, 0), ("d", 1, 3), ("halo",), ("z", 0, 3), ("b", 0, 1, 0),
    ("b", 0, 2, 0), ("a", 0, 1), ("a", 0, 2), ("turn", 2), ("b", 0, 0, 1), ("turn", 3),
    ("b", 0, 2, 1), ("a", 0, 3), ("b", 0, 3, 0), ("b", 0, 1, 1), ("d", 0, 0), ("values",),
    ("b", 0, 3, 1), ("d", 0, 1), ("d", 0, 2), ("d", 0, 3),
)


def dot_nn(a, b):
    return jnp.dot(a, b, preferred_element_type=F32)


def dot_nt(a, b):
    return lax.dot_general(a, b, (((1,), (1,)), ((), ())), preferred_element_type=F32)


def dot_tn(a, b):
    return lax.dot_general(a, b, (((0,), (0,)), ((), ())), preferred_element_type=F32)


def flip(v, f):
    return v + f * (1 - 2 * v)


def remote(src, dst, send, recv, device):
    return pltpu.make_async_remote_copy(
        src_ref=src,
        dst_ref=dst,
        send_sem=send,
        recv_sem=recv,
        device_id=device,
        device_id_type=pl.DeviceIdType.MESH,
    )


CHUNKS = (2, 1, 3, 0)


def fused(
    x_hbm, doc_hbm, w_hbm, do_hbm, dx_hbm, g_ref,
    xv, docv, xt, wv, acc, qs, dos, pgs, kv, dkv, pst, dst_, gp, dxv,
    gb, rd, sb, rb, sa, ra, sz, rz, kz,
    lsem, wsend, wrecv, hsend, hrecv, gsend, grecv, osem,
):
    s = lax.axis_index("seq")
    d = lax.axis_index("dp")
    z, y = s // 2, s % 2
    x, c = d // 2, d % 2
    tok = xv.shape[0]
    rows = wv.shape[2]
    hd = qs.shape[1]
    half = 2 * hd
    inv_root = hd ** (-0.5)
    my_a = x * (1 - c) + y * c
    my_b = y * (1 - c) + x * c

    def device(zz, yy, xx, cc):
        return (zz * 2 + yy, xx * 2 + cc)

    sib = device(z, y, x, 1 - c)
    part_a = device(z, flip(y, c), flip(x, 1 - c), c)
    part_b = device(z, flip(y, 1 - c), flip(x, c), c)
    zdev = [device((z + k) % NZ, y, x, c) for k in range(NZ)]

    z_order = [
        z,
        jnp.where(z == 0, 1, jnp.where(z == 1, 0, jnp.where(z == 2, 3, 2))),
        jnp.where(z == 0, 2, jnp.where(z == 1, 2, 1)),
        jnp.where(z <= 1, 3, 0),
    ]

    def plane_block(k, a, b, plane):
        zz = z_order[k]
        xx = flip(x, a * (1 - plane) + b * plane)
        yy = flip(y, b * (1 - plane) + a * plane)
        return ((zz * 2 + yy) * 2 + xx) * 2 + plane

    own = s * 4 + d
    loads = [
        pltpu.make_async_copy(w_hbm.at[:, pl.ds(half, half)], wv.at[1, own], lsem.at[0]),
        pltpu.make_async_copy(w_hbm.at[:, pl.ds(0, half)], wv.at[0, own], lsem.at[1]),
        pltpu.make_async_copy(x_hbm.at[0], xv, lsem.at[2]),
        pltpu.make_async_copy(doc_hbm, docv, lsem.at[3]),
    ] + [
        pltpu.make_async_copy(
            do_hbm.at[0, :, pl.ds(h * hd, hd)], dos.at[pl.ds(h * tok, tok)], lsem.at[4 + h]
        )
        for h in range(2)
    ]
    for load in loads:
        load.start()

    barrier = pltpu.get_barrier_semaphore()
    for dev in [sib, part_a, part_b] + zdev[1:]:
        pl.semaphore_signal(barrier, inc=1, device_id=dev, device_id_type=pl.DeviceIdType.MESH)
    extra_up = (y == 1) & (z < NZ - 1)
    extra_down = (y == 0) & (z > 0)

    @pl.when(extra_up)
    def _():
        pl.semaphore_signal(
            barrier, inc=1, device_id=(s + 1, d), device_id_type=pl.DeviceIdType.MESH
        )

    @pl.when(extra_down)
    def _():
        pl.semaphore_signal(
            barrier, inc=1, device_id=(s - 1, d), device_id_type=pl.DeviceIdType.MESH
        )

    loads[0].wait()
    loads[1].wait()

    @pl.when(extra_up | extra_down)
    def _():
        pl.semaphore_wait(barrier, 7)

    @pl.when(jnp.logical_not(extra_up | extra_down))
    def _():
        pl.semaphore_wait(barrier, 6)

    sent = []

    def push(h, block, dev, index):
        copy = remote(
            wv.at[h, block], wv.at[h, block], wsend.at[h, index], wrecv.at[h, index], dev
        )
        copy.start()
        sent.append(copy)

    def arrived(h, block, index):
        ref = wv.at[h, block]
        remote(ref, ref, wsend.at[h, 0], wrecv.at[h, index], sib).wait_recv()

    line = []

    def push_line(h, block, zz):
        up = remote(
            wv.at[h, block], wv.at[h, block], wsend.at[h, zz], wrecv.at[h, zz], zdev[1]
        )
        down = remote(
            wv.at[h, block], wv.at[h, block], wsend.at[h, 32 + zz], wrecv.at[h, zz], zdev[3]
        )
        for copy, test in ((up, (zz <= z) & (z < NZ - 1)), (down, (zz >= z) & (z > 0))):
            line.append((copy, test))
            pl.when(test)(copy.start)

    def stage_z(h, k):
        block = plane_block(k, 0, 0, c)
        if k:
            arrived(h, block, z_order[k])
        push_line(h, block, z_order[k])
        push(h, block, part_a, 4 + k)
        push(h, block, part_b, 8 + 2 * k)
        push(h, block, sib, 16 + 4 * k)

    def stage_a(h, k):
        block = plane_block(k, 1, 0, c)
        arrived(h, block, 4 + k)
        push(h, block, part_b, 9 + 2 * k)
        push(h, block, sib, 17 + 4 * k)

    def stage_b(h, k, a):
        block = plane_block(k, a, 1, c)
        arrived(h, block, 8 + 2 * k + a)
        push(h, block, sib, 18 + 4 * k + a)

    def stage_d(h, k):
        for b in range(2):
            for a in range(2):
                arrived(h, plane_block(k, a, b, 1 - c), 16 + 4 * k + 2 * b + a)
        zz = z_order[k]
        span = 8 * rows
        xs = xv[:, pl.ds(pl.multiple_of(zz * span, span), span)]
        part = dot_nn(xs, wv[h, pl.ds(zz * 8, 8)].reshape(span, half))
        if k == 0:
            acc[h] = part
        else:
            acc[h] += part

    def transpose_x(j, carry):
        zz, yy, xx, cc = j // 8, (j // 4) % 2, (j // 2) % 2, j % 2
        b_at = yy * (1 - cc) + xx * cc
        a_at = xx * (1 - cc) + yy * cc
        xt[zz, cc, b_at, a_at] = xv[:, pl.ds(pl.multiple_of(j * rows, rows), rows)].T
        return carry

    halo = remote(kv.at[1], kv.at[0], hsend.at[0], hrecv.at[0], ((s + 1) % 8, d))

    def send_halo():
        kv[1] = acc[1].astype(BF)

        @pl.when(s < 7)
        def _():
            halo.start()

        @pl.when(s == 0)
        def _():
            kv[0] = jnp.zeros_like(kv[0])

    def value_grads():
        @pl.when(s > 0)
        def _():
            halo.wait_recv()

        for j in range(2):
            pgs[j] = dot_nt(dos[...], kv[j, :, hd:])

    for stage, *at in ORDER:
        if stage == "z":
            stage_z(*at)
        elif stage == "a":
            stage_a(*at)
        elif stage == "b":
            stage_b(*at)
        elif stage == "d":
            stage_d(*at)
        elif stage == "turn":
            lax.fori_loop(at[0] * 8, at[0] * 8 + 8, transpose_x, 0)
        elif stage == "halo":
            send_halo()
        elif stage == "values":
            value_grads()
        else:
            for load in loads[2:]:
                load.wait()
            doc = jnp.broadcast_to(docv[...], (tok, tok)).T
            row = lax.broadcasted_iota(jnp.int32, (tok, tok), 0)
            col = lax.broadcasted_iota(jnp.int32, (tok, tok), 1)
            vis_own = jnp.where((col <= row) & (col + s * tok >= doc), 0.0, -jnp.inf)
            vis_pri = jnp.where((col > row) & (col + (s - 1) * tok >= doc), 0.0, -jnp.inf)

    for h in range(2):
        qs[h * tok : (h + 1) * tok, :] = acc[0, :, h * hd : (h + 1) * hd].astype(BF)
    k_own = kv[1, :, :hd]
    k_pri = kv[0, :, :hd]
    for h in range(2):
        span = slice(h * tok, (h + 1) * tok)
        s_own = dot_nt(qs[span, :], k_own) * inv_root + vis_own
        s_pri = dot_nt(qs[span, :], k_pri) * inv_root + vis_pri
        pg_own = pgs[1, span, :]
        pg_pri = pgs[0, span, :]
        top = jnp.max(jnp.maximum(s_own, s_pri), axis=1, keepdims=True)
        e_own = jnp.exp(s_own - top)
        e_pri = jnp.exp(s_pri - top)
        scale = 1.0 / jnp.sum(e_own + e_pri, axis=1, keepdims=True)
        p_own = e_own * scale
        p_pri = e_pri * scale
        l_own = p_own.astype(BF)
        l_pri = p_pri.astype(BF)
        row_dot = jnp.sum(
            l_own.astype(F32) * pg_own + l_pri.astype(F32) * pg_pri, axis=1, keepdims=True
        )
        pst[0, span, :] = l_pri
        pst[1, span, :] = l_own
        dst_[0, span, :] = (p_pri * (pg_pri - row_dot)).astype(BF)
        dst_[1, span, :] = (p_own * (pg_own - row_dot)).astype(BF)

    dkv[0, :, :hd] = (dot_tn(dst_[0], qs[...]) * inv_root).astype(BF)
    dkv[0, :, hd:] = dot_tn(pst[0], dos[...]).astype(BF)
    back = remote(dkv.at[0], dkv.at[1], hsend.at[1], hrecv.at[1], ((s + 7) % 8, d))

    @pl.when(s > 0)
    def _():
        back.start()

    @pl.when(s == 7)
    def _():
        dkv[1] = jnp.zeros_like(dkv[1])

    for h in range(2):
        span = slice(h * tok, (h + 1) * tok)
        gp[0, :, h * hd : (h + 1) * hd] = (
            (dot_nn(dst_[1, span, :], k_own) + dot_nn(dst_[0, span, :], k_pri)) * inv_root
        ).astype(BF)

    rsent = {}

    def rpush(src, dst, h, k, stage, dev):
        index = (h * NZ + k) * 4 + stage
        copy = remote(src, dst, gsend.at[index], grecv.at[index], dev)
        copy.start()
        rsent[h, k, stage] = copy

    def weight_part(h, k, plane):
        lhs = xt[(z + k) % NZ, plane].reshape(4 * rows, tok)
        gb[h, k, plane] = dot_nn(lhs, gp[h]).astype(BF).reshape(2, 2, rows, half)

    def produce(h, k):
        weight_part(h, k, 1 - c)
        rpush(gb.at[h, k, 1 - c], rd.at[h, k], h, k, 0, sib)
        weight_part(h, k, c)

    def chip_sum(h, k, b_at, a_at):
        return gb[h, k, c, b_at, a_at].astype(F32) + rd[h, k, b_at, a_at].astype(F32)

    def send_b(h, k):
        rsent[h, k, 0].wait_recv()
        for a_at in range(2):
            sb[h, k, a_at] = chip_sum(h, k, 1 - my_b, a_at).astype(BF)
        rpush(sb.at[h, k], rb.at[h, k], h, k, 1, part_b)

    def send_a(h, k):
        rsent[h, k, 1].wait_recv()
        sa[h, k] = (
            chip_sum(h, k, my_b, 1 - my_a) + rb[h, k, 1 - my_a].astype(F32)
        ).astype(BF)
        rpush(sa.at[h, k], ra.at[h, k], h, k, 2, part_a)

    def send_z(h, k):
        rsent[h, k, 2].wait_recv()
        total = (
            chip_sum(h, k, my_b, my_a)
            + rb[h, k, my_a].astype(F32)
            + ra[h, k].astype(F32)
        )
        if k:
            sz[h, k] = total.astype(BF)
            rpush(sz.at[h, k], rz.at[h, k], h, k, 3, zdev[k])
        else:
            kz[h] = total

    def finish(h):
        total = kz[h]
        for k in CHUNKS[:3]:
            rsent[h, k, 3].wait_recv()
            total += rz[h, k].astype(F32)
        g_ref[:, h * half : (h + 1) * half] = total

    def input_grad(j, carry):
        width = dxv.shape[1] // 8
        at = pl.multiple_of(j * width, width)
        ws = [wv[h, pl.ds(j * 4, 4)].reshape(width, half) for h in range(2)]
        dxv[:, pl.ds(at, width)] = (dot_nt(gp[0], ws[0]) + dot_nt(gp[1], ws[1])).astype(BF)
        return carry

    c0, c1, c2, c3 = CHUNKS
    produce(0, c0)
    produce(0, c1)
    produce(0, c2)
    send_b(0, c0)
    produce(0, c3)
    send_b(0, c1)
    send_b(0, c2)
    own_dk = dot_tn(dst_[1], qs[...]) * inv_root
    own_dv = dot_tn(pst[1], dos[...])
    send_b(0, c3)

    @pl.when(s < 7)
    def _():
        back.wait_recv()

    gp[1, :, :hd] = (own_dk + dkv[1, :, :hd].astype(F32)).astype(BF)
    gp[1, :, hd:] = (own_dv + dkv[1, :, hd:].astype(F32)).astype(BF)
    def grads(lo, hi):
        lax.fori_loop(lo, hi, input_grad, 0)

    produce(1, c0)
    send_a(0, c0)
    produce(1, c1)
    send_b(1, c0)
    send_a(0, c1)
    produce(1, c2)
    send_b(1, c1)
    send_z(0, c0)
    send_a(0, c2)
    produce(1, c3)
    send_b(1, c2)
    send_z(0, c1)
    send_a(0, c3)
    send_b(1, c3)
    grads(0, 3)
    send_z(0, c2)
    send_a(1, c0)
    grads(3, 6)
    send_z(0, c3)
    send_a(1, c1)
    send_z(1, c0)
    grads(6, 8)
    store_dx = pltpu.make_async_copy(dxv, dx_hbm.at[0], osem)
    store_dx.start()
    send_a(1, c2)
    send_z(1, c1)
    send_a(1, c3)
    send_z(1, c2)
    send_z(1, c3)
    finish(0)
    finish(1)

    store_dx.wait()
    for copy in sent + list(rsent.values()):
        copy.wait_send()
    for copy, test in line:
        pl.when(test)(copy.wait_send)

    @pl.when(s < 7)
    def _():
        halo.wait_send()

    @pl.when(s > 0)
    def _():
        back.wait_send()


def kernel_body(layer_inputs, doc_start, w_qkv, d_context):
    tok, width = layer_inputs.shape[1:]
    rows, cols = w_qkv.shape
    hd = cols // 4
    half = 2 * hd
    blocks = width // rows
    dma = pltpu.SemaphoreType.DMA
    block = (rows, half)
    return pl.pallas_call(
        fused,
        out_shape=(
            jax.ShapeDtypeStruct(layer_inputs.shape, BF),
            jax.ShapeDtypeStruct((rows, cols), F32),
        ),
        in_specs=[pl.BlockSpec(memory_space=pl.ANY)] * 4,
        out_specs=(
            pl.BlockSpec(memory_space=pl.ANY),
            pl.BlockSpec(memory_space=pltpu.VMEM),
        ),
        scratch_shapes=[
            pltpu.VMEM((tok, width), BF),
            pltpu.VMEM((1, tok), jnp.int32),
            pltpu.VMEM((NZ, 2, 2, 2, rows, tok), BF),
            pltpu.VMEM((2, blocks) + block, BF),
            pltpu.VMEM((2, tok, half), F32),
            pltpu.VMEM((2 * tok, hd), BF),
            pltpu.VMEM((2 * tok, hd), BF),
            pltpu.VMEM((2, 2 * tok, tok), F32),
            pltpu.VMEM((2, tok, half), BF),
            pltpu.VMEM((2, tok, half), BF),
            pltpu.VMEM((2, 2 * tok, tok), BF),
            pltpu.VMEM((2, 2 * tok, tok), BF),
            pltpu.VMEM((2, tok, half), BF),
            pltpu.VMEM((tok, width), BF),
            pltpu.VMEM((2, NZ, 2, 2, 2) + block, BF),
            pltpu.VMEM((2, NZ, 2, 2) + block, BF),
            pltpu.VMEM((2, NZ, 2) + block, BF),
            pltpu.VMEM((2, NZ, 2) + block, BF),
            pltpu.VMEM((2, NZ) + block, BF),
            pltpu.VMEM((2, NZ) + block, BF),
            pltpu.VMEM((2, NZ) + block, BF),
            pltpu.VMEM((2, NZ) + block, BF),
            pltpu.VMEM((2,) + block, F32),
            dma((6,)),
            dma((2, 36)),
            dma((2, 32)),
            dma((2,)),
            dma((2,)),
            dma((32,)),
            dma((32,)),
            dma,
        ],
        compiler_params=pltpu.CompilerParams(
            collective_id=0, has_side_effects=True, vmem_limit_bytes=60 * 1024 * 1024
        ),
    )(layer_inputs, doc_start, w_qkv, d_context)


def solution(mesh):
    fits = mesh.shape["seq"] == 8 and mesh.shape["dp"] == 4
    return jax.shard_map(
        kernel_body if fits else body,
        mesh=mesh,
        in_specs=(
            P("dp", "seq", None),
            P("dp", "seq"),
            P(("seq", "dp"), None),
            P("dp", "seq", None),
        ),
        out_specs=(P("dp", "seq", None), P(("seq", "dp"), None)),
        check_vma=False,
    )
```

```python
import jax
import jax.numpy as jnp
from jax import lax
from jax.experimental import pallas as pl
from jax.experimental.pallas import tpu as pltpu
from jax.sharding import PartitionSpec as P

WIN = 256


def from_partner(block, axis, stride):
    count = lax.axis_size(axis)
    route = []
    for low in range(count):
        high = low | 1 << stride
        if high != low and high < count:
            route += [(low, high), (high, low)]
    return lax.ppermute(block, axis, route)


def from_behind(block, axis, distance):
    devices = range(lax.axis_size(axis))
    route = [(i - distance, i) for i in devices if i - distance in devices]
    return lax.ppermute(block, axis, route)


def masked_scores(queries, key_rows, doc_first, query_pos, key_pos):
    inv_root = queries.shape[2] ** (-0.5)
    scores = (
        jnp.einsum("rhd,kd->hrk", queries, key_rows, preferred_element_type=jnp.float32) * inv_root
    )
    visible = (
        (key_pos[None, :] <= query_pos[:, None])
        & (key_pos[None, :] > query_pos[:, None] - WIN)
        & (key_pos[None, :] >= doc_first[:, None])
    )
    return jnp.where(visible[None, :, :], scores, -jnp.inf)


def backward_terms(queries, key_rows, value_rows, out_grad, attn_probs, prob_low, row_dot):
    inv_root = queries.shape[2] ** (-0.5)
    prob_grad = jnp.einsum("rhd,kd->hrk", out_grad, value_rows, preferred_element_type=jnp.float32)
    score_grad = (attn_probs * (prob_grad - row_dot[:, :, None])).astype(jnp.bfloat16)
    grad_query = (
        jnp.einsum("hrk,kd->rhd", score_grad, key_rows, preferred_element_type=jnp.float32)
        * inv_root
    )
    grad_keys = (
        jnp.einsum("hrk,rhd->kd", score_grad, queries, preferred_element_type=jnp.float32)
        * inv_root
    )
    grad_values = jnp.einsum("hrk,rhd->kd", prob_low, out_grad, preferred_element_type=jnp.float32)
    return (grad_query, grad_keys, grad_values)


def local_pass(queries, key_rows, value_rows, out_grad, doc_first, query_pos, key_pos):
    scores = masked_scores(queries, key_rows, doc_first, query_pos, key_pos)
    row_max = jnp.max(scores, axis=2)
    log_total = row_max + jnp.log(jnp.sum(jnp.exp(scores - row_max[:, :, None]), axis=2))
    attn_probs = jnp.exp(scores - log_total[:, :, None])
    prob_low = attn_probs.astype(jnp.bfloat16)
    context = jnp.einsum("hrk,kd->rhd", prob_low, value_rows, preferred_element_type=jnp.float32)
    row_dot = jnp.sum(out_grad.astype(jnp.float32) * context, axis=2).T
    grad_query, grad_keys, grad_values = backward_terms(
        queries, key_rows, value_rows, out_grad, attn_probs, prob_low, row_dot
    )
    return (grad_query, grad_keys, grad_values, log_total, row_dot)


def halve_over_seq(buffer, bit_index):
    half_rows = buffer.shape[0] // 2
    my_bit = lax.axis_index("seq") >> bit_index & 1
    kept_half = lax.dynamic_slice_in_dim(buffer, my_bit * half_rows, half_rows, 0)
    sent_half = lax.dynamic_slice_in_dim(buffer, (1 - my_bit) * half_rows, half_rows, 0)
    return kept_half + from_partner(sent_half.astype(jnp.bfloat16), "seq", bit_index).astype(
        sent_half.dtype
    )


def halve_over_dp(buffer, bit_index):
    half_rows = buffer.shape[0] // 2
    my_bit = lax.axis_index("dp") >> bit_index & 1
    kept_half = lax.dynamic_slice_in_dim(buffer, my_bit * half_rows, half_rows, 0)
    sent_half = lax.dynamic_slice_in_dim(buffer, (1 - my_bit) * half_rows, half_rows, 0)
    return kept_half + from_partner(sent_half.astype(jnp.bfloat16), "dp", bit_index).astype(
        sent_half.dtype
    )


def body(layer_inputs, doc_start, w_qkv, d_context):
    x_local = layer_inputs[0]
    tok_rows = x_local.shape[0]
    q_width = d_context.shape[2]
    head_dim = (w_qkv.shape[1] - q_width) // 2
    heads = q_width // head_dim
    out_grad = d_context[0].reshape(tok_rows, heads, head_dim)
    doc_first = doc_start[0]
    positions = lax.axis_index("seq") * tok_rows + jnp.arange(tok_rows, dtype=jnp.int32)
    full_weights = lax.all_gather(w_qkv, ("seq", "dp"), axis=0, tiled=True)
    projected = jnp.dot(x_local, full_weights, preferred_element_type=jnp.float32)
    projected = projected.astype(jnp.bfloat16)
    queries = projected[:, :q_width].reshape(tok_rows, heads, head_dim)
    key_value = projected[:, q_width:]
    prior = from_behind(key_value, "seq", 1)
    key_rows = jnp.concatenate([prior[:, :head_dim], key_value[:, :head_dim]], axis=0)
    value_rows = jnp.concatenate([prior[:, head_dim:], key_value[:, head_dim:]], axis=0)
    key_pos = jnp.concatenate([positions - tok_rows, positions])
    grad_query, grad_keys, grad_values, log_total, row_dot = local_pass(
        queries, key_rows, value_rows, out_grad, doc_first, positions, key_pos
    )
    returned = from_behind(
        jnp.concatenate([grad_keys[:tok_rows], grad_values[:tok_rows]], axis=1).astype(
            jnp.bfloat16
        ),
        "seq",
        -1,
    ).astype(jnp.float32)
    far_keys = returned[:, :head_dim]
    far_values = returned[:, head_dim:]
    key_grad = (grad_keys[tok_rows:] + far_keys).astype(jnp.bfloat16)
    value_grad = (grad_values[tok_rows:] + far_values).astype(jnp.bfloat16)
    grad_proj = jnp.concatenate(
        [grad_query.astype(jnp.bfloat16).reshape(tok_rows, q_width), key_grad, value_grad], axis=1
    )
    input_grad = lax.dot_general(
        grad_proj, full_weights, (((1,), (1,)), ((), ())), preferred_element_type=jnp.float32
    )
    input_grad = input_grad.astype(jnp.bfloat16).reshape(1, tok_rows, x_local.shape[1])
    partial_grad = lax.dot_general(
        x_local, grad_proj, (((0,), (0,)), ((), ())), preferred_element_type=jnp.float32
    )
    seq_count = lax.axis_size("seq")
    dp_count = lax.axis_size("dp")
    seq_levels = seq_count.bit_length() - 1
    dp_levels = dp_count.bit_length() - 1
    buffer = partial_grad
    for bit_index in range(seq_levels - 1, -1, -1):
        buffer = halve_over_seq(buffer, bit_index)
    for bit_index in range(dp_levels - 1, -1, -1):
        buffer = halve_over_dp(buffer, bit_index)
    return (input_grad, buffer)


BF = jnp.bfloat16
F32 = jnp.float32
NZ = 4
ORDER = (
    ("z", 1, 0), ("swap",), ("z", 1, 1), ("a", 1, 0), ("b", 1, 0, 0), ("z", 1, 2), ("a", 1, 1),
    ("b", 1, 1, 0), ("b", 1, 0, 1), ("z", 1, 3), ("prep",), ("b", 1, 2, 0), ("a", 1, 2),
    ("b", 1, 1, 1), ("b", 1, 3, 0), ("a", 1, 3), ("z", 0, 0), ("take",), ("d", 1, 0),
    ("b", 1, 2, 1), ("d", 1, 1), ("z", 0, 1), ("b", 1, 3, 1), ("d", 1, 2), ("z", 0, 2),
    ("d", 1, 3), ("partial", 1), ("a", 0, 0), ("b", 0, 0, 0), ("halo",), ("z", 0, 3),
    ("b", 0, 1, 0), ("b", 0, 2, 0), ("a", 0, 1), ("a", 0, 2), ("b", 0, 0, 1), ("d", 0, 0),
    ("b", 0, 2, 1), ("a", 0, 3), ("b", 0, 3, 0), ("b", 0, 1, 1), ("d", 0, 1), ("d", 0, 2),
    ("values",), ("b", 0, 3, 1), ("d", 0, 3), ("partial", 0),
)
CHUNKS = (2, 1, 3, 0)


def dot_nn(a, b):
    return jnp.dot(a, b, preferred_element_type=F32)


def dot_nt(a, b):
    return lax.dot_general(a, b, (((1,), (1,)), ((), ())), preferred_element_type=F32)


def dot_tn(a, b):
    return lax.dot_general(a, b, (((0,), (0,)), ((), ())), preferred_element_type=F32)


def flip(v, f):
    return v + f * (1 - 2 * v)


def remote(src, dst, send, recv, device):
    return pltpu.make_async_remote_copy(
        src_ref=src,
        dst_ref=dst,
        send_sem=send,
        recv_sem=recv,
        device_id=device,
        device_id_type=pl.DeviceIdType.MESH,
    )


def fused(
    x_hbm, doc_hbm, w_hbm, do_hbm, dx_hbm, g_ref,
    xo, xs, docv, wv, acc, pacc, qs, qt, dos, dot_, pgs, kv, dkv, pst, dst_, gp, gpt, dxo, dxr,
    gb, rb, sa, ra, sz, rz, kz,
    lsem, xsem, wsend, wrecv, hsend, hrecv, ssend, srecv, gsend, grecv, osem,
):
    s = lax.axis_index("seq")
    d = lax.axis_index("dp")
    z, y = s // 2, s % 2
    x, c = d // 2, d % 2
    tok = xs.shape[1]
    rows = wv.shape[4]
    hd = qs.shape[1]
    half = 2 * hd
    span = 4 * rows
    inv_root = hd ** (-0.5)
    my_a = x * (1 - c) + y * c
    my_b = y * (1 - c) + x * c

    def device(zz, yy, xx, cc):
        return (zz * 2 + yy, xx * 2 + cc)

    sib = device(z, y, x, 1 - c)
    part_a = device(z, flip(y, c), flip(x, 1 - c), c)
    part_b = device(z, flip(y, 1 - c), flip(x, c), c)
    zdev = [device((z + k) % NZ, y, x, c) for k in range(NZ)]
    z_order = [
        z,
        jnp.where(z == 0, 1, jnp.where(z == 1, 0, jnp.where(z == 2, 3, 2))),
        jnp.where(z == 0, 2, jnp.where(z == 1, 2, 1)),
        jnp.where(z <= 1, 3, 0),
    ]

    def columns(plane, zz, q):
        b, a = q // 2, q % 2
        yy = b * (1 - plane) + a * plane
        xx = a * (1 - plane) + b * plane
        block = ((zz * 2 + yy) * 2 + xx) * 2 + plane
        return pl.ds(pl.multiple_of(block * rows, rows), rows)

    def load_swap(j):
        zz, q = j // 4, j % 4
        return pltpu.make_async_copy(
            x_hbm.at[0, :, columns(1 - c, zz, q)],
            xs.at[zz, :, pl.ds(pl.multiple_of(q * rows, rows), rows)],
            xsem.at[j],
        )

    def load_own(j):
        zz, q = j // 4, j % 4
        return pltpu.make_async_copy(
            x_hbm.at[0, :, columns(c, zz, q)],
            xo.at[zz, pl.ds(0, tok), pl.ds(pl.multiple_of(q * rows, rows), rows)],
            xsem.at[16 + j],
        )

    def each(count, action):
        def one(j, carry):
            action(j)
            return carry

        lax.fori_loop(0, count, one, 0)

    loads = [
        pltpu.make_async_copy(
            w_hbm.at[:, pl.ds(h * half, half)], wv.at[h, z, my_b, my_a], lsem.at[h]
        )
        for h in (1, 0)
    ]
    late = [pltpu.make_async_copy(doc_hbm, docv, lsem.at[2])] + [
        pltpu.make_async_copy(
            do_hbm.at[0, :, pl.ds(h * hd, hd)], dos.at[pl.ds(h * tok, tok)], lsem.at[3 + h]
        )
        for h in range(2)
    ]
    for load in loads:
        load.start()
    each(16, lambda j: load_swap(j).start())
    each(16, lambda j: load_own(j).start())
    for load in late:
        load.start()

    barrier = pltpu.get_barrier_semaphore()
    for dev in [sib, part_a, part_b] + zdev[1:]:
        pl.semaphore_signal(barrier, inc=1, device_id=dev, device_id_type=pl.DeviceIdType.MESH)
    extra_up = (y == 1) & (z < NZ - 1)
    extra_down = (y == 0) & (z > 0)

    @pl.when(extra_up)
    def _():
        pl.semaphore_signal(
            barrier, inc=1, device_id=(s + 1, d), device_id_type=pl.DeviceIdType.MESH
        )

    @pl.when(extra_down)
    def _():
        pl.semaphore_signal(
            barrier, inc=1, device_id=(s - 1, d), device_id_type=pl.DeviceIdType.MESH
        )

    loads[0].wait()
    loads[1].wait()

    @pl.when(extra_up | extra_down)
    def _():
        pl.semaphore_wait(barrier, 7)

    @pl.when(jnp.logical_not(extra_up | extra_down))
    def _():
        pl.semaphore_wait(barrier, 6)

    sent = []
    line = []
    swaps = {}

    def swap(src, dst, index):
        copy = remote(src, dst, ssend.at[index], srecv.at[index], sib)
        copy.start()
        sent.append(copy)
        swaps[index] = copy

    def block_at(h, k, b_flip, a_flip):
        return wv.at[h, z_order[k], flip(my_b, b_flip), flip(my_a, a_flip)]

    def push(h, ref, dev, index):
        copy = remote(ref, ref, wsend.at[h, index], wrecv.at[h, index], dev)
        copy.start()
        sent.append(copy)

    def arrived(h, ref, index):
        remote(ref, ref, wsend.at[h, 0], wrecv.at[h, index], sib).wait_recv()

    def stage_z(h, k):
        ref = block_at(h, k, 0, 0)
        zz = z_order[k]
        if k:
            arrived(h, ref, zz)
        up = remote(ref, ref, wsend.at[h, zz], wrecv.at[h, zz], zdev[1])
        down = remote(ref, ref, wsend.at[h, 16 + zz], wrecv.at[h, zz], zdev[3])
        for copy, test in ((up, (zz <= z) & (z < NZ - 1)), (down, (zz >= z) & (z > 0))):
            line.append((copy, test))
            pl.when(test)(copy.start)
        push(h, ref, part_a, 4 + k)
        push(h, ref, part_b, 8 + 2 * k)

    def stage_a(h, k):
        ref = block_at(h, k, 0, 1)
        arrived(h, ref, 4 + k)
        push(h, ref, part_b, 9 + 2 * k)

    def stage_b(h, k, a):
        arrived(h, block_at(h, k, 1, a), 8 + 2 * k + a)

    def stage_d(h, k):
        zz = z_order[k]
        part = dot_nn(xo[zz], wv[h, zz].reshape(span, half))
        if k == 0:
            acc[h] = part
        else:
            acc[h] += part

    def projected(h):
        swaps[4 + h].wait_recv()
        return (acc[h, :tok] + pacc[h]).astype(BF)

    halo = remote(kv.at[1], kv.at[0], hsend.at[0], hrecv.at[0], ((s + 1) % 8, d))

    def send_halo():
        kv[1] = projected(1)

        @pl.when(s < 7)
        def _():
            halo.start()

        @pl.when(s == 0)
        def _():
            kv[0] = jnp.zeros_like(kv[0])

    def value_grads():
        @pl.when(s > 0)
        def _():
            halo.wait_recv()

        for j in range(2):
            pgs[j] = dot_nt(dos[...], kv[j, :, hd:])

    for stage, *at in ORDER:
        if stage == "z":
            stage_z(*at)
        elif stage == "a":
            stage_a(*at)
        elif stage == "b":
            stage_b(*at)
        elif stage == "d":
            stage_d(*at)
        elif stage == "swap":
            each(16, lambda j: load_swap(j).wait())
            for j in range(NZ):
                swap(xs.at[j], xo.at[j, pl.ds(tok, tok)], j)
        elif stage == "take":
            each(16, lambda j: load_own(j).wait())
            for j in range(NZ):
                swaps[j].wait_recv()
        elif stage == "partial":
            swap(acc.at[at[0], pl.ds(tok, tok)], pacc.at[at[0]], 4 + at[0])
        elif stage == "halo":
            send_halo()
        elif stage == "values":
            value_grads()
        else:
            for load in late:
                load.wait()
            doc = jnp.broadcast_to(docv[...], (tok, tok)).T
            row = lax.broadcasted_iota(jnp.int32, (tok, tok), 0)
            col = lax.broadcasted_iota(jnp.int32, (tok, tok), 1)
            vis_own = jnp.where((col <= row) & (col + s * tok >= doc), 0.0, -jnp.inf)
            vis_pri = jnp.where((col > row) & (col + (s - 1) * tok >= doc), 0.0, -jnp.inf)
            dot_[...] = dos[...].T

    q_own = projected(0)
    for h in range(2):
        qs[h * tok : (h + 1) * tok, :] = q_own[:, h * hd : (h + 1) * hd]
    qt[...] = qs[...].T
    k_own = kv[1, :, :hd]
    k_pri = kv[0, :, :hd]
    for h in range(2):
        at = slice(h * tok, (h + 1) * tok)
        s_own = dot_nt(qs[at, :], k_own) * inv_root + vis_own
        s_pri = dot_nt(qs[at, :], k_pri) * inv_root + vis_pri
        pg_own = pgs[1, at, :]
        pg_pri = pgs[0, at, :]
        top = jnp.max(jnp.maximum(s_own, s_pri), axis=1, keepdims=True)
        e_own = jnp.exp(s_own - top)
        e_pri = jnp.exp(s_pri - top)
        scale = 1.0 / jnp.sum(e_own + e_pri, axis=1, keepdims=True)
        p_own = e_own * scale
        p_pri = e_pri * scale
        l_own = p_own.astype(BF)
        l_pri = p_pri.astype(BF)
        row_dot = jnp.sum(
            l_own.astype(F32) * pg_own + l_pri.astype(F32) * pg_pri, axis=1, keepdims=True
        )
        pst[0, at, :] = l_pri
        pst[1, at, :] = l_own
        dst_[0, at, :] = (p_pri * (pg_pri - row_dot)).astype(BF)
        dst_[1, at, :] = (p_own * (pg_own - row_dot)).astype(BF)

    dkv[0, :hd, :] = (dot_nn(qt[...], dst_[0]) * inv_root).astype(BF)
    dkv[0, hd:, :] = dot_nn(dot_[...], pst[0]).astype(BF)
    back = remote(dkv.at[0], dkv.at[1], hsend.at[1], hrecv.at[1], ((s + 7) % 8, d))

    @pl.when(s > 0)
    def _():
        back.start()

    @pl.when(s == 7)
    def _():
        dkv[1] = jnp.zeros_like(dkv[1])

    for h in range(2):
        at = slice(h * tok, (h + 1) * tok)
        gp[0, :tok, h * hd : (h + 1) * hd] = (
            (dot_nn(dst_[1, at, :], k_own) + dot_nn(dst_[0, at, :], k_pri)) * inv_root
        ).astype(BF)

    rsent = {}

    def swap_grads(h):
        swap(gp.at[h, pl.ds(0, tok)], gp.at[h, pl.ds(tok, tok)], 6 + h)

    def take_grads(h):
        swaps[6 + h].wait_recv()
        gpt[h, :, tok:] = gp[h, tok:, :].T

    def rpush(src, dst, h, k, stage, dev):
        index = (h * NZ + k) * 3 + stage
        copy = remote(src, dst, gsend.at[index], grecv.at[index], dev)
        copy.start()
        rsent[h, k, stage] = copy

    def produce(h, k):
        part = dot_nn(gpt[h], xo[(z + k) % NZ]).astype(BF)
        for q in range(4):
            gb[h, k, q // 2, q % 2] = part[:, q * rows : (q + 1) * rows]
        rpush(gb.at[h, k, 1 - my_b], rb.at[h, k], h, k, 0, part_b)

    def sum_b(h, k, a_at):
        return gb[h, k, my_b, a_at].astype(F32) + rb[h, k, a_at].astype(F32)

    def send_a(h, k):
        rsent[h, k, 0].wait_recv()
        sa[h, k] = sum_b(h, k, 1 - my_a).astype(BF)
        rpush(sa.at[h, k], ra.at[h, k], h, k, 1, part_a)

    def send_z(h, k):
        rsent[h, k, 1].wait_recv()
        total = sum_b(h, k, my_a) + ra[h, k].astype(F32)
        if k:
            sz[h, k] = total.astype(BF)
            rpush(sz.at[h, k], rz.at[h, k], h, k, 2, zdev[k])
        else:
            kz[h] = total

    def finish(h):
        total = kz[h]
        for k in CHUNKS[:3]:
            rsent[h, k, 2].wait_recv()
            total += rz[h, k].astype(F32)
        g_ref[:, h * half : (h + 1) * half] = total.T

    def store(src, plane, zz, q, index):
        return pltpu.make_async_copy(
            src.at[zz, pl.ds(0, tok), pl.ds(q * rows, rows)],
            dx_hbm.at[0, :, columns(plane, zz, q)],
            osem.at[index],
        )

    stores = []

    def input_grad(zz):
        part = dot_nt(gp[0], wv[0, zz].reshape(span, half))
        part += dot_nt(gp[1], wv[1, zz].reshape(span, half))
        dxo[zz] = part.astype(BF)
        swap(dxo.at[zz, pl.ds(tok, tok)], dxr.at[zz], 8 + zz)
        for q in range(4):
            stores.append(store(dxo, c, zz, q, zz * 4 + q))
            stores[-1].start()

    def take_input_grad(zz):
        swaps[8 + zz].wait_recv()
        for q in range(4):
            stores.append(store(dxr, 1 - c, zz, q, 16 + zz * 4 + q))
            stores[-1].start()

    c0, c1, c2, c3 = CHUNKS
    swap_grads(0)
    gpt[0, :, :tok] = gp[0, :tok, :].T
    own_dk = dot_nn(qt[...], dst_[1]) * inv_root
    own_dv = dot_nn(dot_[...], pst[1])
    take_grads(0)
    for k in CHUNKS:
        produce(0, k)

    @pl.when(s < 7)
    def _():
        back.wait_recv()

    gpt[1, :hd, :tok] = (own_dk + dkv[1, :hd, :].astype(F32)).astype(BF)
    gpt[1, hd:, :tok] = (own_dv + dkv[1, hd:, :].astype(F32)).astype(BF)
    gp[1, :tok, :] = gpt[1, :, :tok].T
    swap_grads(1)
    send_a(0, c0)
    take_grads(1)
    produce(1, c0)
    send_a(0, c1)
    produce(1, c1)
    send_z(0, c0)
    send_a(0, c2)
    produce(1, c2)
    send_z(0, c1)
    send_a(0, c3)
    produce(1, c3)
    input_grad(0)
    send_z(0, c2)
    input_grad(1)
    send_a(1, c0)
    send_z(0, c3)
    input_grad(2)
    send_a(1, c1)
    send_z(1, c0)
    input_grad(3)
    for zz in range(NZ):
        take_input_grad(zz)
    send_a(1, c2)
    send_z(1, c1)
    finish(0)
    send_a(1, c3)
    send_z(1, c2)
    send_z(1, c3)
    finish(1)

    for copy in stores:
        copy.wait()
    for copy in sent + list(rsent.values()):
        copy.wait_send()
    for copy, test in line:
        pl.when(test)(copy.wait_send)

    @pl.when(s < 7)
    def _():
        halo.wait_send()

    @pl.when(s > 0)
    def _():
        back.wait_send()


def kernel_body(layer_inputs, doc_start, w_qkv, d_context):
    tok, width = layer_inputs.shape[1:]
    rows, cols = w_qkv.shape
    hd = cols // 4
    half = 2 * hd
    dma = pltpu.SemaphoreType.DMA
    block = (half, rows)
    return pl.pallas_call(
        fused,
        out_shape=(
            jax.ShapeDtypeStruct(layer_inputs.shape, BF),
            jax.ShapeDtypeStruct((rows, cols), F32),
        ),
        in_specs=[pl.BlockSpec(memory_space=pl.ANY)] * 4,
        out_specs=(
            pl.BlockSpec(memory_space=pl.ANY),
            pl.BlockSpec(memory_space=pltpu.VMEM),
        ),
        scratch_shapes=[
            pltpu.VMEM((NZ, 2 * tok, 4 * rows), BF),
            pltpu.VMEM((NZ, tok, 4 * rows), BF),
            pltpu.VMEM((1, tok), jnp.int32),
            pltpu.VMEM((2, NZ, 2, 2, rows, half), BF),
            pltpu.VMEM((2, 2 * tok, half), F32),
            pltpu.VMEM((2, tok, half), F32),
            pltpu.VMEM((2 * tok, hd), BF),
            pltpu.VMEM((hd, 2 * tok), BF),
            pltpu.VMEM((2 * tok, hd), BF),
            pltpu.VMEM((hd, 2 * tok), BF),
            pltpu.VMEM((2, 2 * tok, tok), F32),
            pltpu.VMEM((2, tok, half), BF),
            pltpu.VMEM((2, half, tok), BF),
            pltpu.VMEM((2, 2 * tok, tok), BF),
            pltpu.VMEM((2, 2 * tok, tok), BF),
            pltpu.VMEM((2, 2 * tok, half), BF),
            pltpu.VMEM((2, half, 2 * tok), BF),
            pltpu.VMEM((NZ, 2 * tok, 4 * rows), BF),
            pltpu.VMEM((NZ, tok, 4 * rows), BF),
            pltpu.VMEM((2, NZ, 2, 2) + block, BF),
            pltpu.VMEM((2, NZ, 2) + block, BF),
            pltpu.VMEM((2, NZ) + block, BF),
            pltpu.VMEM((2, NZ) + block, BF),
            pltpu.VMEM((2, NZ) + block, BF),
            pltpu.VMEM((2, NZ) + block, BF),
            pltpu.VMEM((2,) + block, F32),
            dma((5,)),
            dma((32,)),
            dma((2, 20)),
            dma((2, 16)),
            dma((2,)),
            dma((2,)),
            dma((12,)),
            dma((12,)),
            dma((24,)),
            dma((24,)),
            dma((32,)),
        ],
        compiler_params=pltpu.CompilerParams(
            collective_id=0, has_side_effects=True, vmem_limit_bytes=60 * 1024 * 1024
        ),
    )(layer_inputs, doc_start, w_qkv, d_context)


def solution(mesh):
    fits = mesh.shape["seq"] == 8 and mesh.shape["dp"] == 4
    return jax.shard_map(
        kernel_body if fits else body,
        mesh=mesh,
        in_specs=(
            P("dp", "seq", None),
            P("dp", "seq"),
            P(("seq", "dp"), None),
            P("dp", "seq", None),
        ),
        out_specs=(P("dp", "seq", None), P(("seq", "dp"), None)),
        check_vma=False,
    )
```

```python
import jax
import jax.numpy as jnp
from jax import lax
from jax.experimental import pallas as pl
from jax.experimental.pallas import tpu as pltpu
from jax.sharding import PartitionSpec as P

WIN = 256


def from_partner(block, axis, stride):
    count = lax.axis_size(axis)
    route = []
    for low in range(count):
        high = low | 1 << stride
        if high != low and high < count:
            route += [(low, high), (high, low)]
    return lax.ppermute(block, axis, route)


def from_behind(block, axis, distance):
    devices = range(lax.axis_size(axis))
    route = [(i - distance, i) for i in devices if i - distance in devices]
    return lax.ppermute(block, axis, route)


def masked_scores(queries, key_rows, doc_first, query_pos, key_pos):
    inv_root = queries.shape[2] ** (-0.5)
    scores = (
        jnp.einsum("rhd,kd->hrk", queries, key_rows, preferred_element_type=jnp.float32) * inv_root
    )
    visible = (
        (key_pos[None, :] <= query_pos[:, None])
        & (key_pos[None, :] > query_pos[:, None] - WIN)
        & (key_pos[None, :] >= doc_first[:, None])
    )
    return jnp.where(visible[None, :, :], scores, -jnp.inf)


def backward_terms(queries, key_rows, value_rows, out_grad, attn_probs, prob_low, row_dot):
    inv_root = queries.shape[2] ** (-0.5)
    prob_grad = jnp.einsum("rhd,kd->hrk", out_grad, value_rows, preferred_element_type=jnp.float32)
    score_grad = (attn_probs * (prob_grad - row_dot[:, :, None])).astype(jnp.bfloat16)
    grad_query = (
        jnp.einsum("hrk,kd->rhd", score_grad, key_rows, preferred_element_type=jnp.float32)
        * inv_root
    )
    grad_keys = (
        jnp.einsum("hrk,rhd->kd", score_grad, queries, preferred_element_type=jnp.float32)
        * inv_root
    )
    grad_values = jnp.einsum("hrk,rhd->kd", prob_low, out_grad, preferred_element_type=jnp.float32)
    return (grad_query, grad_keys, grad_values)


def local_pass(queries, key_rows, value_rows, out_grad, doc_first, query_pos, key_pos):
    scores = masked_scores(queries, key_rows, doc_first, query_pos, key_pos)
    row_max = jnp.max(scores, axis=2)
    log_total = row_max + jnp.log(jnp.sum(jnp.exp(scores - row_max[:, :, None]), axis=2))
    attn_probs = jnp.exp(scores - log_total[:, :, None])
    prob_low = attn_probs.astype(jnp.bfloat16)
    context = jnp.einsum("hrk,kd->rhd", prob_low, value_rows, preferred_element_type=jnp.float32)
    row_dot = jnp.sum(out_grad.astype(jnp.float32) * context, axis=2).T
    grad_query, grad_keys, grad_values = backward_terms(
        queries, key_rows, value_rows, out_grad, attn_probs, prob_low, row_dot
    )
    return (grad_query, grad_keys, grad_values, log_total, row_dot)


def halve_over_seq(buffer, bit_index):
    half_rows = buffer.shape[0] // 2
    my_bit = lax.axis_index("seq") >> bit_index & 1
    kept_half = lax.dynamic_slice_in_dim(buffer, my_bit * half_rows, half_rows, 0)
    sent_half = lax.dynamic_slice_in_dim(buffer, (1 - my_bit) * half_rows, half_rows, 0)
    return kept_half + from_partner(sent_half.astype(jnp.bfloat16), "seq", bit_index).astype(
        sent_half.dtype
    )


def halve_over_dp(buffer, bit_index):
    half_rows = buffer.shape[0] // 2
    my_bit = lax.axis_index("dp") >> bit_index & 1
    kept_half = lax.dynamic_slice_in_dim(buffer, my_bit * half_rows, half_rows, 0)
    sent_half = lax.dynamic_slice_in_dim(buffer, (1 - my_bit) * half_rows, half_rows, 0)
    return kept_half + from_partner(sent_half.astype(jnp.bfloat16), "dp", bit_index).astype(
        sent_half.dtype
    )


def body(layer_inputs, doc_start, w_qkv, d_context):
    x_local = layer_inputs[0]
    tok_rows = x_local.shape[0]
    q_width = d_context.shape[2]
    head_dim = (w_qkv.shape[1] - q_width) // 2
    heads = q_width // head_dim
    out_grad = d_context[0].reshape(tok_rows, heads, head_dim)
    doc_first = doc_start[0]
    positions = lax.axis_index("seq") * tok_rows + jnp.arange(tok_rows, dtype=jnp.int32)
    full_weights = lax.all_gather(w_qkv, ("seq", "dp"), axis=0, tiled=True)
    projected = jnp.dot(x_local, full_weights, preferred_element_type=jnp.float32)
    projected = projected.astype(jnp.bfloat16)
    queries = projected[:, :q_width].reshape(tok_rows, heads, head_dim)
    key_value = projected[:, q_width:]
    prior = from_behind(key_value, "seq", 1)
    key_rows = jnp.concatenate([prior[:, :head_dim], key_value[:, :head_dim]], axis=0)
    value_rows = jnp.concatenate([prior[:, head_dim:], key_value[:, head_dim:]], axis=0)
    key_pos = jnp.concatenate([positions - tok_rows, positions])
    grad_query, grad_keys, grad_values, log_total, row_dot = local_pass(
        queries, key_rows, value_rows, out_grad, doc_first, positions, key_pos
    )
    returned = from_behind(
        jnp.concatenate([grad_keys[:tok_rows], grad_values[:tok_rows]], axis=1).astype(
            jnp.bfloat16
        ),
        "seq",
        -1,
    ).astype(jnp.float32)
    far_keys = returned[:, :head_dim]
    far_values = returned[:, head_dim:]
    key_grad = (grad_keys[tok_rows:] + far_keys).astype(jnp.bfloat16)
    value_grad = (grad_values[tok_rows:] + far_values).astype(jnp.bfloat16)
    grad_proj = jnp.concatenate(
        [grad_query.astype(jnp.bfloat16).reshape(tok_rows, q_width), key_grad, value_grad], axis=1
    )
    input_grad = lax.dot_general(
        grad_proj, full_weights, (((1,), (1,)), ((), ())), preferred_element_type=jnp.float32
    )
    input_grad = input_grad.astype(jnp.bfloat16).reshape(1, tok_rows, x_local.shape[1])
    partial_grad = lax.dot_general(
        x_local, grad_proj, (((0,), (0,)), ((), ())), preferred_element_type=jnp.float32
    )
    seq_count = lax.axis_size("seq")
    dp_count = lax.axis_size("dp")
    seq_levels = seq_count.bit_length() - 1
    dp_levels = dp_count.bit_length() - 1
    buffer = partial_grad
    for bit_index in range(seq_levels - 1, -1, -1):
        buffer = halve_over_seq(buffer, bit_index)
    for bit_index in range(dp_levels - 1, -1, -1):
        buffer = halve_over_dp(buffer, bit_index)
    return (input_grad, buffer)


BF = jnp.bfloat16
F32 = jnp.float32
NZ = 4
ORDER = (
    ("z", 1, 0), ("swap",), ("z", 1, 1), ("a", 1, 0), ("b", 1, 0, 0), ("z", 1, 2), ("a", 1, 1),
    ("b", 1, 1, 0), ("b", 1, 0, 1), ("z", 1, 3), ("prep",), ("b", 1, 2, 0), ("a", 1, 2),
    ("b", 1, 1, 1), ("b", 1, 3, 0), ("a", 1, 3), ("z", 0, 0), ("take",),
    ("b", 1, 2, 1), ("z", 0, 1), ("b", 1, 3, 1), ("d", 1, 0, 4), ("partial", 1), ("z", 0, 2),
    ("a", 0, 0), ("b", 0, 0, 0), ("halo",), ("z", 0, 3),
    ("b", 0, 1, 0), ("b", 0, 2, 0), ("a", 0, 1), ("a", 0, 2), ("b", 0, 0, 1),
    ("b", 0, 2, 1), ("a", 0, 3), ("b", 0, 3, 0), ("values",), ("b", 0, 1, 1),
    ("d", 0, 0, 3), ("b", 0, 3, 1), ("d", 0, 3, 4), ("partial", 0),
)


def dot_nn(a, b):
    return jnp.dot(a, b, preferred_element_type=F32)


def dot_nt(a, b):
    return lax.dot_general(a, b, (((1,), (1,)), ((), ())), preferred_element_type=F32)


def dot_tn(a, b):
    return lax.dot_general(a, b, (((0,), (0,)), ((), ())), preferred_element_type=F32)


def flip(v, f):
    return v + f * (1 - 2 * v)


def remote(src, dst, send, recv, device):
    return pltpu.make_async_remote_copy(
        src_ref=src,
        dst_ref=dst,
        send_sem=send,
        recv_sem=recv,
        device_id=device,
        device_id_type=pl.DeviceIdType.MESH,
    )


def fused(
    x_hbm, doc_hbm, w_hbm, do_hbm, dx_hbm, g_ref,
    xo, xs, docv, vis, wv, acc, pacc, qs, qt, dos, dot_, pgs, kv, dkv, pst, dst_, gp, gpt, dxo, dxr,
    gb, rb, sa, ra, sz, rz,
    lsem, xsem, wsend, wrecv, hsend, hrecv, ssend, srecv, gsend, grecv, osem,
):
    s = lax.axis_index("seq")
    d = lax.axis_index("dp")
    z, y = s // 2, s % 2
    x, c = d // 2, d % 2
    tok = xs.shape[1]
    rows = wv.shape[4]
    hd = qs.shape[1]
    half = 2 * hd
    span = 4 * rows
    inv_root = hd ** (-0.5)
    my_a = x * (1 - c) + y * c
    my_b = y * (1 - c) + x * c

    def device(zz, yy, xx, cc):
        return (zz * 2 + yy, xx * 2 + cc)

    sib = device(z, y, x, 1 - c)
    part_a = device(z, flip(y, c), flip(x, 1 - c), c)
    part_b = device(z, flip(y, 1 - c), flip(x, c), c)
    zdev = [device((z + k) % NZ, y, x, c) for k in range(NZ)]
    z_order = [
        z,
        jnp.where(z == 0, 1, jnp.where(z == 1, 0, jnp.where(z == 2, 3, 2))),
        jnp.where(z == 0, 2, jnp.where(z == 1, 2, 1)),
        jnp.where(z <= 1, 3, 0),
    ]

    def columns(plane, zz, q):
        b, a = q // 2, q % 2
        yy = b * (1 - plane) + a * plane
        xx = a * (1 - plane) + b * plane
        block = ((zz * 2 + yy) * 2 + xx) * 2 + plane
        return pl.ds(pl.multiple_of(block * rows, rows), rows)

    def load_swap(j):
        zz, q = j // 4, j % 4
        return pltpu.make_async_copy(
            x_hbm.at[0, :, columns(1 - c, zz, q)],
            xs.at[zz, :, pl.ds(pl.multiple_of(q * rows, rows), rows)],
            xsem.at[j],
        )

    def load_own(j):
        zz, q = j // 4, j % 4
        return pltpu.make_async_copy(
            x_hbm.at[0, :, columns(c, zz, q)],
            xo.at[zz, pl.ds(0, tok), pl.ds(pl.multiple_of(q * rows, rows), rows)],
            xsem.at[16 + j],
        )

    def each(count, action):
        def one(j, carry):
            action(j)
            return carry

        lax.fori_loop(0, count, one, 0)

    loads = [
        pltpu.make_async_copy(
            w_hbm.at[:, pl.ds(h * half, half)], wv.at[h, z, my_b, my_a], lsem.at[h]
        )
        for h in (1, 0)
    ]
    late = [pltpu.make_async_copy(doc_hbm, docv, lsem.at[2])] + [
        pltpu.make_async_copy(
            do_hbm.at[0, :, pl.ds(h * hd, hd)], dos.at[pl.ds(h * tok, tok)], lsem.at[3 + h]
        )
        for h in range(2)
    ]
    for load in loads:
        load.start()
    each(16, lambda j: load_swap(j).start())
    each(16, lambda j: load_own(j).start())
    for load in late:
        load.start()

    barrier = pltpu.get_barrier_semaphore()
    for dev in [sib, part_a, part_b] + zdev[1:]:
        pl.semaphore_signal(barrier, inc=1, device_id=dev, device_id_type=pl.DeviceIdType.MESH)
    extra_up = (y == 1) & (z < NZ - 1)
    extra_down = (y == 0) & (z > 0)

    @pl.when(extra_up)
    def _():
        pl.semaphore_signal(
            barrier, inc=1, device_id=(s + 1, d), device_id_type=pl.DeviceIdType.MESH
        )

    @pl.when(extra_down)
    def _():
        pl.semaphore_signal(
            barrier, inc=1, device_id=(s - 1, d), device_id_type=pl.DeviceIdType.MESH
        )

    loads[0].wait()
    loads[1].wait()

    @pl.when(extra_up | extra_down)
    def _():
        pl.semaphore_wait(barrier, 7)

    @pl.when(jnp.logical_not(extra_up | extra_down))
    def _():
        pl.semaphore_wait(barrier, 6)

    sent = []
    line = []
    swaps = {}

    def swap(src, dst, index):
        copy = remote(src, dst, ssend.at[index], srecv.at[index], sib)
        copy.start()
        sent.append(copy)
        swaps[index] = copy

    def block_at(h, k, b_flip, a_flip):
        return wv.at[h, z_order[k], flip(my_b, b_flip), flip(my_a, a_flip)]

    def push(h, ref, dev, index):
        copy = remote(ref, ref, wsend.at[h, index], wrecv.at[h, index], dev)
        copy.start()
        sent.append(copy)

    def arrived(h, ref, index):
        remote(ref, ref, wsend.at[h, 0], wrecv.at[h, index], sib).wait_recv()

    def stage_z(h, k):
        ref = block_at(h, k, 0, 0)
        zz = z_order[k]
        if k:
            arrived(h, ref, zz)
        up = remote(ref, ref, wsend.at[h, zz], wrecv.at[h, zz], zdev[1])
        down = remote(ref, ref, wsend.at[h, 16 + zz], wrecv.at[h, zz], zdev[3])
        for copy, test in ((up, (zz <= z) & (z < NZ - 1)), (down, (zz >= z) & (z > 0))):
            line.append((copy, test))
            pl.when(test)(copy.start)
        push(h, ref, part_a, 4 + k)
        push(h, ref, part_b, 8 + 2 * k)

    def stage_a(h, k):
        ref = block_at(h, k, 0, 1)
        arrived(h, ref, 4 + k)
        push(h, ref, part_b, 9 + 2 * k)

    def stage_b(h, k, a):
        arrived(h, block_at(h, k, 1, a), 8 + 2 * k + a)

    def stage_d(h, low, high):
        def one(j, carry):
            zz = jnp.where(
                j == 0,
                z_order[0],
                jnp.where(j == 1, z_order[1], jnp.where(j == 2, z_order[2], z_order[3])),
            )
            acc[h] += dot_nn(xo[zz], wv[h, zz].reshape(span, half))
            return carry

        if low == 0:
            acc[h] = jnp.zeros_like(acc[h])
        lax.fori_loop(low, high, one, 0)

    def projected(h):
        swaps[4 + h].wait_recv()
        return (acc[h, :tok] + pacc[h]).astype(BF)

    halo = remote(kv.at[1], kv.at[0], hsend.at[0], hrecv.at[0], ((s + 1) % 8, d))

    def send_halo():
        kv[1] = projected(1)

        @pl.when(s < 7)
        def _():
            halo.start()

        @pl.when(s == 0)
        def _():
            kv[0] = jnp.zeros_like(kv[0])

    def value_grads():
        @pl.when(s > 0)
        def _():
            halo.wait_recv()

        def one(j):
            pgs[j] = dot_nt(dos[...], kv[j, :, hd:])

        each(2, one)

    for stage, *at in ORDER:
        if stage == "z":
            stage_z(*at)
        elif stage == "a":
            stage_a(*at)
        elif stage == "b":
            stage_b(*at)
        elif stage == "d":
            stage_d(*at)
        elif stage == "swap":
            each(16, lambda j: load_swap(j).wait())
            for j in range(NZ):
                swap(xs.at[j], xo.at[j, pl.ds(tok, tok)], j)
        elif stage == "take":
            each(16, lambda j: load_own(j).wait())
            for j in range(NZ):
                swaps[j].wait_recv()
        elif stage == "partial":
            swap(acc.at[at[0], pl.ds(tok, tok)], pacc.at[at[0]], 4 + at[0])
        elif stage == "halo":
            send_halo()
        elif stage == "values":
            value_grads()
        else:
            for load in late:
                load.wait()
            doc = jnp.broadcast_to(docv[...], (tok, tok)).T
            row = lax.broadcasted_iota(jnp.int32, (tok, tok), 0)
            col = lax.broadcasted_iota(jnp.int32, (tok, tok), 1)
            vis[1] = jnp.where((col <= row) & (col + s * tok >= doc), 0.0, -jnp.inf)
            vis[0] = jnp.where((col > row) & (col + (s - 1) * tok >= doc), 0.0, -jnp.inf)
            dot_[...] = dos[...].T

    q_own = projected(0)
    for h in range(2):
        qs[h * tok : (h + 1) * tok, :] = q_own[:, h * hd : (h + 1) * hd]
    qt[...] = qs[...].T

    def attend(h):
        k_own = kv[1, :, :hd]
        k_pri = kv[0, :, :hd]
        at = pl.ds(pl.multiple_of(h * tok, tok), tok)
        s_own = dot_nt(qs[at, :], k_own) * inv_root + vis[1]
        s_pri = dot_nt(qs[at, :], k_pri) * inv_root + vis[0]
        pg_own = pgs[1, at, :]
        pg_pri = pgs[0, at, :]
        top = jnp.max(jnp.maximum(s_own, s_pri), axis=1, keepdims=True)
        e_own = jnp.exp(s_own - top)
        e_pri = jnp.exp(s_pri - top)
        scale = 1.0 / jnp.sum(e_own + e_pri, axis=1, keepdims=True)
        p_own = e_own * scale
        p_pri = e_pri * scale
        l_own = p_own.astype(BF)
        l_pri = p_pri.astype(BF)
        row_dot = jnp.sum(
            l_own.astype(F32) * pg_own + l_pri.astype(F32) * pg_pri, axis=1, keepdims=True
        )
        pst[0, at, :] = l_pri
        pst[1, at, :] = l_own
        dst_[0, at, :] = (p_pri * (pg_pri - row_dot)).astype(BF)
        dst_[1, at, :] = (p_own * (pg_own - row_dot)).astype(BF)

    each(2, attend)

    dkv[0, :hd, :] = (dot_nn(qt[...], dst_[0]) * inv_root).astype(BF)
    dkv[0, hd:, :] = dot_nn(dot_[...], pst[0]).astype(BF)
    back = remote(dkv.at[0], dkv.at[1], hsend.at[1], hrecv.at[1], ((s + 7) % 8, d))

    @pl.when(s > 0)
    def _():
        back.start()

    @pl.when(s == 7)
    def _():
        dkv[1] = jnp.zeros_like(dkv[1])

    dq = (
        (dot_nn(dst_[1], kv[1, :, :hd]) + dot_nn(dst_[0], kv[0, :, :hd])) * inv_root
    ).astype(BF)
    for h in range(2):
        gp[0, :tok, h * hd : (h + 1) * hd] = dq[h * tok : (h + 1) * tok]

    def swap_grads(h):
        swap(gp.at[h, pl.ds(0, tok)], gp.at[h, pl.ds(tok, tok)], 6 + h)

    def take_grads(h):
        swaps[6 + h].wait_recv()
        gpt[h, :, tok:] = gp[h, tok:, :].T

    def chunk(h, i, stage):
        src, dst, dev = {
            0: (gb.at[h, i, 1 - my_b], rb.at[h, i], part_b),
            1: (sa.at[h, i], ra.at[h, i], part_a),
            2: (sz.at[h, i], rz.at[h, i], ((z + i + 1) % NZ * 2 + y, d)),
        }[stage]
        index = (h * NZ + i) * 3 + stage
        return remote(src, dst, gsend.at[index], grecv.at[index], dev)

    def produce(h, i):
        part = dot_nn(gpt[h], xo[(z + i + 1) % NZ]).astype(BF)
        for q in range(4):
            gb[h, i, q // 2, q % 2] = part[:, q * rows : (q + 1) * rows]
        chunk(h, i, 0).start()

    def sum_b(h, i, a_at):
        return gb[h, i, my_b, a_at].astype(F32) + rb[h, i, a_at].astype(F32)

    def send_a(h, i):
        chunk(h, i, 0).wait_recv()
        sa[h, i] = sum_b(h, i, 1 - my_a).astype(BF)
        chunk(h, i, 1).start()

    def send_z(h, i):
        chunk(h, i, 1).wait_recv()
        sz[h, i] = (sum_b(h, i, my_a) + ra[h, i].astype(F32)).astype(BF)
        chunk(h, i, 2).start()

    def finish(h):
        chunk(h, NZ - 1, 1).wait_recv()
        total = sum_b(h, NZ - 1, my_a) + ra[h, NZ - 1].astype(F32)
        for i in range(NZ - 1):
            chunk(h, i, 2).wait_recv()
            total += rz[h, i].astype(F32)
        g_ref[:, h * half : (h + 1) * half] = total.T

    def store(src, plane, zz, q, index):
        return pltpu.make_async_copy(
            src.at[zz, pl.ds(0, tok), pl.ds(q * rows, rows)],
            dx_hbm.at[0, :, columns(plane, zz, q)],
            osem.at[index],
        )

    def swap_dx(zz):
        return remote(
            dxo.at[zz, pl.ds(tok, tok)], dxr.at[zz], ssend.at[8 + zz], srecv.at[8 + zz], sib
        )

    def input_grad(zz):
        part = dot_nt(gp[0], wv[0, zz].reshape(span, half))
        part += dot_nt(gp[1], wv[1, zz].reshape(span, half))
        dxo[zz] = part.astype(BF)
        swap_dx(zz).start()
        for q in range(4):
            store(dxo, c, zz, q, zz * 4 + q).start()

    def take_input_grad(zz):
        swap_dx(zz).wait_recv()
        for q in range(4):
            store(dxr, 1 - c, zz, q, 16 + zz * 4 + q).start()

    swap_grads(0)
    gpt[0, :, :tok] = gp[0, :tok, :].T
    own_dk = dot_nn(qt[...], dst_[1]) * inv_root
    own_dv = dot_nn(dot_[...], pst[1])
    take_grads(0)
    each(NZ, lambda i: produce(0, i))

    @pl.when(s < 7)
    def _():
        back.wait_recv()

    gpt[1, :hd, :tok] = (own_dk + dkv[1, :hd, :].astype(F32)).astype(BF)
    gpt[1, hd:, :tok] = (own_dv + dkv[1, hd:, :].astype(F32)).astype(BF)
    gp[1, :tok, :] = gpt[1, :, :tok].T
    swap_grads(1)
    take_grads(1)

    def both(i):
        produce(1, i)
        send_a(0, i)

    each(NZ, both)

    def spread(i):
        input_grad(i)

        @pl.when(i < NZ - 1)
        def _():
            send_z(0, i)

    each(NZ, spread)

    def tail(i):
        take_input_grad(i)
        send_a(1, i)

        @pl.when(i > 0)
        def _():
            send_z(1, i - 1)

    each(NZ, tail)
    finish(0)
    finish(1)

    def drain(i):
        swap_dx(i).wait_send()
        for q in range(4):
            store(dxo, c, i, q, i * 4 + q).wait()
            store(dxr, 1 - c, i, q, 16 + i * 4 + q).wait()
        for h in range(2):
            chunk(h, i, 0).wait_send()
            chunk(h, i, 1).wait_send()

            @pl.when(i < NZ - 1)
            def _():
                chunk(h, i, 2).wait_send()

    each(NZ, drain)
    for copy in sent:
        copy.wait_send()
    for copy, test in line:
        pl.when(test)(copy.wait_send)

    @pl.when(s < 7)
    def _():
        halo.wait_send()

    @pl.when(s > 0)
    def _():
        back.wait_send()


def kernel_body(layer_inputs, doc_start, w_qkv, d_context):
    tok, width = layer_inputs.shape[1:]
    rows, cols = w_qkv.shape
    hd = cols // 4
    half = 2 * hd
    dma = pltpu.SemaphoreType.DMA
    block = (half, rows)
    return pl.pallas_call(
        fused,
        out_shape=(
            jax.ShapeDtypeStruct(layer_inputs.shape, BF),
            jax.ShapeDtypeStruct((rows, cols), F32),
        ),
        in_specs=[pl.BlockSpec(memory_space=pl.ANY)] * 4,
        out_specs=(
            pl.BlockSpec(memory_space=pl.ANY),
            pl.BlockSpec(memory_space=pltpu.VMEM),
        ),
        scratch_shapes=[
            pltpu.VMEM((NZ, 2 * tok, 4 * rows), BF),
            pltpu.VMEM((NZ, tok, 4 * rows), BF),
            pltpu.VMEM((1, tok), jnp.int32),
            pltpu.VMEM((2, tok, tok), F32),
            pltpu.VMEM((2, NZ, 2, 2, rows, half), BF),
            pltpu.VMEM((2, 2 * tok, half), F32),
            pltpu.VMEM((2, tok, half), F32),
            pltpu.VMEM((2 * tok, hd), BF),
            pltpu.VMEM((hd, 2 * tok), BF),
            pltpu.VMEM((2 * tok, hd), BF),
            pltpu.VMEM((hd, 2 * tok), BF),
            pltpu.VMEM((2, 2 * tok, tok), F32),
            pltpu.VMEM((2, tok, half), BF),
            pltpu.VMEM((2, half, tok), BF),
            pltpu.VMEM((2, 2 * tok, tok), BF),
            pltpu.VMEM((2, 2 * tok, tok), BF),
            pltpu.VMEM((2, 2 * tok, half), BF),
            pltpu.VMEM((2, half, 2 * tok), BF),
            pltpu.VMEM((NZ, 2 * tok, 4 * rows), BF),
            pltpu.VMEM((NZ, tok, 4 * rows), BF),
            pltpu.VMEM((2, NZ, 2, 2) + block, BF),
            pltpu.VMEM((2, NZ, 2) + block, BF),
            pltpu.VMEM((2, NZ) + block, BF),
            pltpu.VMEM((2, NZ) + block, BF),
            pltpu.VMEM((2, NZ) + block, BF),
            pltpu.VMEM((2, NZ) + block, BF),
            dma((5,)),
            dma((32,)),
            dma((2, 20)),
            dma((2, 16)),
            dma((2,)),
            dma((2,)),
            dma((12,)),
            dma((12,)),
            dma((24,)),
            dma((24,)),
            dma((32,)),
        ],
        compiler_params=pltpu.CompilerParams(
            collective_id=0, has_side_effects=True, vmem_limit_bytes=60 * 1024 * 1024
        ),
    )(layer_inputs, doc_start, w_qkv, d_context)


def solution(mesh):
    fits = mesh.shape["seq"] == 8 and mesh.shape["dp"] == 4
    return jax.shard_map(
        kernel_body if fits else body,
        mesh=mesh,
        in_specs=(
            P("dp", "seq", None),
            P("dp", "seq"),
            P(("seq", "dp"), None),
            P("dp", "seq", None),
        ),
        out_specs=(P("dp", "seq", None), P(("seq", "dp"), None)),
        check_vma=False,
    )
```

```python
import jax
import jax.numpy as jnp
from jax import lax
from jax.experimental import pallas as pl
from jax.experimental.pallas import tpu as pltpu
from jax.sharding import PartitionSpec as P

WIN = 256


def from_partner(block, axis, stride):
    count = lax.axis_size(axis)
    route = []
    for low in range(count):
        high = low | 1 << stride
        if high != low and high < count:
            route += [(low, high), (high, low)]
    return lax.ppermute(block, axis, route)


def from_behind(block, axis, distance):
    devices = range(lax.axis_size(axis))
    route = [(i - distance, i) for i in devices if i - distance in devices]
    return lax.ppermute(block, axis, route)


def masked_scores(queries, key_rows, doc_first, query_pos, key_pos):
    inv_root = queries.shape[2] ** (-0.5)
    scores = (
        jnp.einsum("rhd,kd->hrk", queries, key_rows, preferred_element_type=jnp.float32) * inv_root
    )
    visible = (
        (key_pos[None, :] <= query_pos[:, None])
        & (key_pos[None, :] > query_pos[:, None] - WIN)
        & (key_pos[None, :] >= doc_first[:, None])
    )
    return jnp.where(visible[None, :, :], scores, -jnp.inf)


def backward_terms(queries, key_rows, value_rows, out_grad, attn_probs, prob_low, row_dot):
    inv_root = queries.shape[2] ** (-0.5)
    prob_grad = jnp.einsum("rhd,kd->hrk", out_grad, value_rows, preferred_element_type=jnp.float32)
    score_grad = (attn_probs * (prob_grad - row_dot[:, :, None])).astype(jnp.bfloat16)
    grad_query = (
        jnp.einsum("hrk,kd->rhd", score_grad, key_rows, preferred_element_type=jnp.float32)
        * inv_root
    )
    grad_keys = (
        jnp.einsum("hrk,rhd->kd", score_grad, queries, preferred_element_type=jnp.float32)
        * inv_root
    )
    grad_values = jnp.einsum("hrk,rhd->kd", prob_low, out_grad, preferred_element_type=jnp.float32)
    return (grad_query, grad_keys, grad_values)


def local_pass(queries, key_rows, value_rows, out_grad, doc_first, query_pos, key_pos):
    scores = masked_scores(queries, key_rows, doc_first, query_pos, key_pos)
    row_max = jnp.max(scores, axis=2)
    log_total = row_max + jnp.log(jnp.sum(jnp.exp(scores - row_max[:, :, None]), axis=2))
    attn_probs = jnp.exp(scores - log_total[:, :, None])
    prob_low = attn_probs.astype(jnp.bfloat16)
    context = jnp.einsum("hrk,kd->rhd", prob_low, value_rows, preferred_element_type=jnp.float32)
    row_dot = jnp.sum(out_grad.astype(jnp.float32) * context, axis=2).T
    grad_query, grad_keys, grad_values = backward_terms(
        queries, key_rows, value_rows, out_grad, attn_probs, prob_low, row_dot
    )
    return (grad_query, grad_keys, grad_values, log_total, row_dot)


def halve_over_seq(buffer, bit_index):
    half_rows = buffer.shape[0] // 2
    my_bit = lax.axis_index("seq") >> bit_index & 1
    kept_half = lax.dynamic_slice_in_dim(buffer, my_bit * half_rows, half_rows, 0)
    sent_half = lax.dynamic_slice_in_dim(buffer, (1 - my_bit) * half_rows, half_rows, 0)
    return kept_half + from_partner(sent_half.astype(jnp.bfloat16), "seq", bit_index).astype(
        sent_half.dtype
    )


def halve_over_dp(buffer, bit_index):
    half_rows = buffer.shape[0] // 2
    my_bit = lax.axis_index("dp") >> bit_index & 1
    kept_half = lax.dynamic_slice_in_dim(buffer, my_bit * half_rows, half_rows, 0)
    sent_half = lax.dynamic_slice_in_dim(buffer, (1 - my_bit) * half_rows, half_rows, 0)
    return kept_half + from_partner(sent_half.astype(jnp.bfloat16), "dp", bit_index).astype(
        sent_half.dtype
    )


def body(layer_inputs, doc_start, w_qkv, d_context):
    x_local = layer_inputs[0]
    tok_rows = x_local.shape[0]
    q_width = d_context.shape[2]
    head_dim = (w_qkv.shape[1] - q_width) // 2
    heads = q_width // head_dim
    out_grad = d_context[0].reshape(tok_rows, heads, head_dim)
    doc_first = doc_start[0]
    positions = lax.axis_index("seq") * tok_rows + jnp.arange(tok_rows, dtype=jnp.int32)
    full_weights = lax.all_gather(w_qkv, ("seq", "dp"), axis=0, tiled=True)
    projected = jnp.dot(x_local, full_weights, preferred_element_type=jnp.float32)
    projected = projected.astype(jnp.bfloat16)
    queries = projected[:, :q_width].reshape(tok_rows, heads, head_dim)
    key_value = projected[:, q_width:]
    prior = from_behind(key_value, "seq", 1)
    key_rows = jnp.concatenate([prior[:, :head_dim], key_value[:, :head_dim]], axis=0)
    value_rows = jnp.concatenate([prior[:, head_dim:], key_value[:, head_dim:]], axis=0)
    key_pos = jnp.concatenate([positions - tok_rows, positions])
    grad_query, grad_keys, grad_values, log_total, row_dot = local_pass(
        queries, key_rows, value_rows, out_grad, doc_first, positions, key_pos
    )
    returned = from_behind(
        jnp.concatenate([grad_keys[:tok_rows], grad_values[:tok_rows]], axis=1).astype(
            jnp.bfloat16
        ),
        "seq",
        -1,
    ).astype(jnp.float32)
    far_keys = returned[:, :head_dim]
    far_values = returned[:, head_dim:]
    key_grad = (grad_keys[tok_rows:] + far_keys).astype(jnp.bfloat16)
    value_grad = (grad_values[tok_rows:] + far_values).astype(jnp.bfloat16)
    grad_proj = jnp.concatenate(
        [grad_query.astype(jnp.bfloat16).reshape(tok_rows, q_width), key_grad, value_grad], axis=1
    )
    input_grad = lax.dot_general(
        grad_proj, full_weights, (((1,), (1,)), ((), ())), preferred_element_type=jnp.float32
    )
    input_grad = input_grad.astype(jnp.bfloat16).reshape(1, tok_rows, x_local.shape[1])
    partial_grad = lax.dot_general(
        x_local, grad_proj, (((0,), (0,)), ((), ())), preferred_element_type=jnp.float32
    )
    seq_count = lax.axis_size("seq")
    dp_count = lax.axis_size("dp")
    seq_levels = seq_count.bit_length() - 1
    dp_levels = dp_count.bit_length() - 1
    buffer = partial_grad
    for bit_index in range(seq_levels - 1, -1, -1):
        buffer = halve_over_seq(buffer, bit_index)
    for bit_index in range(dp_levels - 1, -1, -1):
        buffer = halve_over_dp(buffer, bit_index)
    return (input_grad, buffer)


BF = jnp.bfloat16
F32 = jnp.float32
NZ = 4
ORDER = (
    ("z", 1, 0), ("swap",), ("z", 1, 1), ("a", 1, 0), ("b", 1, 0, 0), ("z", 1, 2), ("a", 1, 1),
    ("b", 1, 1, 0), ("b", 1, 0, 1), ("z", 1, 3), ("prep",), ("b", 1, 2, 0), ("a", 1, 2),
    ("b", 1, 1, 1), ("b", 1, 3, 0), ("a", 1, 3), ("z", 0, 0), ("take",),
    ("b", 1, 2, 1), ("z", 0, 1), ("b", 1, 3, 1), ("d", 1, 0, 4), ("partial", 1), ("z", 0, 2),
    ("a", 0, 0), ("b", 0, 0, 0), ("halo",), ("z", 0, 3),
    ("b", 0, 1, 0), ("b", 0, 2, 0), ("a", 0, 1), ("a", 0, 2), ("b", 0, 0, 1),
    ("b", 0, 2, 1), ("a", 0, 3), ("b", 0, 3, 0), ("values",), ("b", 0, 1, 1),
    ("d", 0, 0, 3), ("b", 0, 3, 1), ("d", 0, 3, 4), ("partial", 0),
)


def dot_nn(a, b):
    return jnp.dot(a, b, preferred_element_type=F32)


def dot_nt(a, b):
    return lax.dot_general(a, b, (((1,), (1,)), ((), ())), preferred_element_type=F32)


def dot_tn(a, b):
    return lax.dot_general(a, b, (((0,), (0,)), ((), ())), preferred_element_type=F32)


def flip(v, f):
    return v + f * (1 - 2 * v)


def remote(src, dst, send, recv, device):
    return pltpu.make_async_remote_copy(
        src_ref=src,
        dst_ref=dst,
        send_sem=send,
        recv_sem=recv,
        device_id=device,
        device_id_type=pl.DeviceIdType.MESH,
    )


def fused(
    x_hbm, doc_hbm, w_hbm, do_hbm, dx_hbm, g_ref,
    xo, xs, docv, vis, wv, acc, pacc, qs, qt, dos, dot_, pgs, kv, dkv, pst, dst_, gp, gpt, dxo, dxr,
    gb, rb, sa, ra, sz, rz,
    lsem, xsem, wsend, wrecv, hsend, hrecv, ssend, srecv, gsend, grecv, osem,
):
    s = lax.axis_index("seq")
    d = lax.axis_index("dp")
    z, y = s // 2, s % 2
    x, c = d // 2, d % 2
    tok = xs.shape[1]
    rows = wv.shape[4]
    hd = qs.shape[1]
    half = 2 * hd
    span = 4 * rows
    inv_root = hd ** (-0.5)
    my_a = x * (1 - c) + y * c
    my_b = y * (1 - c) + x * c

    def device(zz, yy, xx, cc):
        return (zz * 2 + yy, xx * 2 + cc)

    sib = device(z, y, x, 1 - c)
    part_a = device(z, flip(y, c), flip(x, 1 - c), c)
    part_b = device(z, flip(y, 1 - c), flip(x, c), c)
    zdev = [device((z + k) % NZ, y, x, c) for k in range(NZ)]
    z_order = [
        z,
        jnp.where(z == 0, 1, jnp.where(z == 1, 0, jnp.where(z == 2, 3, 2))),
        jnp.where(z == 0, 2, jnp.where(z == 1, 2, 1)),
        jnp.where(z <= 1, 3, 0),
    ]

    def columns(plane, zz, q):
        b, a = q // 2, q % 2
        yy = b * (1 - plane) + a * plane
        xx = a * (1 - plane) + b * plane
        block = ((zz * 2 + yy) * 2 + xx) * 2 + plane
        return pl.ds(pl.multiple_of(block * rows, rows), rows)

    def load_swap(j):
        zz, q = j // 4, j % 4
        return pltpu.make_async_copy(
            x_hbm.at[0, :, columns(1 - c, zz, q)],
            xs.at[zz, :, pl.ds(pl.multiple_of(q * rows, rows), rows)],
            xsem.at[j],
        )

    def load_own(j):
        zz, q = j // 4, j % 4
        return pltpu.make_async_copy(
            x_hbm.at[0, :, columns(c, zz, q)],
            xo.at[zz, pl.ds(0, tok), pl.ds(pl.multiple_of(q * rows, rows), rows)],
            xsem.at[16 + j],
        )

    def each(count, action):
        def one(j, carry):
            action(j)
            return carry

        lax.fori_loop(0, count, one, 0)

    loads = [
        pltpu.make_async_copy(
            w_hbm.at[:, pl.ds(h * half, half)], wv.at[h, z, my_b, my_a], lsem.at[h]
        )
        for h in (1, 0)
    ]
    late = [pltpu.make_async_copy(doc_hbm, docv, lsem.at[2])] + [
        pltpu.make_async_copy(
            do_hbm.at[0, :, pl.ds(h * hd, hd)], dos.at[pl.ds(h * tok, tok)], lsem.at[3 + h]
        )
        for h in range(2)
    ]
    for load in loads:
        load.start()
    each(16, lambda j: load_swap(j).start())
    each(16, lambda j: load_own(j).start())
    for load in late:
        load.start()

    barrier = pltpu.get_barrier_semaphore()
    for dev in [sib, part_a, part_b] + zdev[1:]:
        pl.semaphore_signal(barrier, inc=1, device_id=dev, device_id_type=pl.DeviceIdType.MESH)
    extra_up = (y == 1) & (z < NZ - 1)
    extra_down = (y == 0) & (z > 0)

    @pl.when(extra_up)
    def _():
        pl.semaphore_signal(
            barrier, inc=1, device_id=(s + 1, d), device_id_type=pl.DeviceIdType.MESH
        )

    @pl.when(extra_down)
    def _():
        pl.semaphore_signal(
            barrier, inc=1, device_id=(s - 1, d), device_id_type=pl.DeviceIdType.MESH
        )

    loads[0].wait()
    loads[1].wait()

    @pl.when(extra_up | extra_down)
    def _():
        pl.semaphore_wait(barrier, 7)

    @pl.when(jnp.logical_not(extra_up | extra_down))
    def _():
        pl.semaphore_wait(barrier, 6)

    sent = []
    line = []
    swaps = {}

    def swap(src, dst, index):
        copy = remote(src, dst, ssend.at[index], srecv.at[index], sib)
        copy.start()
        sent.append(copy)
        swaps[index] = copy

    def block_at(h, k, b_flip, a_flip):
        return wv.at[h, z_order[k], flip(my_b, b_flip), flip(my_a, a_flip)]

    def push(h, ref, dev, index):
        copy = remote(ref, ref, wsend.at[h, index], wrecv.at[h, index], dev)
        copy.start()
        sent.append(copy)

    def arrived(h, ref, index):
        remote(ref, ref, wsend.at[h, 0], wrecv.at[h, index], sib).wait_recv()

    def stage_z(h, k):
        ref = block_at(h, k, 0, 0)
        zz = z_order[k]
        if k:
            arrived(h, ref, zz)
        up = remote(ref, ref, wsend.at[h, zz], wrecv.at[h, zz], zdev[1])
        down = remote(ref, ref, wsend.at[h, 16 + zz], wrecv.at[h, zz], zdev[3])
        for copy, test in ((up, (zz <= z) & (z < NZ - 1)), (down, (zz >= z) & (z > 0))):
            line.append((copy, test))
            pl.when(test)(copy.start)
        push(h, ref, part_a, 4 + k)
        push(h, ref, part_b, 8 + 2 * k)

    def stage_a(h, k):
        ref = block_at(h, k, 0, 1)
        arrived(h, ref, 4 + k)
        push(h, ref, part_b, 9 + 2 * k)

    def stage_b(h, k, a):
        arrived(h, block_at(h, k, 1, a), 8 + 2 * k + a)

    def stage_d(h, low, high):
        def one(j, carry):
            zz = jnp.where(
                j == 0,
                z_order[0],
                jnp.where(j == 1, z_order[1], jnp.where(j == 2, z_order[2], z_order[3])),
            )
            acc[h] += dot_nn(xo[zz], wv[h, zz].reshape(span, half))
            return carry

        if low == 0:
            acc[h] = jnp.zeros_like(acc[h])
        lax.fori_loop(low, high, one, 0)

    def projected(h):
        swaps[4 + h].wait_recv()
        return (acc[h, :tok] + pacc[h]).astype(BF)

    halo = remote(kv.at[1], kv.at[0], hsend.at[0], hrecv.at[0], ((s + 1) % 8, d))

    def send_halo():
        kv[1] = projected(1)

        @pl.when(s < 7)
        def _():
            halo.start()

        @pl.when(s == 0)
        def _():
            kv[0] = jnp.zeros_like(kv[0])

    def value_grads():
        @pl.when(s > 0)
        def _():
            halo.wait_recv()

        def one(j):
            pgs[j] = dot_nt(dos[...], kv[j, :, hd:])

        each(2, one)

    for stage, *at in ORDER:
        if stage == "z":
            stage_z(*at)
        elif stage == "a":
            stage_a(*at)
        elif stage == "b":
            stage_b(*at)
        elif stage == "d":
            stage_d(*at)
        elif stage == "swap":
            each(16, lambda j: load_swap(j).wait())
            for j in range(NZ):
                swap(xs.at[j], xo.at[j, pl.ds(tok, tok)], j)
        elif stage == "take":
            each(16, lambda j: load_own(j).wait())
            for j in range(NZ):
                swaps[j].wait_recv()
        elif stage == "partial":
            swap(acc.at[at[0], pl.ds(tok, tok)], pacc.at[at[0]], 4 + at[0])
        elif stage == "halo":
            send_halo()
        elif stage == "values":
            value_grads()
        else:
            for load in late:
                load.wait()
            doc = jnp.broadcast_to(docv[...], (tok, tok)).T
            row = lax.broadcasted_iota(jnp.int32, (tok, tok), 0)
            col = lax.broadcasted_iota(jnp.int32, (tok, tok), 1)
            vis[1] = jnp.where((col <= row) & (col + s * tok >= doc), 0.0, -jnp.inf)
            vis[0] = jnp.where((col > row) & (col + (s - 1) * tok >= doc), 0.0, -jnp.inf)
            dot_[...] = dos[...].T

    q_own = projected(0)
    for h in range(2):
        qs[h * tok : (h + 1) * tok, :] = q_own[:, h * hd : (h + 1) * hd]
    qt[...] = qs[...].T

    part_rows = tok // 2

    def attend(j):
        k_own = kv[1, :, :hd]
        k_pri = kv[0, :, :hd]
        at = pl.ds(pl.multiple_of(j * part_rows, part_rows), part_rows)
        seen = pl.ds(pl.multiple_of(j % 2 * part_rows, part_rows), part_rows)
        s_own = dot_nt(qs[at, :], k_own) * inv_root + vis[1, seen, :]
        s_pri = dot_nt(qs[at, :], k_pri) * inv_root + vis[0, seen, :]
        pg_own = pgs[1, at, :]
        pg_pri = pgs[0, at, :]
        top = jnp.max(jnp.maximum(s_own, s_pri), axis=1, keepdims=True)
        e_own = jnp.exp(s_own - top)
        e_pri = jnp.exp(s_pri - top)
        scale = 1.0 / jnp.sum(e_own + e_pri, axis=1, keepdims=True)
        p_own = e_own * scale
        p_pri = e_pri * scale
        l_own = p_own.astype(BF)
        l_pri = p_pri.astype(BF)
        row_dot = jnp.sum(
            l_own.astype(F32) * pg_own + l_pri.astype(F32) * pg_pri, axis=1, keepdims=True
        )
        pst[0, at, :] = l_pri
        pst[1, at, :] = l_own
        dst_[0, at, :] = (p_pri * (pg_pri - row_dot)).astype(BF)
        dst_[1, at, :] = (p_own * (pg_own - row_dot)).astype(BF)

    each(4, attend)

    dkv[0, :hd, :] = (dot_nn(qt[...], dst_[0]) * inv_root).astype(BF)
    dkv[0, hd:, :] = dot_nn(dot_[...], pst[0]).astype(BF)
    back = remote(dkv.at[0], dkv.at[1], hsend.at[1], hrecv.at[1], ((s + 7) % 8, d))

    @pl.when(s > 0)
    def _():
        back.start()

    @pl.when(s == 7)
    def _():
        dkv[1] = jnp.zeros_like(dkv[1])

    dq = (
        (dot_nn(dst_[1], kv[1, :, :hd]) + dot_nn(dst_[0], kv[0, :, :hd])) * inv_root
    ).astype(BF)
    for h in range(2):
        gp[0, :tok, h * hd : (h + 1) * hd] = dq[h * tok : (h + 1) * tok]

    def swap_grads(h):
        swap(gp.at[h, pl.ds(0, tok)], gp.at[h, pl.ds(tok, tok)], 6 + h)

    def take_grads(h):
        swaps[6 + h].wait_recv()
        gpt[h, :, tok:] = gp[h, tok:, :].T

    def chunk(h, i, stage):
        src, dst, dev = {
            0: (gb.at[h, i, 1 - my_b], rb.at[h, i], part_b),
            1: (sa.at[h, i], ra.at[h, i], part_a),
            2: (sz.at[h, i], rz.at[h, i], ((z + i + 1) % NZ * 2 + y, d)),
        }[stage]
        index = (h * NZ + i) * 3 + stage
        return remote(src, dst, gsend.at[index], grecv.at[index], dev)

    def produce(h, i):
        part = dot_nn(gpt[h], xo[(z + i + 1) % NZ]).astype(BF)
        for q in range(4):
            gb[h, i, q // 2, q % 2] = part[:, q * rows : (q + 1) * rows]
        chunk(h, i, 0).start()

    def sum_b(h, i, a_at):
        return gb[h, i, my_b, a_at].astype(F32) + rb[h, i, a_at].astype(F32)

    def send_a(h, i):
        chunk(h, i, 0).wait_recv()
        sa[h, i] = sum_b(h, i, 1 - my_a).astype(BF)
        chunk(h, i, 1).start()

    def send_z(h, i):
        chunk(h, i, 1).wait_recv()
        sz[h, i] = (sum_b(h, i, my_a) + ra[h, i].astype(F32)).astype(BF)
        chunk(h, i, 2).start()

    def finish(h):
        chunk(h, NZ - 1, 1).wait_recv()
        total = sum_b(h, NZ - 1, my_a) + ra[h, NZ - 1].astype(F32)
        for i in range(NZ - 1):
            chunk(h, i, 2).wait_recv()
            total += rz[h, i].astype(F32)
        g_ref[:, h * half : (h + 1) * half] = total.T

    def store(src, plane, zz, q, index):
        return pltpu.make_async_copy(
            src.at[zz, pl.ds(0, tok), pl.ds(q * rows, rows)],
            dx_hbm.at[0, :, columns(plane, zz, q)],
            osem.at[index],
        )

    def swap_dx(zz):
        return remote(
            dxo.at[zz, pl.ds(tok, tok)], dxr.at[zz], ssend.at[8 + zz], srecv.at[8 + zz], sib
        )

    def input_grad(zz):
        part = dot_nt(gp[0], wv[0, zz].reshape(span, half))
        part += dot_nt(gp[1], wv[1, zz].reshape(span, half))
        dxo[zz] = part.astype(BF)
        swap_dx(zz).start()
        for q in range(4):
            store(dxo, c, zz, q, zz * 4 + q).start()

    def take_input_grad(zz):
        swap_dx(zz).wait_recv()
        for q in range(4):
            store(dxr, 1 - c, zz, q, 16 + zz * 4 + q).start()

    swap_grads(0)
    gpt[0, :, :tok] = gp[0, :tok, :].T
    own_dk = dot_nn(qt[...], dst_[1]) * inv_root
    own_dv = dot_nn(dot_[...], pst[1])
    take_grads(0)
    each(NZ, lambda i: produce(0, i))

    @pl.when(s < 7)
    def _():
        back.wait_recv()

    gpt[1, :hd, :tok] = (own_dk + dkv[1, :hd, :].astype(F32)).astype(BF)
    gpt[1, hd:, :tok] = (own_dv + dkv[1, hd:, :].astype(F32)).astype(BF)
    gp[1, :tok, :] = gpt[1, :, :tok].T
    swap_grads(1)
    take_grads(1)

    def both(i):
        produce(1, i)
        send_a(0, i)

    each(NZ, both)

    def spread(i):
        @pl.when(i < NZ - 1)
        def _():
            send_z(0, i)

        input_grad(i)
        send_a(1, i)

        @pl.when(i > 0)
        def _():
            send_z(1, i - 1)

    each(NZ, spread)
    each(NZ, take_input_grad)
    finish(0)
    finish(1)

    def drain(i):
        swap_dx(i).wait_send()
        for q in range(4):
            store(dxo, c, i, q, i * 4 + q).wait()
            store(dxr, 1 - c, i, q, 16 + i * 4 + q).wait()
        for h in range(2):
            chunk(h, i, 0).wait_send()
            chunk(h, i, 1).wait_send()

            @pl.when(i < NZ - 1)
            def _():
                chunk(h, i, 2).wait_send()

    each(NZ, drain)
    for copy in sent:
        copy.wait_send()
    for copy, test in line:
        pl.when(test)(copy.wait_send)

    @pl.when(s < 7)
    def _():
        halo.wait_send()

    @pl.when(s > 0)
    def _():
        back.wait_send()


def kernel_body(layer_inputs, doc_start, w_qkv, d_context):
    tok, width = layer_inputs.shape[1:]
    rows, cols = w_qkv.shape
    hd = cols // 4
    half = 2 * hd
    dma = pltpu.SemaphoreType.DMA
    block = (half, rows)
    return pl.pallas_call(
        fused,
        out_shape=(
            jax.ShapeDtypeStruct(layer_inputs.shape, BF),
            jax.ShapeDtypeStruct((rows, cols), F32),
        ),
        in_specs=[pl.BlockSpec(memory_space=pl.ANY)] * 4,
        out_specs=(
            pl.BlockSpec(memory_space=pl.ANY),
            pl.BlockSpec(memory_space=pltpu.VMEM),
        ),
        scratch_shapes=[
            pltpu.VMEM((NZ, 2 * tok, 4 * rows), BF),
            pltpu.VMEM((NZ, tok, 4 * rows), BF),
            pltpu.VMEM((1, tok), jnp.int32),
            pltpu.VMEM((2, tok, tok), F32),
            pltpu.VMEM((2, NZ, 2, 2, rows, half), BF),
            pltpu.VMEM((2, 2 * tok, half), F32),
            pltpu.VMEM((2, tok, half), F32),
            pltpu.VMEM((2 * tok, hd), BF),
            pltpu.VMEM((hd, 2 * tok), BF),
            pltpu.VMEM((2 * tok, hd), BF),
            pltpu.VMEM((hd, 2 * tok), BF),
            pltpu.VMEM((2, 2 * tok, tok), F32),
            pltpu.VMEM((2, tok, half), BF),
            pltpu.VMEM((2, half, tok), BF),
            pltpu.VMEM((2, 2 * tok, tok), BF),
            pltpu.VMEM((2, 2 * tok, tok), BF),
            pltpu.VMEM((2, 2 * tok, half), BF),
            pltpu.VMEM((2, half, 2 * tok), BF),
            pltpu.VMEM((NZ, 2 * tok, 4 * rows), BF),
            pltpu.VMEM((NZ, tok, 4 * rows), BF),
            pltpu.VMEM((2, NZ, 2, 2) + block, BF),
            pltpu.VMEM((2, NZ, 2) + block, BF),
            pltpu.VMEM((2, NZ) + block, BF),
            pltpu.VMEM((2, NZ) + block, BF),
            pltpu.VMEM((2, NZ) + block, BF),
            pltpu.VMEM((2, NZ) + block, BF),
            dma((5,)),
            dma((32,)),
            dma((2, 20)),
            dma((2, 16)),
            dma((2,)),
            dma((2,)),
            dma((12,)),
            dma((12,)),
            dma((24,)),
            dma((24,)),
            dma((32,)),
        ],
        compiler_params=pltpu.CompilerParams(
            collective_id=0, has_side_effects=True, vmem_limit_bytes=60 * 1024 * 1024
        ),
    )(layer_inputs, doc_start, w_qkv, d_context)


def solution(mesh):
    fits = mesh.shape["seq"] == 8 and mesh.shape["dp"] == 4
    return jax.shard_map(
        kernel_body if fits else body,
        mesh=mesh,
        in_specs=(
            P("dp", "seq", None),
            P("dp", "seq"),
            P(("seq", "dp"), None),
            P("dp", "seq", None),
        ),
        out_specs=(P("dp", "seq", None), P(("seq", "dp"), None)),
        check_vma=False,
    )
```

```python
import jax
import jax.numpy as jnp
from jax import lax
from jax.experimental import pallas as pl
from jax.experimental.pallas import tpu as pltpu
from jax.sharding import PartitionSpec as P

WIN = 256


def from_partner(block, axis, stride):
    count = lax.axis_size(axis)
    route = []
    for low in range(count):
        high = low | 1 << stride
        if high != low and high < count:
            route += [(low, high), (high, low)]
    return lax.ppermute(block, axis, route)


def from_behind(block, axis, distance):
    devices = range(lax.axis_size(axis))
    route = [(i - distance, i) for i in devices if i - distance in devices]
    return lax.ppermute(block, axis, route)


def masked_scores(queries, key_rows, doc_first, query_pos, key_pos):
    inv_root = queries.shape[2] ** (-0.5)
    scores = (
        jnp.einsum("rhd,kd->hrk", queries, key_rows, preferred_element_type=jnp.float32) * inv_root
    )
    visible = (
        (key_pos[None, :] <= query_pos[:, None])
        & (key_pos[None, :] > query_pos[:, None] - WIN)
        & (key_pos[None, :] >= doc_first[:, None])
    )
    return jnp.where(visible[None, :, :], scores, -jnp.inf)


def backward_terms(queries, key_rows, value_rows, out_grad, attn_probs, prob_low, row_dot):
    inv_root = queries.shape[2] ** (-0.5)
    prob_grad = jnp.einsum("rhd,kd->hrk", out_grad, value_rows, preferred_element_type=jnp.float32)
    score_grad = (attn_probs * (prob_grad - row_dot[:, :, None])).astype(jnp.bfloat16)
    grad_query = (
        jnp.einsum("hrk,kd->rhd", score_grad, key_rows, preferred_element_type=jnp.float32)
        * inv_root
    )
    grad_keys = (
        jnp.einsum("hrk,rhd->kd", score_grad, queries, preferred_element_type=jnp.float32)
        * inv_root
    )
    grad_values = jnp.einsum("hrk,rhd->kd", prob_low, out_grad, preferred_element_type=jnp.float32)
    return (grad_query, grad_keys, grad_values)


def local_pass(queries, key_rows, value_rows, out_grad, doc_first, query_pos, key_pos):
    scores = masked_scores(queries, key_rows, doc_first, query_pos, key_pos)
    row_max = jnp.max(scores, axis=2)
    log_total = row_max + jnp.log(jnp.sum(jnp.exp(scores - row_max[:, :, None]), axis=2))
    attn_probs = jnp.exp(scores - log_total[:, :, None])
    prob_low = attn_probs.astype(jnp.bfloat16)
    context = jnp.einsum("hrk,kd->rhd", prob_low, value_rows, preferred_element_type=jnp.float32)
    row_dot = jnp.sum(out_grad.astype(jnp.float32) * context, axis=2).T
    grad_query, grad_keys, grad_values = backward_terms(
        queries, key_rows, value_rows, out_grad, attn_probs, prob_low, row_dot
    )
    return (grad_query, grad_keys, grad_values, log_total, row_dot)


def halve_over_seq(buffer, bit_index):
    half_rows = buffer.shape[0] // 2
    my_bit = lax.axis_index("seq") >> bit_index & 1
    kept_half = lax.dynamic_slice_in_dim(buffer, my_bit * half_rows, half_rows, 0)
    sent_half = lax.dynamic_slice_in_dim(buffer, (1 - my_bit) * half_rows, half_rows, 0)
    return kept_half + from_partner(sent_half.astype(jnp.bfloat16), "seq", bit_index).astype(
        sent_half.dtype
    )


def halve_over_dp(buffer, bit_index):
    half_rows = buffer.shape[0] // 2
    my_bit = lax.axis_index("dp") >> bit_index & 1
    kept_half = lax.dynamic_slice_in_dim(buffer, my_bit * half_rows, half_rows, 0)
    sent_half = lax.dynamic_slice_in_dim(buffer, (1 - my_bit) * half_rows, half_rows, 0)
    return kept_half + from_partner(sent_half.astype(jnp.bfloat16), "dp", bit_index).astype(
        sent_half.dtype
    )


def body(layer_inputs, doc_start, w_qkv, d_context):
    x_local = layer_inputs[0]
    tok_rows = x_local.shape[0]
    q_width = d_context.shape[2]
    head_dim = (w_qkv.shape[1] - q_width) // 2
    heads = q_width // head_dim
    out_grad = d_context[0].reshape(tok_rows, heads, head_dim)
    doc_first = doc_start[0]
    positions = lax.axis_index("seq") * tok_rows + jnp.arange(tok_rows, dtype=jnp.int32)
    full_weights = lax.all_gather(w_qkv, ("seq", "dp"), axis=0, tiled=True)
    projected = jnp.dot(x_local, full_weights, preferred_element_type=jnp.float32)
    projected = projected.astype(jnp.bfloat16)
    queries = projected[:, :q_width].reshape(tok_rows, heads, head_dim)
    key_value = projected[:, q_width:]
    prior = from_behind(key_value, "seq", 1)
    key_rows = jnp.concatenate([prior[:, :head_dim], key_value[:, :head_dim]], axis=0)
    value_rows = jnp.concatenate([prior[:, head_dim:], key_value[:, head_dim:]], axis=0)
    key_pos = jnp.concatenate([positions - tok_rows, positions])
    grad_query, grad_keys, grad_values, log_total, row_dot = local_pass(
        queries, key_rows, value_rows, out_grad, doc_first, positions, key_pos
    )
    returned = from_behind(
        jnp.concatenate([grad_keys[:tok_rows], grad_values[:tok_rows]], axis=1).astype(
            jnp.bfloat16
        ),
        "seq",
        -1,
    ).astype(jnp.float32)
    far_keys = returned[:, :head_dim]
    far_values = returned[:, head_dim:]
    key_grad = (grad_keys[tok_rows:] + far_keys).astype(jnp.bfloat16)
    value_grad = (grad_values[tok_rows:] + far_values).astype(jnp.bfloat16)
    grad_proj = jnp.concatenate(
        [grad_query.astype(jnp.bfloat16).reshape(tok_rows, q_width), key_grad, value_grad], axis=1
    )
    input_grad = lax.dot_general(
        grad_proj, full_weights, (((1,), (1,)), ((), ())), preferred_element_type=jnp.float32
    )
    input_grad = input_grad.astype(jnp.bfloat16).reshape(1, tok_rows, x_local.shape[1])
    partial_grad = lax.dot_general(
        x_local, grad_proj, (((0,), (0,)), ((), ())), preferred_element_type=jnp.float32
    )
    seq_count = lax.axis_size("seq")
    dp_count = lax.axis_size("dp")
    seq_levels = seq_count.bit_length() - 1
    dp_levels = dp_count.bit_length() - 1
    buffer = partial_grad
    for bit_index in range(seq_levels - 1, -1, -1):
        buffer = halve_over_seq(buffer, bit_index)
    for bit_index in range(dp_levels - 1, -1, -1):
        buffer = halve_over_dp(buffer, bit_index)
    return (input_grad, buffer)


BF = jnp.bfloat16
F32 = jnp.float32
NZ = 4
ORDER = (
    ("z", 0), ("swap",), ("z", 1), ("a", 0), ("b", 0, 0), ("z", 2), ("a", 1), ("b", 1, 0),
    ("b", 0, 1), ("z", 3), ("prep",), ("a", 2), ("b", 2, 0), ("b", 1, 1), ("a", 3), ("take",),
    ("d", 0, 2), ("b", 3, 0), ("b", 2, 1), ("d", 2, 3), ("b", 3, 1), ("d", 3, 4),
    ("partial", 1), ("partial", 0), ("halo",), ("values",),
)


def dot_nn(a, b):
    return jnp.dot(a, b, preferred_element_type=F32)


def dot_nt(a, b):
    return lax.dot_general(a, b, (((1,), (1,)), ((), ())), preferred_element_type=F32)


def dot_tn(a, b):
    return lax.dot_general(a, b, (((0,), (0,)), ((), ())), preferred_element_type=F32)


def flip(v, f):
    return v + f * (1 - 2 * v)


def remote(src, dst, send, recv, device):
    return pltpu.make_async_remote_copy(
        src_ref=src,
        dst_ref=dst,
        send_sem=send,
        recv_sem=recv,
        device_id=device,
        device_id_type=pl.DeviceIdType.MESH,
    )


def fused(
    x_hbm, doc_hbm, w_hbm, do_hbm, dx_hbm, g_ref,
    xo, xs, docv, vis, wv, acc, pacc, qs, qt, dos, dot_, pgs, kv, dkv, pst, dst_, gp, gpt, dxo, dxr,
    gb, rb, sa, ra, sz, rz,
    lsem, xsem, wsend, wrecv, hsend, hrecv, ssend, srecv, gsend, grecv, osem,
):
    s = lax.axis_index("seq")
    d = lax.axis_index("dp")
    z, y = s // 2, s % 2
    x, c = d // 2, d % 2
    tok = xs.shape[1]
    rows = wv.shape[3]
    hd = qs.shape[1]
    half = 2 * hd
    span = 4 * rows
    inv_root = hd ** (-0.5)
    my_a = x * (1 - c) + y * c
    my_b = y * (1 - c) + x * c

    def device(zz, yy, xx, cc):
        return (zz * 2 + yy, xx * 2 + cc)

    sib = device(z, y, x, 1 - c)
    part_a = device(z, flip(y, c), flip(x, 1 - c), c)
    part_b = device(z, flip(y, 1 - c), flip(x, c), c)
    zdev = [device((z + k) % NZ, y, x, c) for k in range(NZ)]
    z_order = [
        z,
        jnp.where(z == 0, 1, jnp.where(z == 1, 0, jnp.where(z == 2, 3, 2))),
        jnp.where(z == 0, 2, jnp.where(z == 1, 2, 1)),
        jnp.where(z <= 1, 3, 0),
    ]

    def columns(plane, zz, q):
        b, a = q // 2, q % 2
        yy = b * (1 - plane) + a * plane
        xx = a * (1 - plane) + b * plane
        block = ((zz * 2 + yy) * 2 + xx) * 2 + plane
        return pl.ds(pl.multiple_of(block * rows, rows), rows)

    def load_swap(j):
        zz, q = j // 4, j % 4
        return pltpu.make_async_copy(
            x_hbm.at[0, :, columns(1 - c, zz, q)],
            xs.at[zz, :, pl.ds(pl.multiple_of(q * rows, rows), rows)],
            xsem.at[j],
        )

    def load_own(j):
        zz, q = j // 4, j % 4
        return pltpu.make_async_copy(
            x_hbm.at[0, :, columns(c, zz, q)],
            xo.at[zz, pl.ds(0, tok), pl.ds(pl.multiple_of(q * rows, rows), rows)],
            xsem.at[16 + j],
        )

    def each(count, action):
        def one(j, carry):
            action(j)
            return carry

        lax.fori_loop(0, count, one, 0)

    load_w = pltpu.make_async_copy(w_hbm, wv.at[z, my_b, my_a], lsem.at[0])
    late = [pltpu.make_async_copy(doc_hbm, docv, lsem.at[2])] + [
        pltpu.make_async_copy(
            do_hbm.at[0, :, pl.ds(h * hd, hd)], dos.at[pl.ds(h * tok, tok)], lsem.at[3 + h]
        )
        for h in range(2)
    ]
    load_w.start()
    each(16, lambda j: load_swap(j).start())
    each(16, lambda j: load_own(j).start())
    for load in late:
        load.start()

    barrier = pltpu.get_barrier_semaphore()
    for dev in [sib, part_a, part_b] + zdev[1:]:
        pl.semaphore_signal(barrier, inc=1, device_id=dev, device_id_type=pl.DeviceIdType.MESH)
    extra_up = (y == 1) & (z < NZ - 1)
    extra_down = (y == 0) & (z > 0)

    @pl.when(extra_up)
    def _():
        pl.semaphore_signal(
            barrier, inc=1, device_id=(s + 1, d), device_id_type=pl.DeviceIdType.MESH
        )

    @pl.when(extra_down)
    def _():
        pl.semaphore_signal(
            barrier, inc=1, device_id=(s - 1, d), device_id_type=pl.DeviceIdType.MESH
        )

    load_w.wait()

    @pl.when(extra_up | extra_down)
    def _():
        pl.semaphore_wait(barrier, 7)

    @pl.when(jnp.logical_not(extra_up | extra_down))
    def _():
        pl.semaphore_wait(barrier, 6)

    sent = []
    line = []
    swaps = {}

    def swap(src, dst, index):
        copy = remote(src, dst, ssend.at[index], srecv.at[index], sib)
        copy.start()
        sent.append(copy)
        swaps[index] = copy

    def block_at(k, b_flip, a_flip):
        return wv.at[z_order[k], flip(my_b, b_flip), flip(my_a, a_flip)]

    def push(ref, dev, index):
        copy = remote(ref, ref, wsend.at[index], wrecv.at[index], dev)
        copy.start()
        sent.append(copy)

    def arrived(ref, index):
        remote(ref, ref, wsend.at[0], wrecv.at[index], sib).wait_recv()

    def stage_z(k):
        ref = block_at(k, 0, 0)
        zz = z_order[k]
        if k:
            arrived(ref, zz)
        up = remote(ref, ref, wsend.at[zz], wrecv.at[zz], zdev[1])
        down = remote(ref, ref, wsend.at[16 + zz], wrecv.at[zz], zdev[3])
        for copy, test in ((up, (zz <= z) & (z < NZ - 1)), (down, (zz >= z) & (z > 0))):
            line.append((copy, test))
            pl.when(test)(copy.start)
        push(ref, part_a, 4 + k)
        push(ref, part_b, 8 + 2 * k)

    def stage_a(k):
        ref = block_at(k, 0, 1)
        arrived(ref, 4 + k)
        push(ref, part_b, 9 + 2 * k)

    def stage_b(k, a):
        arrived(block_at(k, 1, a), 8 + 2 * k + a)

    def stage_d(low, high):
        def one(j, carry):
            zz = jnp.where(
                j == 0,
                z_order[0],
                jnp.where(j == 1, z_order[1], jnp.where(j == 2, z_order[2], z_order[3])),
            )
            for h in (1, 0):
                ws = wv[zz, :, :, :, h * half : (h + 1) * half].reshape(span, half)
                acc[h] += dot_nn(xo[zz], ws)
            return carry

        if low == 0:
            acc[...] = jnp.zeros_like(acc)
        lax.fori_loop(low, high, one, 0)

    def projected(h):
        swaps[4 + h].wait_recv()
        return (acc[h, :tok] + pacc[h]).astype(BF)

    halo = remote(kv.at[1], kv.at[0], hsend.at[0], hrecv.at[0], ((s + 1) % 8, d))

    def send_halo():
        kv[1] = projected(1)

        @pl.when(s < 7)
        def _():
            halo.start()

        @pl.when(s == 0)
        def _():
            kv[0] = jnp.zeros_like(kv[0])

    def value_grads():
        pgs[1] = dot_nt(dos[...], kv[1, :, hd:])
        q_own = projected(0)
        for h in range(2):
            qs[h * tok : (h + 1) * tok, :] = q_own[:, h * hd : (h + 1) * hd]
        qt[...] = qs[...].T

        @pl.when(s > 0)
        def _():
            halo.wait_recv()

        pgs[0] = dot_nt(dos[...], kv[0, :, hd:])

    for stage, *at in ORDER:
        if stage == "z":
            stage_z(*at)
        elif stage == "a":
            stage_a(*at)
        elif stage == "b":
            stage_b(*at)
        elif stage == "d":
            stage_d(*at)
        elif stage == "swap":
            each(16, lambda j: load_swap(j).wait())
            for j in range(NZ):
                swap(xs.at[j], xo.at[j, pl.ds(tok, tok)], j)
        elif stage == "take":
            each(16, lambda j: load_own(j).wait())
            for j in range(NZ):
                swaps[j].wait_recv()
        elif stage == "partial":
            swap(acc.at[at[0], pl.ds(tok, tok)], pacc.at[at[0]], 4 + at[0])
        elif stage == "halo":
            send_halo()
        elif stage == "values":
            value_grads()
        else:
            for load in late:
                load.wait()
            doc = jnp.broadcast_to(docv[...], (tok, tok)).T
            row = lax.broadcasted_iota(jnp.int32, (tok, tok), 0)
            col = lax.broadcasted_iota(jnp.int32, (tok, tok), 1)
            vis[1] = jnp.where((col <= row) & (col + s * tok >= doc), 0.0, -jnp.inf)
            vis[0] = jnp.where((col > row) & (col + (s - 1) * tok >= doc), 0.0, -jnp.inf)
            dot_[...] = dos[...].T

    part_rows = tok // 2

    def attend(j):
        k_own = kv[1, :, :hd]
        k_pri = kv[0, :, :hd]
        at = pl.ds(pl.multiple_of(j * part_rows, part_rows), part_rows)
        seen = pl.ds(pl.multiple_of(j % 2 * part_rows, part_rows), part_rows)
        s_own = dot_nt(qs[at, :], k_own) * inv_root + vis[1, seen, :]
        s_pri = dot_nt(qs[at, :], k_pri) * inv_root + vis[0, seen, :]
        pg_own = pgs[1, at, :]
        pg_pri = pgs[0, at, :]
        top = jnp.max(jnp.maximum(s_own, s_pri), axis=1, keepdims=True)
        e_own = jnp.exp(s_own - top)
        e_pri = jnp.exp(s_pri - top)
        scale = 1.0 / jnp.sum(e_own + e_pri, axis=1, keepdims=True)
        p_own = e_own * scale
        p_pri = e_pri * scale
        l_own = p_own.astype(BF)
        l_pri = p_pri.astype(BF)
        row_dot = jnp.sum(
            l_own.astype(F32) * pg_own + l_pri.astype(F32) * pg_pri, axis=1, keepdims=True
        )
        pst[0, at, :] = l_pri
        pst[1, at, :] = l_own
        dst_[0, at, :] = (p_pri * (pg_pri - row_dot)).astype(BF)
        dst_[1, at, :] = (p_own * (pg_own - row_dot)).astype(BF)

    each(4, attend)

    dkv[0, :hd, :] = (dot_nn(qt[...], dst_[0]) * inv_root).astype(BF)
    dkv[0, hd:, :] = dot_nn(dot_[...], pst[0]).astype(BF)
    back = remote(dkv.at[0], dkv.at[1], hsend.at[1], hrecv.at[1], ((s + 7) % 8, d))

    @pl.when(s > 0)
    def _():
        back.start()

    @pl.when(s == 7)
    def _():
        dkv[1] = jnp.zeros_like(dkv[1])

    dq = (
        (dot_nn(dst_[1], kv[1, :, :hd]) + dot_nn(dst_[0], kv[0, :, :hd])) * inv_root
    ).astype(BF)
    for h in range(2):
        gp[0, :tok, h * hd : (h + 1) * hd] = dq[h * tok : (h + 1) * tok]

    def swap_grads(h):
        swap(gp.at[h, pl.ds(0, tok)], gp.at[h, pl.ds(tok, tok)], 6 + h)

    def take_grads(h):
        swaps[6 + h].wait_recv()
        gpt[h, :, tok:] = gp[h, tok:, :].T

    def to_b(h, p):
        at = h * 2 + p
        return remote(gb.at[h, p, 1 - my_b], rb.at[h, p], gsend.at[at], grecv.at[at], part_b)

    def to_a(h, p):
        at = 4 + h * 2 + p
        return remote(sa.at[h, p], ra.at[h, p], gsend.at[at], grecv.at[at], part_a)

    def to_z(h, i):
        at = 8 + h * 3 + i
        dev = ((z + i + 1) % NZ * 2 + y, d)
        return remote(sz.at[h, i], rz.at[h, i], gsend.at[at], grecv.at[at], dev)

    def produce(h, p):
        for e in range(2):
            part = dot_nn(gpt[h], xo[(z + p * 2 + e + 1) % NZ]).astype(BF)
            for q in range(4):
                gb[h, p, q // 2, q % 2, e] = part[:, q * rows : (q + 1) * rows]
        to_b(h, p).start()

    def sum_b(h, p, a_at, e):
        return gb[h, p, my_b, a_at, e].astype(F32) + rb[h, p, a_at, e].astype(F32)

    def send_a(h, p):
        to_b(h, p).wait_recv()
        for e in range(2):
            sa[h, p, e] = sum_b(h, p, 1 - my_a, e).astype(BF)
        to_a(h, p).start()

    def send_z(h, p):
        to_a(h, p).wait_recv()
        for e in range(2 - p):
            i = p * 2 + e
            sz[h, i] = (sum_b(h, p, my_a, e) + ra[h, p, e].astype(F32)).astype(BF)
            to_z(h, i).start()

    def finish(h):
        total = sum_b(h, 1, my_a, 1) + ra[h, 1, 1].astype(F32)
        for i in range(NZ - 1):
            to_z(h, i).wait_recv()
            total += rz[h, i].astype(F32)
        g_ref[:, h * half : (h + 1) * half] = total.T

    def store(src, plane, zz, q, index):
        return pltpu.make_async_copy(
            src.at[zz, pl.ds(0, tok), pl.ds(q * rows, rows)],
            dx_hbm.at[0, :, columns(plane, zz, q)],
            osem.at[index],
        )

    def swap_dx(zz):
        return remote(
            dxo.at[zz, pl.ds(tok, tok)], dxr.at[zz], ssend.at[8 + zz], srecv.at[8 + zz], sib
        )

    def input_grad(zz):
        ws = wv[zz].reshape(span, 2 * half)
        part = dot_nt(gp[0], ws[:, :half]) + dot_nt(gp[1], ws[:, half:])
        dxo[zz] = part.astype(BF)
        swap_dx(zz).start()
        for q in range(4):
            store(dxo, c, zz, q, zz * 4 + q).start()

    def take_input_grad(zz):
        swap_dx(zz).wait_recv()
        for q in range(4):
            store(dxr, 1 - c, zz, q, 16 + zz * 4 + q).start()

    swap_grads(0)
    gpt[0, :, :tok] = gp[0, :tok, :].T
    own_dk = dot_nn(qt[...], dst_[1]) * inv_root
    own_dv = dot_nn(dot_[...], pst[1])
    take_grads(0)
    produce(0, 0)
    produce(0, 1)

    @pl.when(s < 7)
    def _():
        back.wait_recv()

    gpt[1, :hd, :tok] = (own_dk + dkv[1, :hd, :].astype(F32)).astype(BF)
    gpt[1, hd:, :tok] = (own_dv + dkv[1, hd:, :].astype(F32)).astype(BF)
    gp[1, :tok, :] = gpt[1, :, :tok].T
    swap_grads(1)
    take_grads(1)

    for p in range(2):
        produce(1, p)
        send_a(0, p)
    send_z(0, 0)
    lax.fori_loop(0, 2, lambda i, carry: (input_grad(i), carry)[1], 0)
    send_a(1, 0)
    send_z(0, 1)
    lax.fori_loop(2, 4, lambda i, carry: (input_grad(i), carry)[1], 0)
    send_a(1, 1)
    send_z(1, 0)
    each(NZ, take_input_grad)
    send_z(1, 1)
    finish(0)
    finish(1)

    def drain(i):
        swap_dx(i).wait_send()
        for q in range(4):
            store(dxo, c, i, q, i * 4 + q).wait()
            store(dxr, 1 - c, i, q, 16 + i * 4 + q).wait()

    each(NZ, drain)
    for copy in sent:
        copy.wait_send()
    for h in range(2):
        for p in range(2):
            to_b(h, p).wait_send()
            to_a(h, p).wait_send()
        for i in range(NZ - 1):
            to_z(h, i).wait_send()
    for copy, test in line:
        pl.when(test)(copy.wait_send)

    @pl.when(s < 7)
    def _():
        halo.wait_send()

    @pl.when(s > 0)
    def _():
        back.wait_send()


def kernel_body(layer_inputs, doc_start, w_qkv, d_context):
    tok, width = layer_inputs.shape[1:]
    rows, cols = w_qkv.shape
    hd = cols // 4
    half = 2 * hd
    dma = pltpu.SemaphoreType.DMA
    block = (half, rows)
    return pl.pallas_call(
        fused,
        out_shape=(
            jax.ShapeDtypeStruct(layer_inputs.shape, BF),
            jax.ShapeDtypeStruct((rows, cols), F32),
        ),
        in_specs=[pl.BlockSpec(memory_space=pl.ANY)] * 4,
        out_specs=(
            pl.BlockSpec(memory_space=pl.ANY),
            pl.BlockSpec(memory_space=pltpu.VMEM),
        ),
        scratch_shapes=[
            pltpu.VMEM((NZ, 2 * tok, 4 * rows), BF),
            pltpu.VMEM((NZ, tok, 4 * rows), BF),
            pltpu.VMEM((1, tok), jnp.int32),
            pltpu.VMEM((2, tok, tok), F32),
            pltpu.VMEM((NZ, 2, 2, rows, cols), BF),
            pltpu.VMEM((2, 2 * tok, half), F32),
            pltpu.VMEM((2, tok, half), F32),
            pltpu.VMEM((2 * tok, hd), BF),
            pltpu.VMEM((hd, 2 * tok), BF),
            pltpu.VMEM((2 * tok, hd), BF),
            pltpu.VMEM((hd, 2 * tok), BF),
            pltpu.VMEM((2, 2 * tok, tok), F32),
            pltpu.VMEM((2, tok, half), BF),
            pltpu.VMEM((2, half, tok), BF),
            pltpu.VMEM((2, 2 * tok, tok), BF),
            pltpu.VMEM((2, 2 * tok, tok), BF),
            pltpu.VMEM((2, 2 * tok, half), BF),
            pltpu.VMEM((2, half, 2 * tok), BF),
            pltpu.VMEM((NZ, 2 * tok, 4 * rows), BF),
            pltpu.VMEM((NZ, tok, 4 * rows), BF),
            pltpu.VMEM((2, 2, 2, 2, 2) + block, BF),
            pltpu.VMEM((2, 2, 2, 2) + block, BF),
            pltpu.VMEM((2, 2, 2) + block, BF),
            pltpu.VMEM((2, 2, 2) + block, BF),
            pltpu.VMEM((2, NZ) + block, BF),
            pltpu.VMEM((2, NZ) + block, BF),
            dma((5,)),
            dma((32,)),
            dma((20,)),
            dma((16,)),
            dma((2,)),
            dma((2,)),
            dma((12,)),
            dma((12,)),
            dma((14,)),
            dma((14,)),
            dma((32,)),
        ],
        compiler_params=pltpu.CompilerParams(
            collective_id=0, has_side_effects=True, vmem_limit_bytes=60 * 1024 * 1024
        ),
    )(layer_inputs, doc_start, w_qkv, d_context)


def solution(mesh):
    fits = mesh.shape["seq"] == 8 and mesh.shape["dp"] == 4
    return jax.shard_map(
        kernel_body if fits else body,
        mesh=mesh,
        in_specs=(
            P("dp", "seq", None),
            P("dp", "seq"),
            P(("seq", "dp"), None),
            P("dp", "seq", None),
        ),
        out_specs=(P("dp", "seq", None), P(("seq", "dp"), None)),
        check_vma=False,
    )
```

```python
import jax
import jax.numpy as jnp
from jax import lax
from jax.experimental import pallas as pl
from jax.experimental.pallas import tpu as pltpu
from jax.sharding import PartitionSpec as P

WIN = 256


def from_partner(block, axis, stride):
    count = lax.axis_size(axis)
    route = []
    for low in range(count):
        high = low | 1 << stride
        if high != low and high < count:
            route += [(low, high), (high, low)]
    return lax.ppermute(block, axis, route)


def from_behind(block, axis, distance):
    devices = range(lax.axis_size(axis))
    route = [(i - distance, i) for i in devices if i - distance in devices]
    return lax.ppermute(block, axis, route)


def masked_scores(queries, key_rows, doc_first, query_pos, key_pos):
    inv_root = queries.shape[2] ** (-0.5)
    scores = (
        jnp.einsum("rhd,kd->hrk", queries, key_rows, preferred_element_type=jnp.float32) * inv_root
    )
    visible = (
        (key_pos[None, :] <= query_pos[:, None])
        & (key_pos[None, :] > query_pos[:, None] - WIN)
        & (key_pos[None, :] >= doc_first[:, None])
    )
    return jnp.where(visible[None, :, :], scores, -jnp.inf)


def backward_terms(queries, key_rows, value_rows, out_grad, attn_probs, prob_low, row_dot):
    inv_root = queries.shape[2] ** (-0.5)
    prob_grad = jnp.einsum("rhd,kd->hrk", out_grad, value_rows, preferred_element_type=jnp.float32)
    score_grad = (attn_probs * (prob_grad - row_dot[:, :, None])).astype(jnp.bfloat16)
    grad_query = (
        jnp.einsum("hrk,kd->rhd", score_grad, key_rows, preferred_element_type=jnp.float32)
        * inv_root
    )
    grad_keys = (
        jnp.einsum("hrk,rhd->kd", score_grad, queries, preferred_element_type=jnp.float32)
        * inv_root
    )
    grad_values = jnp.einsum("hrk,rhd->kd", prob_low, out_grad, preferred_element_type=jnp.float32)
    return (grad_query, grad_keys, grad_values)


def local_pass(queries, key_rows, value_rows, out_grad, doc_first, query_pos, key_pos):
    scores = masked_scores(queries, key_rows, doc_first, query_pos, key_pos)
    row_max = jnp.max(scores, axis=2)
    log_total = row_max + jnp.log(jnp.sum(jnp.exp(scores - row_max[:, :, None]), axis=2))
    attn_probs = jnp.exp(scores - log_total[:, :, None])
    prob_low = attn_probs.astype(jnp.bfloat16)
    context = jnp.einsum("hrk,kd->rhd", prob_low, value_rows, preferred_element_type=jnp.float32)
    row_dot = jnp.sum(out_grad.astype(jnp.float32) * context, axis=2).T
    grad_query, grad_keys, grad_values = backward_terms(
        queries, key_rows, value_rows, out_grad, attn_probs, prob_low, row_dot
    )
    return (grad_query, grad_keys, grad_values, log_total, row_dot)


def halve_over_seq(buffer, bit_index):
    half_rows = buffer.shape[0] // 2
    my_bit = lax.axis_index("seq") >> bit_index & 1
    kept_half = lax.dynamic_slice_in_dim(buffer, my_bit * half_rows, half_rows, 0)
    sent_half = lax.dynamic_slice_in_dim(buffer, (1 - my_bit) * half_rows, half_rows, 0)
    return kept_half + from_partner(sent_half.astype(jnp.bfloat16), "seq", bit_index).astype(
        sent_half.dtype
    )


def halve_over_dp(buffer, bit_index):
    half_rows = buffer.shape[0] // 2
    my_bit = lax.axis_index("dp") >> bit_index & 1
    kept_half = lax.dynamic_slice_in_dim(buffer, my_bit * half_rows, half_rows, 0)
    sent_half = lax.dynamic_slice_in_dim(buffer, (1 - my_bit) * half_rows, half_rows, 0)
    return kept_half + from_partner(sent_half.astype(jnp.bfloat16), "dp", bit_index).astype(
        sent_half.dtype
    )


def body(layer_inputs, doc_start, w_qkv, d_context):
    x_local = layer_inputs[0]
    tok_rows = x_local.shape[0]
    q_width = d_context.shape[2]
    head_dim = (w_qkv.shape[1] - q_width) // 2
    heads = q_width // head_dim
    out_grad = d_context[0].reshape(tok_rows, heads, head_dim)
    doc_first = doc_start[0]
    positions = lax.axis_index("seq") * tok_rows + jnp.arange(tok_rows, dtype=jnp.int32)
    full_weights = lax.all_gather(w_qkv, ("seq", "dp"), axis=0, tiled=True)
    projected = jnp.dot(x_local, full_weights, preferred_element_type=jnp.float32)
    projected = projected.astype(jnp.bfloat16)
    queries = projected[:, :q_width].reshape(tok_rows, heads, head_dim)
    key_value = projected[:, q_width:]
    prior = from_behind(key_value, "seq", 1)
    key_rows = jnp.concatenate([prior[:, :head_dim], key_value[:, :head_dim]], axis=0)
    value_rows = jnp.concatenate([prior[:, head_dim:], key_value[:, head_dim:]], axis=0)
    key_pos = jnp.concatenate([positions - tok_rows, positions])
    grad_query, grad_keys, grad_values, log_total, row_dot = local_pass(
        queries, key_rows, value_rows, out_grad, doc_first, positions, key_pos
    )
    returned = from_behind(
        jnp.concatenate([grad_keys[:tok_rows], grad_values[:tok_rows]], axis=1).astype(
            jnp.bfloat16
        ),
        "seq",
        -1,
    ).astype(jnp.float32)
    far_keys = returned[:, :head_dim]
    far_values = returned[:, head_dim:]
    key_grad = (grad_keys[tok_rows:] + far_keys).astype(jnp.bfloat16)
    value_grad = (grad_values[tok_rows:] + far_values).astype(jnp.bfloat16)
    grad_proj = jnp.concatenate(
        [grad_query.astype(jnp.bfloat16).reshape(tok_rows, q_width), key_grad, value_grad], axis=1
    )
    input_grad = lax.dot_general(
        grad_proj, full_weights, (((1,), (1,)), ((), ())), preferred_element_type=jnp.float32
    )
    input_grad = input_grad.astype(jnp.bfloat16).reshape(1, tok_rows, x_local.shape[1])
    partial_grad = lax.dot_general(
        x_local, grad_proj, (((0,), (0,)), ((), ())), preferred_element_type=jnp.float32
    )
    seq_count = lax.axis_size("seq")
    dp_count = lax.axis_size("dp")
    seq_levels = seq_count.bit_length() - 1
    dp_levels = dp_count.bit_length() - 1
    buffer = partial_grad
    for bit_index in range(seq_levels - 1, -1, -1):
        buffer = halve_over_seq(buffer, bit_index)
    for bit_index in range(dp_levels - 1, -1, -1):
        buffer = halve_over_dp(buffer, bit_index)
    return (input_grad, buffer)


BF = jnp.bfloat16
F32 = jnp.float32
NZ = 4
ORDER = (
    ("z", 1, 0), ("swap",), ("z", 1, 1), ("a", 1, 0), ("b", 1, 0, 0), ("z", 1, 2), ("a", 1, 1),
    ("b", 1, 1, 0), ("b", 1, 0, 1), ("z", 1, 3), ("prep",), ("b", 1, 2, 0), ("a", 1, 2),
    ("b", 1, 1, 1), ("b", 1, 3, 0), ("a", 1, 3), ("z", 0, 0), ("take",),
    ("b", 1, 2, 1), ("z", 0, 1), ("b", 1, 3, 1), ("d", 1, 0, 4), ("partial", 1), ("z", 0, 2),
    ("a", 0, 0), ("b", 0, 0, 0), ("halo",), ("z", 0, 3),
    ("b", 0, 1, 0), ("b", 0, 2, 0), ("a", 0, 1), ("a", 0, 2), ("b", 0, 0, 1),
    ("b", 0, 2, 1), ("a", 0, 3), ("b", 0, 3, 0), ("values",), ("b", 0, 1, 1),
    ("d", 0, 0, 3), ("b", 0, 3, 1), ("d", 0, 3, 4), ("partial", 0),
)


def dot_nn(a, b):
    return jnp.dot(a, b, preferred_element_type=F32)


def dot_nt(a, b):
    return lax.dot_general(a, b, (((1,), (1,)), ((), ())), preferred_element_type=F32)


def dot_tn(a, b):
    return lax.dot_general(a, b, (((0,), (0,)), ((), ())), preferred_element_type=F32)


def flip(v, f):
    return v + f * (1 - 2 * v)


def remote(src, dst, send, recv, device):
    return pltpu.make_async_remote_copy(
        src_ref=src,
        dst_ref=dst,
        send_sem=send,
        recv_sem=recv,
        device_id=device,
        device_id_type=pl.DeviceIdType.MESH,
    )


def fused(
    x_hbm, doc_hbm, w_hbm, do_hbm, dx_hbm, g_ref,
    xo, xs, docv, vis, wv, acc, pacc, qs, qt, dos, dot_, pgs, kv, dkv, pst, dst_, gp, gpt, dxo, dxr,
    gb, rb, sa, ra, sz, rz,
    lsem, xsem, wsend, wrecv, hsend, hrecv, ssend, srecv, gsend, grecv, osem,
):
    s = lax.axis_index("seq")
    d = lax.axis_index("dp")
    z, y = s // 2, s % 2
    x, c = d // 2, d % 2
    tok = xs.shape[1]
    rows = wv.shape[4]
    hd = qs.shape[1]
    half = 2 * hd
    span = 4 * rows
    inv_root = hd ** (-0.5)
    my_a = x * (1 - c) + y * c
    my_b = y * (1 - c) + x * c

    def device(zz, yy, xx, cc):
        return (zz * 2 + yy, xx * 2 + cc)

    sib = device(z, y, x, 1 - c)
    part_a = device(z, flip(y, c), flip(x, 1 - c), c)
    part_b = device(z, flip(y, 1 - c), flip(x, c), c)
    zdev = [device((z + k) % NZ, y, x, c) for k in range(NZ)]
    z_order = [
        z,
        jnp.where(z == 0, 1, jnp.where(z == 1, 0, jnp.where(z == 2, 3, 2))),
        jnp.where(z == 0, 2, jnp.where(z == 1, 2, 1)),
        jnp.where(z <= 1, 3, 0),
    ]

    def columns(plane, zz, q):
        b, a = q // 2, q % 2
        yy = b * (1 - plane) + a * plane
        xx = a * (1 - plane) + b * plane
        block = ((zz * 2 + yy) * 2 + xx) * 2 + plane
        return pl.ds(pl.multiple_of(block * rows, rows), rows)

    def load_swap(j):
        zz, q = j // 4, j % 4
        return pltpu.make_async_copy(
            x_hbm.at[0, :, columns(1 - c, zz, q)],
            xs.at[zz, :, pl.ds(pl.multiple_of(q * rows, rows), rows)],
            xsem.at[j],
        )

    def load_own(j):
        zz, q = j // 4, j % 4
        return pltpu.make_async_copy(
            x_hbm.at[0, :, columns(c, zz, q)],
            xo.at[zz, pl.ds(0, tok), pl.ds(pl.multiple_of(q * rows, rows), rows)],
            xsem.at[16 + j],
        )

    def each(count, action):
        def one(j, carry):
            action(j)
            return carry

        lax.fori_loop(0, count, one, 0)

    loads = [
        pltpu.make_async_copy(
            w_hbm.at[:, pl.ds(h * half, half)], wv.at[h, z, my_b, my_a], lsem.at[h]
        )
        for h in (1, 0)
    ]
    late = [pltpu.make_async_copy(doc_hbm, docv, lsem.at[2])] + [
        pltpu.make_async_copy(
            do_hbm.at[0, :, pl.ds(h * hd, hd)], dos.at[pl.ds(h * tok, tok)], lsem.at[3 + h]
        )
        for h in range(2)
    ]
    for load in loads:
        load.start()
    each(16, lambda j: load_swap(j).start())
    each(16, lambda j: load_own(j).start())
    for load in late:
        load.start()

    barrier = pltpu.get_barrier_semaphore()
    for dev in [sib, part_a, part_b] + zdev[1:]:
        pl.semaphore_signal(barrier, inc=1, device_id=dev, device_id_type=pl.DeviceIdType.MESH)
    extra_up = (y == 1) & (z < NZ - 1)
    extra_down = (y == 0) & (z > 0)

    @pl.when(extra_up)
    def _():
        pl.semaphore_signal(
            barrier, inc=1, device_id=(s + 1, d), device_id_type=pl.DeviceIdType.MESH
        )

    @pl.when(extra_down)
    def _():
        pl.semaphore_signal(
            barrier, inc=1, device_id=(s - 1, d), device_id_type=pl.DeviceIdType.MESH
        )

    loads[0].wait()
    loads[1].wait()

    @pl.when(extra_up | extra_down)
    def _():
        pl.semaphore_wait(barrier, 7)

    @pl.when(jnp.logical_not(extra_up | extra_down))
    def _():
        pl.semaphore_wait(barrier, 6)

    sent = []
    line = []
    swaps = {}

    def swap(src, dst, index):
        copy = remote(src, dst, ssend.at[index], srecv.at[index], sib)
        copy.start()
        sent.append(copy)
        swaps[index] = copy

    def block_at(h, k, b_flip, a_flip):
        return wv.at[h, z_order[k], flip(my_b, b_flip), flip(my_a, a_flip)]

    def push(h, ref, dev, index):
        copy = remote(ref, ref, wsend.at[h, index], wrecv.at[h, index], dev)
        copy.start()
        sent.append(copy)

    def arrived(h, ref, index):
        remote(ref, ref, wsend.at[h, 0], wrecv.at[h, index], sib).wait_recv()

    def stage_z(h, k):
        ref = block_at(h, k, 0, 0)
        zz = z_order[k]
        if k:
            arrived(h, ref, zz)
        up = remote(ref, ref, wsend.at[h, zz], wrecv.at[h, zz], zdev[1])
        down = remote(ref, ref, wsend.at[h, 16 + zz], wrecv.at[h, zz], zdev[3])
        for copy, test in ((up, (zz <= z) & (z < NZ - 1)), (down, (zz >= z) & (z > 0))):
            line.append((copy, test))
            pl.when(test)(copy.start)
        push(h, ref, part_a, 4 + k)
        push(h, ref, part_b, 8 + 2 * k)

    def stage_a(h, k):
        ref = block_at(h, k, 0, 1)
        arrived(h, ref, 4 + k)
        push(h, ref, part_b, 9 + 2 * k)

    def stage_b(h, k, a):
        arrived(h, block_at(h, k, 1, a), 8 + 2 * k + a)

    def stage_d(h, low, high):
        def one(j, carry):
            zz = jnp.where(
                j == 0,
                z_order[0],
                jnp.where(j == 1, z_order[1], jnp.where(j == 2, z_order[2], z_order[3])),
            )
            acc[h] += dot_nn(xo[zz], wv[h, zz].reshape(span, half))
            return carry

        if low == 0:
            acc[h] = jnp.zeros_like(acc[h])
        lax.fori_loop(low, high, one, 0)

    def projected(h):
        swaps[4 + h].wait_recv()
        return (acc[h, :tok] + pacc[h]).astype(BF)

    halo = remote(kv.at[1], kv.at[0], hsend.at[0], hrecv.at[0], ((s + 1) % 8, d))

    def send_halo():
        kv[1] = projected(1)

        @pl.when(s < 7)
        def _():
            halo.start()

        @pl.when(s == 0)
        def _():
            kv[0] = jnp.zeros_like(kv[0])

    def value_grads():
        @pl.when(s > 0)
        def _():
            halo.wait_recv()

        def one(j):
            pgs[j] = dot_nt(dos[...], kv[j, :, hd:])

        each(2, one)

    for stage, *at in ORDER:
        if stage == "z":
            stage_z(*at)
        elif stage == "a":
            stage_a(*at)
        elif stage == "b":
            stage_b(*at)
        elif stage == "d":
            stage_d(*at)
        elif stage == "swap":
            each(16, lambda j: load_swap(j).wait())
            for j in range(NZ):
                swap(xs.at[j], xo.at[j, pl.ds(tok, tok)], j)
        elif stage == "take":
            each(16, lambda j: load_own(j).wait())
            for j in range(NZ):
                swaps[j].wait_recv()
        elif stage == "partial":
            swap(acc.at[at[0], pl.ds(tok, tok)], pacc.at[at[0]], 4 + at[0])
        elif stage == "halo":
            send_halo()
        elif stage == "values":
            value_grads()
        else:
            for load in late:
                load.wait()
            doc = jnp.broadcast_to(docv[...], (tok, tok)).T
            row = lax.broadcasted_iota(jnp.int32, (tok, tok), 0)
            col = lax.broadcasted_iota(jnp.int32, (tok, tok), 1)
            vis[1] = jnp.where((col <= row) & (col + s * tok >= doc), 0.0, -jnp.inf)
            vis[0] = jnp.where((col > row) & (col + (s - 1) * tok >= doc), 0.0, -jnp.inf)
            dot_[...] = dos[...].T

    q_own = projected(0)
    for h in range(2):
        qs[h * tok : (h + 1) * tok, :] = q_own[:, h * hd : (h + 1) * hd]
    qt[...] = qs[...].T

    part_rows = tok // 2

    def attend(j):
        k_own = kv[1, :, :hd]
        k_pri = kv[0, :, :hd]
        at = pl.ds(pl.multiple_of(j * part_rows, part_rows), part_rows)
        seen = pl.ds(pl.multiple_of(j % 2 * part_rows, part_rows), part_rows)
        s_own = dot_nt(qs[at, :], k_own) * inv_root + vis[1, seen, :]
        s_pri = dot_nt(qs[at, :], k_pri) * inv_root + vis[0, seen, :]
        pg_own = pgs[1, at, :]
        pg_pri = pgs[0, at, :]
        top = jnp.max(jnp.maximum(s_own, s_pri), axis=1, keepdims=True)
        e_own = jnp.exp(s_own - top)
        e_pri = jnp.exp(s_pri - top)
        scale = 1.0 / jnp.sum(e_own + e_pri, axis=1, keepdims=True)
        p_own = e_own * scale
        p_pri = e_pri * scale
        l_own = p_own.astype(BF)
        l_pri = p_pri.astype(BF)
        row_dot = jnp.sum(
            l_own.astype(F32) * pg_own + l_pri.astype(F32) * pg_pri, axis=1, keepdims=True
        )
        pst[0, at, :] = l_pri
        pst[1, at, :] = l_own
        dst_[0, at, :] = (p_pri * (pg_pri - row_dot)).astype(BF)
        dst_[1, at, :] = (p_own * (pg_own - row_dot)).astype(BF)

    each(4, attend)

    dkv[0, :hd, :] = (dot_nn(qt[...], dst_[0]) * inv_root).astype(BF)
    dkv[0, hd:, :] = dot_nn(dot_[...], pst[0]).astype(BF)
    back = remote(dkv.at[0], dkv.at[1], hsend.at[1], hrecv.at[1], ((s + 7) % 8, d))

    @pl.when(s > 0)
    def _():
        back.start()

    @pl.when(s == 7)
    def _():
        dkv[1] = jnp.zeros_like(dkv[1])

    dq = (
        (dot_nn(dst_[1], kv[1, :, :hd]) + dot_nn(dst_[0], kv[0, :, :hd])) * inv_root
    ).astype(BF)
    for h in range(2):
        gp[0, :tok, h * hd : (h + 1) * hd] = dq[h * tok : (h + 1) * tok]

    def swap_grads(h):
        swap(gp.at[h, pl.ds(0, tok)], gp.at[h, pl.ds(tok, tok)], 6 + h)

    def take_grads(h):
        swaps[6 + h].wait_recv()
        gpt[h, :, tok:] = gp[h, tok:, :].T

    def to_b(h, p):
        at = h * 2 + p
        return remote(gb.at[h, p, 1 - my_b], rb.at[h, p], gsend.at[at], grecv.at[at], part_b)

    def to_a(h, p):
        at = 4 + h * 2 + p
        return remote(sa.at[h, p], ra.at[h, p], gsend.at[at], grecv.at[at], part_a)

    def to_z(h, i):
        at = 8 + h * 3 + i
        dev = ((z + i + 1) % NZ * 2 + y, d)
        return remote(sz.at[h, i], rz.at[h, i], gsend.at[at], grecv.at[at], dev)

    def produce(h, p):
        for e in range(2):
            part = dot_nn(gpt[h], xo[(z + p * 2 + e + 1) % NZ]).astype(BF)
            for q in range(4):
                gb[h, p, q // 2, q % 2, e] = part[:, q * rows : (q + 1) * rows]
        to_b(h, p).start()

    def sum_b(h, p, a_at, e):
        return gb[h, p, my_b, a_at, e].astype(F32) + rb[h, p, a_at, e].astype(F32)

    def send_a(h, p):
        to_b(h, p).wait_recv()
        for e in range(2):
            sa[h, p, e] = sum_b(h, p, 1 - my_a, e).astype(BF)
        to_a(h, p).start()

    def send_z(h, p):
        to_a(h, p).wait_recv()
        for e in range(2 - p):
            i = p * 2 + e
            sz[h, i] = (sum_b(h, p, my_a, e) + ra[h, p, e].astype(F32)).astype(BF)
            to_z(h, i).start()

    def finish(h):
        total = sum_b(h, 1, my_a, 1) + ra[h, 1, 1].astype(F32)
        for i in range(NZ - 1):
            to_z(h, i).wait_recv()
            total += rz[h, i].astype(F32)
        g_ref[:, h * half : (h + 1) * half] = total.T

    def store(src, plane, zz, q, index):
        return pltpu.make_async_copy(
            src.at[zz, pl.ds(0, tok), pl.ds(q * rows, rows)],
            dx_hbm.at[0, :, columns(plane, zz, q)],
            osem.at[index],
        )

    def swap_dx(zz):
        return remote(
            dxo.at[zz, pl.ds(tok, tok)], dxr.at[zz], ssend.at[8 + zz], srecv.at[8 + zz], sib
        )

    def input_grad(zz):
        part = dot_nt(gp[0], wv[0, zz].reshape(span, half))
        part += dot_nt(gp[1], wv[1, zz].reshape(span, half))
        dxo[zz] = part.astype(BF)
        swap_dx(zz).start()
        for q in range(4):
            store(dxo, c, zz, q, zz * 4 + q).start()

    def take_input_grad(zz):
        swap_dx(zz).wait_recv()
        for q in range(4):
            store(dxr, 1 - c, zz, q, 16 + zz * 4 + q).start()

    swap_grads(0)
    gpt[0, :, :tok] = gp[0, :tok, :].T
    own_dk = dot_nn(qt[...], dst_[1]) * inv_root
    own_dv = dot_nn(dot_[...], pst[1])
    take_grads(0)
    produce(0, 0)
    produce(0, 1)

    @pl.when(s < 7)
    def _():
        back.wait_recv()

    gpt[1, :hd, :tok] = (own_dk + dkv[1, :hd, :].astype(F32)).astype(BF)
    gpt[1, hd:, :tok] = (own_dv + dkv[1, hd:, :].astype(F32)).astype(BF)
    gp[1, :tok, :] = gpt[1, :, :tok].T
    swap_grads(1)
    take_grads(1)

    for p in range(2):
        produce(1, p)
        send_a(0, p)
    send_z(0, 0)
    lax.fori_loop(0, 2, lambda i, carry: (input_grad(i), carry)[1], 0)
    send_a(1, 0)
    send_z(0, 1)
    lax.fori_loop(2, 4, lambda i, carry: (input_grad(i), carry)[1], 0)
    send_a(1, 1)
    send_z(1, 0)
    each(NZ, take_input_grad)
    send_z(1, 1)
    finish(0)
    finish(1)

    def drain(i):
        swap_dx(i).wait_send()
        for q in range(4):
            store(dxo, c, i, q, i * 4 + q).wait()
            store(dxr, 1 - c, i, q, 16 + i * 4 + q).wait()

    each(NZ, drain)
    for copy in sent:
        copy.wait_send()
    for h in range(2):
        for p in range(2):
            to_b(h, p).wait_send()
            to_a(h, p).wait_send()
        for i in range(NZ - 1):
            to_z(h, i).wait_send()
    for copy, test in line:
        pl.when(test)(copy.wait_send)

    @pl.when(s < 7)
    def _():
        halo.wait_send()

    @pl.when(s > 0)
    def _():
        back.wait_send()


def kernel_body(layer_inputs, doc_start, w_qkv, d_context):
    tok, width = layer_inputs.shape[1:]
    rows, cols = w_qkv.shape
    hd = cols // 4
    half = 2 * hd
    dma = pltpu.SemaphoreType.DMA
    block = (half, rows)
    return pl.pallas_call(
        fused,
        out_shape=(
            jax.ShapeDtypeStruct(layer_inputs.shape, BF),
            jax.ShapeDtypeStruct((rows, cols), F32),
        ),
        in_specs=[pl.BlockSpec(memory_space=pl.ANY)] * 4,
        out_specs=(
            pl.BlockSpec(memory_space=pl.ANY),
            pl.BlockSpec(memory_space=pltpu.VMEM),
        ),
        scratch_shapes=[
            pltpu.VMEM((NZ, 2 * tok, 4 * rows), BF),
            pltpu.VMEM((NZ, tok, 4 * rows), BF),
            pltpu.VMEM((1, tok), jnp.int32),
            pltpu.VMEM((2, tok, tok), F32),
            pltpu.VMEM((2, NZ, 2, 2, rows, half), BF),
            pltpu.VMEM((2, 2 * tok, half), F32),
            pltpu.VMEM((2, tok, half), F32),
            pltpu.VMEM((2 * tok, hd), BF),
            pltpu.VMEM((hd, 2 * tok), BF),
            pltpu.VMEM((2 * tok, hd), BF),
            pltpu.VMEM((hd, 2 * tok), BF),
            pltpu.VMEM((2, 2 * tok, tok), F32),
            pltpu.VMEM((2, tok, half), BF),
            pltpu.VMEM((2, half, tok), BF),
            pltpu.VMEM((2, 2 * tok, tok), BF),
            pltpu.VMEM((2, 2 * tok, tok), BF),
            pltpu.VMEM((2, 2 * tok, half), BF),
            pltpu.VMEM((2, half, 2 * tok), BF),
            pltpu.VMEM((NZ, 2 * tok, 4 * rows), BF),
            pltpu.VMEM((NZ, tok, 4 * rows), BF),
            pltpu.VMEM((2, 2, 2, 2, 2) + block, BF),
            pltpu.VMEM((2, 2, 2, 2) + block, BF),
            pltpu.VMEM((2, 2, 2) + block, BF),
            pltpu.VMEM((2, 2, 2) + block, BF),
            pltpu.VMEM((2, NZ) + block, BF),
            pltpu.VMEM((2, NZ) + block, BF),
            dma((5,)),
            dma((32,)),
            dma((2, 20)),
            dma((2, 16)),
            dma((2,)),
            dma((2,)),
            dma((12,)),
            dma((12,)),
            dma((14,)),
            dma((14,)),
            dma((32,)),
        ],
        compiler_params=pltpu.CompilerParams(
            collective_id=0, has_side_effects=True, vmem_limit_bytes=60 * 1024 * 1024
        ),
    )(layer_inputs, doc_start, w_qkv, d_context)


def solution(mesh):
    fits = mesh.shape["seq"] == 8 and mesh.shape["dp"] == 4
    return jax.shard_map(
        kernel_body if fits else body,
        mesh=mesh,
        in_specs=(
            P("dp", "seq", None),
            P("dp", "seq"),
            P(("seq", "dp"), None),
            P("dp", "seq", None),
        ),
        out_specs=(P("dp", "seq", None), P(("seq", "dp"), None)),
        check_vma=False,
    )
```

```python
import jax
import jax.numpy as jnp
from jax import lax
from jax.experimental import pallas as pl
from jax.experimental.pallas import tpu as pltpu
from jax.sharding import PartitionSpec as P

WIN = 256


def from_partner(block, axis, stride):
    count = lax.axis_size(axis)
    route = []
    for low in range(count):
        high = low | 1 << stride
        if high != low and high < count:
            route += [(low, high), (high, low)]
    return lax.ppermute(block, axis, route)


def from_behind(block, axis, distance):
    devices = range(lax.axis_size(axis))
    route = [(i - distance, i) for i in devices if i - distance in devices]
    return lax.ppermute(block, axis, route)


def masked_scores(queries, key_rows, doc_first, query_pos, key_pos):
    inv_root = queries.shape[2] ** (-0.5)
    scores = (
        jnp.einsum("rhd,kd->hrk", queries, key_rows, preferred_element_type=jnp.float32) * inv_root
    )
    visible = (
        (key_pos[None, :] <= query_pos[:, None])
        & (key_pos[None, :] > query_pos[:, None] - WIN)
        & (key_pos[None, :] >= doc_first[:, None])
    )
    return jnp.where(visible[None, :, :], scores, -jnp.inf)


def backward_terms(queries, key_rows, value_rows, out_grad, attn_probs, prob_low, row_dot):
    inv_root = queries.shape[2] ** (-0.5)
    prob_grad = jnp.einsum("rhd,kd->hrk", out_grad, value_rows, preferred_element_type=jnp.float32)
    score_grad = (attn_probs * (prob_grad - row_dot[:, :, None])).astype(jnp.bfloat16)
    grad_query = (
        jnp.einsum("hrk,kd->rhd", score_grad, key_rows, preferred_element_type=jnp.float32)
        * inv_root
    )
    grad_keys = (
        jnp.einsum("hrk,rhd->kd", score_grad, queries, preferred_element_type=jnp.float32)
        * inv_root
    )
    grad_values = jnp.einsum("hrk,rhd->kd", prob_low, out_grad, preferred_element_type=jnp.float32)
    return (grad_query, grad_keys, grad_values)


def local_pass(queries, key_rows, value_rows, out_grad, doc_first, query_pos, key_pos):
    scores = masked_scores(queries, key_rows, doc_first, query_pos, key_pos)
    row_max = jnp.max(scores, axis=2)
    log_total = row_max + jnp.log(jnp.sum(jnp.exp(scores - row_max[:, :, None]), axis=2))
    attn_probs = jnp.exp(scores - log_total[:, :, None])
    prob_low = attn_probs.astype(jnp.bfloat16)
    context = jnp.einsum("hrk,kd->rhd", prob_low, value_rows, preferred_element_type=jnp.float32)
    row_dot = jnp.sum(out_grad.astype(jnp.float32) * context, axis=2).T
    grad_query, grad_keys, grad_values = backward_terms(
        queries, key_rows, value_rows, out_grad, attn_probs, prob_low, row_dot
    )
    return (grad_query, grad_keys, grad_values, log_total, row_dot)


def halve_over_seq(buffer, bit_index):
    half_rows = buffer.shape[0] // 2
    my_bit = lax.axis_index("seq") >> bit_index & 1
    kept_half = lax.dynamic_slice_in_dim(buffer, my_bit * half_rows, half_rows, 0)
    sent_half = lax.dynamic_slice_in_dim(buffer, (1 - my_bit) * half_rows, half_rows, 0)
    return kept_half + from_partner(sent_half.astype(jnp.bfloat16), "seq", bit_index).astype(
        sent_half.dtype
    )


def halve_over_dp(buffer, bit_index):
    half_rows = buffer.shape[0] // 2
    my_bit = lax.axis_index("dp") >> bit_index & 1
    kept_half = lax.dynamic_slice_in_dim(buffer, my_bit * half_rows, half_rows, 0)
    sent_half = lax.dynamic_slice_in_dim(buffer, (1 - my_bit) * half_rows, half_rows, 0)
    return kept_half + from_partner(sent_half.astype(jnp.bfloat16), "dp", bit_index).astype(
        sent_half.dtype
    )


def body(layer_inputs, doc_start, w_qkv, d_context):
    x_local = layer_inputs[0]
    tok_rows = x_local.shape[0]
    q_width = d_context.shape[2]
    head_dim = (w_qkv.shape[1] - q_width) // 2
    heads = q_width // head_dim
    out_grad = d_context[0].reshape(tok_rows, heads, head_dim)
    doc_first = doc_start[0]
    positions = lax.axis_index("seq") * tok_rows + jnp.arange(tok_rows, dtype=jnp.int32)
    full_weights = lax.all_gather(w_qkv, ("seq", "dp"), axis=0, tiled=True)
    projected = jnp.dot(x_local, full_weights, preferred_element_type=jnp.float32)
    projected = projected.astype(jnp.bfloat16)
    queries = projected[:, :q_width].reshape(tok_rows, heads, head_dim)
    key_value = projected[:, q_width:]
    prior = from_behind(key_value, "seq", 1)
    key_rows = jnp.concatenate([prior[:, :head_dim], key_value[:, :head_dim]], axis=0)
    value_rows = jnp.concatenate([prior[:, head_dim:], key_value[:, head_dim:]], axis=0)
    key_pos = jnp.concatenate([positions - tok_rows, positions])
    grad_query, grad_keys, grad_values, log_total, row_dot = local_pass(
        queries, key_rows, value_rows, out_grad, doc_first, positions, key_pos
    )
    returned = from_behind(
        jnp.concatenate([grad_keys[:tok_rows], grad_values[:tok_rows]], axis=1).astype(
            jnp.bfloat16
        ),
        "seq",
        -1,
    ).astype(jnp.float32)
    far_keys = returned[:, :head_dim]
    far_values = returned[:, head_dim:]
    key_grad = (grad_keys[tok_rows:] + far_keys).astype(jnp.bfloat16)
    value_grad = (grad_values[tok_rows:] + far_values).astype(jnp.bfloat16)
    grad_proj = jnp.concatenate(
        [grad_query.astype(jnp.bfloat16).reshape(tok_rows, q_width), key_grad, value_grad], axis=1
    )
    input_grad = lax.dot_general(
        grad_proj, full_weights, (((1,), (1,)), ((), ())), preferred_element_type=jnp.float32
    )
    input_grad = input_grad.astype(jnp.bfloat16).reshape(1, tok_rows, x_local.shape[1])
    partial_grad = lax.dot_general(
        x_local, grad_proj, (((0,), (0,)), ((), ())), preferred_element_type=jnp.float32
    )
    seq_count = lax.axis_size("seq")
    dp_count = lax.axis_size("dp")
    seq_levels = seq_count.bit_length() - 1
    dp_levels = dp_count.bit_length() - 1
    buffer = partial_grad
    for bit_index in range(seq_levels - 1, -1, -1):
        buffer = halve_over_seq(buffer, bit_index)
    for bit_index in range(dp_levels - 1, -1, -1):
        buffer = halve_over_dp(buffer, bit_index)
    return (input_grad, buffer)


BF = jnp.bfloat16
F32 = jnp.float32
NZ = 4
ORDER = (
    ("z", 0), ("swap",), ("z", 1), ("a", 0), ("b", 0, 0), ("z", 2), ("a", 1), ("b", 1, 0),
    ("b", 0, 1), ("z", 3), ("prep",), ("a", 2), ("b", 2, 0), ("b", 1, 1), ("a", 3), ("take",),
    ("d", 0, 2), ("b", 3, 0), ("b", 2, 1), ("d", 2, 3), ("b", 3, 1), ("d", 3, 4),
    ("partial", 1), ("partial", 0), ("halo",), ("values",),
)


def dot_nn(a, b):
    return jnp.dot(a, b, preferred_element_type=F32)


def dot_nt(a, b):
    return lax.dot_general(a, b, (((1,), (1,)), ((), ())), preferred_element_type=F32)


def dot_tn(a, b):
    return lax.dot_general(a, b, (((0,), (0,)), ((), ())), preferred_element_type=F32)


def flip(v, f):
    return v + f * (1 - 2 * v)


def remote(src, dst, send, recv, device):
    return pltpu.make_async_remote_copy(
        src_ref=src,
        dst_ref=dst,
        send_sem=send,
        recv_sem=recv,
        device_id=device,
        device_id_type=pl.DeviceIdType.MESH,
    )


def fused(
    x_hbm, doc_hbm, w_hbm, do_hbm, dx_hbm, g_ref,
    xo, xs, docv, vis, wv, acc, pacc, qs, qt, dos, dot_, pgs, kv, dkv, pst, dst_, gp, gpt, dxo, dxr,
    gb, rb, sa, ra, sz, rz,
    lsem, xsem, wsend, wrecv, hsend, hrecv, ssend, srecv, gsend, grecv, osem,
):
    s = lax.axis_index("seq")
    d = lax.axis_index("dp")
    z, y = s // 2, s % 2
    x, c = d // 2, d % 2
    tok = xs.shape[1]
    rows = wv.shape[3]
    hd = qs.shape[1]
    half = 2 * hd
    span = 4 * rows
    inv_root = hd ** (-0.5)
    my_a = x * (1 - c) + y * c
    my_b = y * (1 - c) + x * c

    def device(zz, yy, xx, cc):
        return (zz * 2 + yy, xx * 2 + cc)

    sib = device(z, y, x, 1 - c)
    part_a = device(z, flip(y, c), flip(x, 1 - c), c)
    part_b = device(z, flip(y, 1 - c), flip(x, c), c)
    zdev = [device((z + k) % NZ, y, x, c) for k in range(NZ)]
    z_order = [
        z,
        jnp.where(z == 0, 1, jnp.where(z == 1, 0, jnp.where(z == 2, 3, 2))),
        jnp.where(z == 0, 2, jnp.where(z == 1, 2, 1)),
        jnp.where(z <= 1, 3, 0),
    ]

    def columns(plane, zz, q):
        b, a = q // 2, q % 2
        yy = b * (1 - plane) + a * plane
        xx = a * (1 - plane) + b * plane
        block = ((zz * 2 + yy) * 2 + xx) * 2 + plane
        return pl.ds(pl.multiple_of(block * rows, rows), rows)

    def load_swap(j):
        zz, q = j // 4, j % 4
        return pltpu.make_async_copy(
            x_hbm.at[0, :, columns(1 - c, zz, q)],
            xs.at[zz, :, pl.ds(pl.multiple_of(q * rows, rows), rows)],
            xsem.at[j],
        )

    def load_own(j):
        zz, q = j // 4, j % 4
        return pltpu.make_async_copy(
            x_hbm.at[0, :, columns(c, zz, q)],
            xo.at[zz, pl.ds(0, tok), pl.ds(pl.multiple_of(q * rows, rows), rows)],
            xsem.at[16 + j],
        )

    def each(count, action):
        def one(j, carry):
            action(j)
            return carry

        lax.fori_loop(0, count, one, 0)

    load_w = pltpu.make_async_copy(w_hbm, wv.at[z, my_b, my_a], lsem.at[0])
    late = [pltpu.make_async_copy(doc_hbm, docv, lsem.at[2])] + [
        pltpu.make_async_copy(
            do_hbm.at[0, :, pl.ds(h * hd, hd)], dos.at[pl.ds(h * tok, tok)], lsem.at[3 + h]
        )
        for h in range(2)
    ]
    load_w.start()
    each(16, lambda j: load_swap(j).start())
    each(16, lambda j: load_own(j).start())
    for load in late:
        load.start()

    barrier = pltpu.get_barrier_semaphore()
    for dev in [sib, part_a, part_b] + zdev[1:]:
        pl.semaphore_signal(barrier, inc=1, device_id=dev, device_id_type=pl.DeviceIdType.MESH)
    extra_up = (y == 1) & (z < NZ - 1)
    extra_down = (y == 0) & (z > 0)

    @pl.when(extra_up)
    def _():
        pl.semaphore_signal(
            barrier, inc=1, device_id=(s + 1, d), device_id_type=pl.DeviceIdType.MESH
        )

    @pl.when(extra_down)
    def _():
        pl.semaphore_signal(
            barrier, inc=1, device_id=(s - 1, d), device_id_type=pl.DeviceIdType.MESH
        )

    load_w.wait()

    @pl.when(extra_up | extra_down)
    def _():
        pl.semaphore_wait(barrier, 7)

    @pl.when(jnp.logical_not(extra_up | extra_down))
    def _():
        pl.semaphore_wait(barrier, 6)

    sent = []
    line = []
    swaps = {}

    def swap(src, dst, index):
        copy = remote(src, dst, ssend.at[index], srecv.at[index], sib)
        copy.start()
        sent.append(copy)
        swaps[index] = copy

    def block_at(k, b_flip, a_flip):
        return wv.at[z_order[k], flip(my_b, b_flip), flip(my_a, a_flip)]

    def push(ref, dev, index):
        copy = remote(ref, ref, wsend.at[index], wrecv.at[index], dev)
        copy.start()
        sent.append(copy)

    def arrived(ref, index):
        remote(ref, ref, wsend.at[0], wrecv.at[index], sib).wait_recv()

    def stage_z(k):
        ref = block_at(k, 0, 0)
        zz = z_order[k]
        if k:
            arrived(ref, zz)
        up = remote(ref, ref, wsend.at[zz], wrecv.at[zz], zdev[1])
        down = remote(ref, ref, wsend.at[16 + zz], wrecv.at[zz], zdev[3])
        for copy, test in ((up, (zz <= z) & (z < NZ - 1)), (down, (zz >= z) & (z > 0))):
            line.append((copy, test))
            pl.when(test)(copy.start)
        push(ref, part_a, 4 + k)
        push(ref, part_b, 8 + 2 * k)

    def stage_a(k):
        ref = block_at(k, 0, 1)
        arrived(ref, 4 + k)
        push(ref, part_b, 9 + 2 * k)

    def stage_b(k, a):
        arrived(block_at(k, 1, a), 8 + 2 * k + a)

    def stage_d(low, high):
        def one(j, carry):
            zz = jnp.where(
                j == 0,
                z_order[0],
                jnp.where(j == 1, z_order[1], jnp.where(j == 2, z_order[2], z_order[3])),
            )
            for h in (1, 0):
                ws = wv[zz, :, :, :, h * half : (h + 1) * half].reshape(span, half)
                acc[h] += dot_nn(xo[zz], ws)
            return carry

        if low == 0:
            acc[...] = jnp.zeros_like(acc)
        lax.fori_loop(low, high, one, 0)

    def projected(h):
        swaps[4 + h].wait_recv()
        return (acc[h, :tok] + pacc[h]).astype(BF)

    halo = remote(kv.at[1], kv.at[0], hsend.at[0], hrecv.at[0], ((s + 1) % 8, d))

    def send_halo():
        kv[1] = projected(1)

        @pl.when(s < 7)
        def _():
            halo.start()

        @pl.when(s == 0)
        def _():
            kv[0] = jnp.zeros_like(kv[0])

    def value_grads():
        pgs[1] = dot_nt(dos[...], kv[1, :, hd:])
        q_own = projected(0)
        for h in range(2):
            qs[h * tok : (h + 1) * tok, :] = q_own[:, h * hd : (h + 1) * hd]
        qt[...] = qs[...].T

        @pl.when(s > 0)
        def _():
            halo.wait_recv()

        pgs[0] = dot_nt(dos[...], kv[0, :, hd:])

    for stage, *at in ORDER:
        if stage == "z":
            stage_z(*at)
        elif stage == "a":
            stage_a(*at)
        elif stage == "b":
            stage_b(*at)
        elif stage == "d":
            stage_d(*at)
        elif stage == "swap":
            each(16, lambda j: load_swap(j).wait())
            for j in range(NZ):
                swap(xs.at[j], xo.at[j, pl.ds(tok, tok)], j)
        elif stage == "take":
            each(16, lambda j: load_own(j).wait())
            for j in range(NZ):
                swaps[j].wait_recv()
        elif stage == "partial":
            swap(acc.at[at[0], pl.ds(tok, tok)], pacc.at[at[0]], 4 + at[0])
        elif stage == "halo":
            send_halo()
        elif stage == "values":
            value_grads()
        else:
            for load in late:
                load.wait()
            doc = jnp.broadcast_to(docv[...], (tok, tok)).T
            row = lax.broadcasted_iota(jnp.int32, (tok, tok), 0)
            col = lax.broadcasted_iota(jnp.int32, (tok, tok), 1)
            vis[1] = jnp.where((col <= row) & (col + s * tok >= doc), 0.0, -jnp.inf)
            vis[0] = jnp.where((col > row) & (col + (s - 1) * tok >= doc), 0.0, -jnp.inf)
            dot_[...] = dos[...].T

    part_rows = tok // 2

    def attend(j):
        k_own = kv[1, :, :hd]
        k_pri = kv[0, :, :hd]
        at = pl.ds(pl.multiple_of(j * part_rows, part_rows), part_rows)
        seen = pl.ds(pl.multiple_of(j % 2 * part_rows, part_rows), part_rows)
        s_own = dot_nt(qs[at, :], k_own) * inv_root + vis[1, seen, :]
        s_pri = dot_nt(qs[at, :], k_pri) * inv_root + vis[0, seen, :]
        pg_own = pgs[1, at, :]
        pg_pri = pgs[0, at, :]
        top = jnp.max(jnp.maximum(s_own, s_pri), axis=1, keepdims=True)
        e_own = jnp.exp(s_own - top)
        e_pri = jnp.exp(s_pri - top)
        scale = 1.0 / jnp.sum(e_own + e_pri, axis=1, keepdims=True)
        p_own = e_own * scale
        p_pri = e_pri * scale
        l_own = p_own.astype(BF)
        l_pri = p_pri.astype(BF)
        row_dot = jnp.sum(
            l_own.astype(F32) * pg_own + l_pri.astype(F32) * pg_pri, axis=1, keepdims=True
        )
        pst[0, at, :] = l_pri
        pst[1, at, :] = l_own
        dst_[0, at, :] = (p_pri * (pg_pri - row_dot)).astype(BF)
        dst_[1, at, :] = (p_own * (pg_own - row_dot)).astype(BF)

    each(4, attend)

    dkv[0, :hd, :] = (dot_nn(qt[...], dst_[0]) * inv_root).astype(BF)
    dkv[0, hd:, :] = dot_nn(dot_[...], pst[0]).astype(BF)
    back = remote(dkv.at[0], dkv.at[1], hsend.at[1], hrecv.at[1], ((s + 7) % 8, d))

    @pl.when(s > 0)
    def _():
        back.start()

    @pl.when(s == 7)
    def _():
        dkv[1] = jnp.zeros_like(dkv[1])

    dq = (
        (dot_nn(dst_[1], kv[1, :, :hd]) + dot_nn(dst_[0], kv[0, :, :hd])) * inv_root
    ).astype(BF)
    for h in range(2):
        gp[0, :tok, h * hd : (h + 1) * hd] = dq[h * tok : (h + 1) * tok]

    def swap_grads(h):
        swap(gp.at[h, pl.ds(0, tok)], gp.at[h, pl.ds(tok, tok)], 6 + h)

    def take_grads(h):
        swaps[6 + h].wait_recv()
        gpt[h, :, tok:] = gp[h, tok:, :].T

    def chunk(h, i, stage):
        src, dst, dev = {
            0: (gb.at[h, i, 1 - my_b], rb.at[h, i], part_b),
            1: (sa.at[h, i], ra.at[h, i], part_a),
            2: (sz.at[h, i], rz.at[h, i], ((z + i + 1) % NZ * 2 + y, d)),
        }[stage]
        index = (h * NZ + i) * 3 + stage
        return remote(src, dst, gsend.at[index], grecv.at[index], dev)

    def produce(h, i):
        part = dot_nn(gpt[h], xo[(z + i + 1) % NZ]).astype(BF)
        for q in range(4):
            gb[h, i, q // 2, q % 2] = part[:, q * rows : (q + 1) * rows]
        chunk(h, i, 0).start()

    def sum_b(h, i, a_at):
        return gb[h, i, my_b, a_at].astype(F32) + rb[h, i, a_at].astype(F32)

    def send_a(h, i):
        chunk(h, i, 0).wait_recv()
        sa[h, i] = sum_b(h, i, 1 - my_a).astype(BF)
        chunk(h, i, 1).start()

    def send_z(h, i):
        chunk(h, i, 1).wait_recv()
        sz[h, i] = (sum_b(h, i, my_a) + ra[h, i].astype(F32)).astype(BF)
        chunk(h, i, 2).start()

    def finish(h):
        chunk(h, NZ - 1, 1).wait_recv()
        total = sum_b(h, NZ - 1, my_a) + ra[h, NZ - 1].astype(F32)
        for i in range(NZ - 1):
            chunk(h, i, 2).wait_recv()
            total += rz[h, i].astype(F32)
        g_ref[:, h * half : (h + 1) * half] = total.T

    def store(src, plane, zz, q, index):
        return pltpu.make_async_copy(
            src.at[zz, pl.ds(0, tok), pl.ds(q * rows, rows)],
            dx_hbm.at[0, :, columns(plane, zz, q)],
            osem.at[index],
        )

    def swap_dx(zz):
        return remote(
            dxo.at[zz, pl.ds(tok, tok)], dxr.at[zz], ssend.at[8 + zz], srecv.at[8 + zz], sib
        )

    def input_grad(zz):
        ws = wv[zz].reshape(span, 2 * half)
        part = dot_nt(gp[0], ws[:, :half]) + dot_nt(gp[1], ws[:, half:])
        dxo[zz] = part.astype(BF)
        swap_dx(zz).start()
        for q in range(4):
            store(dxo, c, zz, q, zz * 4 + q).start()

    def take_input_grad(zz):
        swap_dx(zz).wait_recv()
        for q in range(4):
            store(dxr, 1 - c, zz, q, 16 + zz * 4 + q).start()

    swap_grads(0)
    gpt[0, :, :tok] = gp[0, :tok, :].T
    own_dk = dot_nn(qt[...], dst_[1]) * inv_root
    own_dv = dot_nn(dot_[...], pst[1])
    take_grads(0)
    each(NZ, lambda i: produce(0, i))

    @pl.when(s < 7)
    def _():
        back.wait_recv()

    gpt[1, :hd, :tok] = (own_dk + dkv[1, :hd, :].astype(F32)).astype(BF)
    gpt[1, hd:, :tok] = (own_dv + dkv[1, hd:, :].astype(F32)).astype(BF)
    gp[1, :tok, :] = gpt[1, :, :tok].T
    swap_grads(1)
    take_grads(1)

    def both(i):
        produce(1, i)
        send_a(0, i)

    each(NZ, both)

    def spread(i):
        input_grad(i)

        @pl.when(i < NZ - 1)
        def _():
            send_z(0, i)

    each(NZ, spread)

    def tail(i):
        take_input_grad(i)
        send_a(1, i)

        @pl.when(i > 0)
        def _():
            send_z(1, i - 1)

    each(NZ, tail)
    finish(0)
    finish(1)

    def drain(i):
        swap_dx(i).wait_send()
        for q in range(4):
            store(dxo, c, i, q, i * 4 + q).wait()
            store(dxr, 1 - c, i, q, 16 + i * 4 + q).wait()
        for h in range(2):
            chunk(h, i, 0).wait_send()
            chunk(h, i, 1).wait_send()

            @pl.when(i < NZ - 1)
            def _():
                chunk(h, i, 2).wait_send()

    each(NZ, drain)
    for copy in sent:
        copy.wait_send()
    for copy, test in line:
        pl.when(test)(copy.wait_send)

    @pl.when(s < 7)
    def _():
        halo.wait_send()

    @pl.when(s > 0)
    def _():
        back.wait_send()


def kernel_body(layer_inputs, doc_start, w_qkv, d_context):
    tok, width = layer_inputs.shape[1:]
    rows, cols = w_qkv.shape
    hd = cols // 4
    half = 2 * hd
    dma = pltpu.SemaphoreType.DMA
    block = (half, rows)
    return pl.pallas_call(
        fused,
        out_shape=(
            jax.ShapeDtypeStruct(layer_inputs.shape, BF),
            jax.ShapeDtypeStruct((rows, cols), F32),
        ),
        in_specs=[pl.BlockSpec(memory_space=pl.ANY)] * 4,
        out_specs=(
            pl.BlockSpec(memory_space=pl.ANY),
            pl.BlockSpec(memory_space=pltpu.VMEM),
        ),
        scratch_shapes=[
            pltpu.VMEM((NZ, 2 * tok, 4 * rows), BF),
            pltpu.VMEM((NZ, tok, 4 * rows), BF),
            pltpu.VMEM((1, tok), jnp.int32),
            pltpu.VMEM((2, tok, tok), F32),
            pltpu.VMEM((NZ, 2, 2, rows, cols), BF),
            pltpu.VMEM((2, 2 * tok, half), F32),
            pltpu.VMEM((2, tok, half), F32),
            pltpu.VMEM((2 * tok, hd), BF),
            pltpu.VMEM((hd, 2 * tok), BF),
            pltpu.VMEM((2 * tok, hd), BF),
            pltpu.VMEM((hd, 2 * tok), BF),
            pltpu.VMEM((2, 2 * tok, tok), F32),
            pltpu.VMEM((2, tok, half), BF),
            pltpu.VMEM((2, half, tok), BF),
            pltpu.VMEM((2, 2 * tok, tok), BF),
            pltpu.VMEM((2, 2 * tok, tok), BF),
            pltpu.VMEM((2, 2 * tok, half), BF),
            pltpu.VMEM((2, half, 2 * tok), BF),
            pltpu.VMEM((NZ, 2 * tok, 4 * rows), BF),
            pltpu.VMEM((NZ, tok, 4 * rows), BF),
            pltpu.VMEM((2, NZ, 2, 2) + block, BF),
            pltpu.VMEM((2, NZ, 2) + block, BF),
            pltpu.VMEM((2, NZ) + block, BF),
            pltpu.VMEM((2, NZ) + block, BF),
            pltpu.VMEM((2, NZ) + block, BF),
            pltpu.VMEM((2, NZ) + block, BF),
            dma((5,)),
            dma((32,)),
            dma((20,)),
            dma((16,)),
            dma((2,)),
            dma((2,)),
            dma((12,)),
            dma((12,)),
            dma((24,)),
            dma((24,)),
            dma((32,)),
        ],
        compiler_params=pltpu.CompilerParams(
            collective_id=0, has_side_effects=True, vmem_limit_bytes=60 * 1024 * 1024
        ),
    )(layer_inputs, doc_start, w_qkv, d_context)


def solution(mesh):
    fits = mesh.shape["seq"] == 8 and mesh.shape["dp"] == 4
    return jax.shard_map(
        kernel_body if fits else body,
        mesh=mesh,
        in_specs=(
            P("dp", "seq", None),
            P("dp", "seq"),
            P(("seq", "dp"), None),
            P("dp", "seq", None),
        ),
        out_specs=(P("dp", "seq", None), P(("seq", "dp"), None)),
        check_vma=False,
    )
```
